32 devices in a mesh: groups: 2 (over x), expert: 4 (over y, core), mp: 4 (over z).
Axes of the slice: x: 2, y: 2, z: 4, core: 2. Of those that a mesh axis runs over, the one named last changes fastest.
Arguments:
- tokens: bfloat16 [256, 4096], P(('groups', 'expert', 'mp')), parts along dimension 0, may hold values from -6 to 6
- routes: int32 [256, 8], P(('groups', 'expert', 'mp')), parts along dimension 0, may hold values from 0 to 15, all different within a row; in each aligned block of 8 rows (0 to 7, 8 to 15, ...) at most 5 rows name the same one
- probs: float32 [256, 8], P(('groups', 'expert', 'mp')), parts along dimension 0, may hold values from 0.1 to 1
- w_gate: bfloat16 [16, 4096, 768], P('expert', None, 'mp'), may hold values from -0.09375 to 0.09375
- w_up: bfloat16 [16, 4096, 768], P('expert', None, 'mp'), may hold values from -0.09375 to 0.09375
- w_down: bfloat16 [16, 768, 4096], P('expert', 'mp'), may hold values from -0.21875 to 0.21875
- gate_left: bfloat16 [16, 32, 4096], P('expert', None, 'mp'), may hold values from -0.046875 to 0.046875
- gate_right: bfloat16 [16, 32, 768], P('expert', 'mp'), may hold values from -1 to 1
- up_left: bfloat16 [16, 32, 4096], P('expert', None, 'mp'), may hold values from -0.046875 to 0.046875
- up_right: bfloat16 [16, 32, 768], P('expert', 'mp'), may hold values from -1 to 1
- down_left: bfloat16 [16, 32, 768], P('expert', 'mp'), may hold values from -0.109375 to 0.109375
- down_right: bfloat16 [16, 32, 4096], P('expert', None, 'mp'), may hold values from -1 to 1
Outputs:
- mixed: bfloat16 [256, 4096], P(('groups', 'expert', 'mp')), parts along dimension 0
The draws below stay inside these ranges and needn't reach their ends.
There are 2 independent parts, one for each index of `groups`. The reference program is written for one: setup_inputs(seed, part) draws one part's arguments, and reference() takes and returns one part's arrays. A program takes and returns all parts, laid end to end along the dimension named above; an argument that names none is the same for every part. Nothing has to cross between parts.
Inputs may be any that keep to these rules, and one draw needn't show every extreme that they name: `routes`: each row names 8 different experts; within the rows of one device no expert is named by more than 5 rows, a bound that some block reaches.
All inputs are finite; a program needn't handle non-finite values.
Results may differ from the reference program's by a relative error of at most 0.014.
Values may be sent and summed in bfloat16 or wider, within the bound.
No kernel may reach another device: no remote copies, remote signals or barrier semaphores. Data moves between devices by JAX's collectives and lax.ppermute only.
A program may use at most 128 MiB of HBM per device.

```python
import math
import jax
import jax.numpy as jnp
import numpy as np
from jax import lax

D = 4096
FF = 768
EXPERTS = 16
TOP = 8
R = 32
TOK_DEV = 8
TOKENS = 128
C = 5
N_MP = 4


def steps_of(key, dims, shards, least, high):
    def one(dim, blocks):
        steps = jax.random.uniform(jax.random.fold_in(jax.random.fold_in(key, 6), dim), (blocks,), jnp.float32, least / len(shards), high / len(shards))
        return jnp.repeat(jnp.exp(steps), dims[dim] // blocks).reshape((-1,) + (1,) * (len(dims) - dim - 1))

    level = one(*shards[0])
    for cut in shards[1:]:
        level = level * one(*cut)
    return level


def shared_out(key, own, number, rows, count, top, reach, slope):
    ranking = jax.random.permutation(key, count)
    heavy_load, ordinary = shares(count, rows * top, reach, slope, True), shares(count, rows * top, reach, slope, False)
    places = jnp.arange(count)

    def named(sizes, offset_by):
        used = int((sizes > 0).sum())
        fixed = max(1, used // 4)
        shifted = fixed + (places - fixed + offset_by * (used - fixed)) % max(1, count - fixed)
        return jnp.zeros((count,), jnp.int32).at[ranking[jnp.where(places < fixed, places, shifted)]].set(jnp.asarray(sizes, jnp.int32))

    sizes = jnp.where(number % 4 == 0, named(heavy_load, number // 4), named(ordinary, number - number // 4 - 1))
    mixed = jax.random.permutation(jax.random.fold_in(own, 3), count)
    giver, receiver = mixed[0:count // 2 * 2:2], mixed[1:count // 2 * 2:2]
    margin = jnp.minimum(sizes[giver] - 1, reach - sizes[receiver]) // 2
    margin = jnp.where((giver == ranking[0]) | (receiver == ranking[0]) | (sizes[receiver] == 0), 0, jnp.maximum(margin, 0))
    shifted = jax.random.randint(jax.random.fold_in(own, 4), (count // 2,), 0, 1 << 20) % (margin + 1)
    sizes = sizes.at[giver].add(-shifted).at[receiver].add(shifted)
    members = jnp.searchsorted(jnp.cumsum(sizes), jnp.arange(rows * top), side="right").astype(jnp.int32)
    listing = members.reshape(top, rows).T
    listing = listing[jax.random.permutation(jax.random.fold_in(own, 1), rows)]
    offset_by = jax.random.randint(jax.random.fold_in(own, 2), (rows, 1), 0, top)
    return jnp.take_along_axis(listing, (jnp.arange(top)[None, :] + offset_by) % top, axis=1)


def shares(amount, total, limit, slope, full):
    portions = [(1 << 20) // math.isqrt(standing ** slope) + 1 for standing in range(1, amount + 1)]
    largest = limit if full else min(limit, max(-(-total // amount), total * portions[0] // sum(portions)))
    least = 1 if total - largest >= amount - 1 else 0
    holding, rest = [largest] + [least] * (amount - 1), total - largest - least * (amount - 1)
    while rest > 0:
        free = [i for i in range(1, amount) if holding[i] < largest] or [i for i in range(1, amount) if holding[i] < limit]
        mass, budget = sum([portions[i] for i in free]), rest
        for i in free:
            more = min(limit - holding[i], max(1, budget * portions[i] // mass), rest)
            holding[i] = holding[i] + more
            rest = rest - more
    return np.array(holding)


def centred(key, dims, spread, reach, cuts=(), kind=jnp.bfloat16):
    result = spread * jax.random.normal(key, dims, jnp.float32)
    if cuts:
        result = result * steps_of(key, dims, cuts, -0.22, 0.18)
    return jnp.clip(result, -reach, reach).astype(kind)


def setup_inputs(seed: int = 0, part: int = 0) -> dict:
    key_list = jax.random.split(jax.random.key(seed), 13)
    part_splits = jax.random.split(jax.random.fold_in(key_list[12], part), 13)
    tokens = centred(part_splits[0], (TOKENS, D), 1.0, 6.0, ((0, 16),))
    routes_keys = jax.random.split(jax.random.fold_in(part_splits[1], 1), TOKENS // TOK_DEV)
    routes_turns = jax.random.permutation(jax.random.fold_in(part_splits[1], 3), TOKENS // TOK_DEV)
    routes = jax.vmap(lambda own, number: shared_out(jax.random.fold_in(part_splits[1], 2), own, number, TOK_DEV, EXPERTS, TOP, C, 2))(routes_keys, routes_turns).reshape((TOKENS, TOP))
    probs = jnp.clip(jnp.exp(math.log(1.0) - 2.3025851 * jax.random.uniform(part_splits[2], (TOKENS, TOP), jnp.float32) ** steps_of(part_splits[2], (TOKENS, TOP), ((0, 16),), -0.2, 0.2)), 0.1, 1.0)
    w_gate = centred(key_list[3], (EXPERTS, D, FF), D ** -0.5, 0.09375, ((0, 4), (2, 4)))
    w_up = centred(key_list[4], (EXPERTS, D, FF), D ** -0.5, 0.09375, ((0, 4), (2, 4)))
    w_down = centred(key_list[5], (EXPERTS, FF, D), FF ** -0.5, 0.21875, ((0, 4), (1, 4)))
    gate_left = centred(key_list[6], (EXPERTS, R, D), (4 * D) ** -0.5, 0.046875, ((0, 4), (2, 4)))
    gate_right = centred(key_list[7], (EXPERTS, R, FF), R ** -0.5, 1.0, ((0, 4), (1, 4)))
    up_left = centred(key_list[8], (EXPERTS, R, D), (4 * D) ** -0.5, 0.046875, ((0, 4), (2, 4)))
    up_right = centred(key_list[9], (EXPERTS, R, FF), R ** -0.5, 1.0, ((0, 4), (1, 4)))
    down_left = centred(key_list[10], (EXPERTS, R, FF), (4 * FF) ** -0.5, 0.109375, ((0, 4), (1, 4)))
    down_right = centred(key_list[11], (EXPERTS, R, D), R ** -0.5, 1.0, ((0, 4), (2, 4)))
    return {"tokens": tokens, "routes": routes, "probs": probs, "w_gate": w_gate, "w_up": w_up, "w_down": w_down, "gate_left": gate_left, "gate_right": gate_right, "up_left": up_left, "up_right": up_right, "down_left": down_left, "down_right": down_right}


def merge_pair(base, left, right):
    product = jnp.dot(left.T, right, preferred_element_type=jnp.float32)
    return (base.astype(jnp.float32) + product).astype(jnp.bfloat16)


def reference(tokens, routes, probs, w_gate, w_up, w_down, gate_left, gate_right, up_left, up_right, down_left, down_right):
    highest = lax.Precision.HIGHEST
    blocks = TOKENS // TOK_DEV
    entries = TOK_DEV * TOP
    route_blocks = routes.reshape(blocks, entries)
    prob_blocks = probs.reshape(blocks, entries).astype(jnp.float32)
    token_blocks = tokens.reshape(blocks, TOK_DEV, D).astype(jnp.float32)
    entry_ids = jnp.arange(entries, dtype=jnp.int32) // TOP
    owner_token = (entry_ids[:, None] == jnp.arange(TOK_DEV, dtype=jnp.int32)[None, :]).astype(jnp.float32)
    slot_ids = jnp.arange(C, dtype=jnp.int32)

    def add_expert(expert_id, total):
        hits = (route_blocks == expert_id).astype(jnp.int32)
        order = jnp.cumsum(hits, axis=1) - 1
        chosen = (hits[:, None, :] * (order[:, None, :] == slot_ids[None, :, None]).astype(jnp.int32)).astype(jnp.float32)
        picks = jnp.einsum('bcj,jt->bct', chosen, owner_token, precision=highest)
        routed = jnp.einsum('bct,btd->bcd', picks, token_blocks, precision=highest).astype(jnp.bfloat16)
        routed = routed.reshape(blocks * C, D)
        weights = jnp.einsum('bcj,jt->bct', chosen * prob_blocks[:, None, :], owner_token, precision=highest)
        gate_merged = merge_pair(w_gate[expert_id], gate_left[expert_id], gate_right[expert_id])
        up_merged = merge_pair(w_up[expert_id], up_left[expert_id], up_right[expert_id])
        down_merged = (w_down[expert_id].astype(jnp.float32) + jnp.dot(down_left[expert_id].T, down_right[expert_id], preferred_element_type=jnp.float32)).astype(jnp.bfloat16)
        gate_act = jnp.dot(routed, gate_merged, preferred_element_type=jnp.float32)
        up_act = jnp.dot(routed, up_merged, preferred_element_type=jnp.float32)
        hidden = (jax.nn.silu(gate_act) * up_act).astype(jnp.bfloat16)
        split_hidden = hidden.reshape(blocks * C, N_MP, FF // N_MP).astype(jnp.float32)
        split_down = down_merged.reshape(N_MP, FF // N_MP, D).astype(jnp.float32)
        partial_out = jnp.einsum('nmf,mfd->mnd', split_hidden, split_down, precision=highest).astype(jnp.bfloat16)
        expert_out = jnp.sum(partial_out.astype(jnp.float32), axis=0).astype(jnp.bfloat16)
        contrib = jnp.einsum('bct,bcd->btd', weights, expert_out.astype(jnp.float32).reshape(blocks, C, D), precision=highest)
        return total + contrib

    total = lax.fori_loop(0, EXPERTS, add_expert, jnp.zeros((blocks, TOK_DEV, D), jnp.float32))
    return total.reshape(TOKENS, D).astype(jnp.bfloat16)
```

```python
import jax
import jax.numpy as jnp
from jax import lax
from jax.sharding import PartitionSpec as P

BF = jnp.bfloat16
F32 = jnp.float32


def dot_nt(a, b):
    return lax.dot_general(a, b, (((1,), (1,)), ((), ())), preferred_element_type=F32)


def dot_nn(a, b):
    return lax.dot_general(a, b, (((1,), (0,)), ((), ())), preferred_element_type=F32)


def local(
    tokens,
    routes,
    probs,
    w_gate,
    w_up,
    w_down,
    gate_left,
    gate_right,
    up_left,
    up_right,
    down_left,
    down_right,
):
    rows, width = tokens.shape
    exp_dev, _, cols = w_gate.shape
    rank = gate_left.shape[1]
    piece = gate_right.shape[1]
    block = gate_left.shape[2]
    groups = lax.axis_size("expert")
    parts = lax.axis_size("mp")
    experts = exp_dev * groups
    me_g = lax.axis_index("expert")
    me_m = lax.axis_index("mp")
    ranks = exp_dev * rank
    hid = exp_dev * cols

    chosen = routes[:, :, None] == jnp.arange(experts, dtype=jnp.int32)
    weight = jnp.sum(jnp.where(chosen, probs[:, :, None], 0.0), axis=1)
    high = lax.reduce_precision(weight, 8, 7)
    low = (weight - high).astype(BF)
    side = jnp.concatenate([high.astype(BF), low], axis=1)
    pad = -(2 * experts) % 128
    sent = jnp.concatenate([tokens, jnp.pad(side, ((0, 0), (0, pad)))], axis=1)
    every = lax.all_gather(sent, ("expert", "mp"), axis=0, tiled=True)
    total = every.shape[0]
    x = every[:, :width]
    side = every[:, width : width + 2 * experts].astype(F32)
    weight = side[:, :experts] + side[:, experts:]
    weight = lax.dynamic_slice(weight, (0, me_g * exp_dev), (total, exp_dev))

    small = jnp.stack([gate_right, up_right, down_left])
    small = small.reshape(3, exp_dev, piece, parts, cols)
    small = lax.all_to_all(small, "mp", split_axis=3, concat_axis=2, tiled=True)
    small = small.reshape(3, ranks, cols)
    same = (jnp.arange(ranks) // rank)[:, None] == (jnp.arange(hid) // cols)[None, :]
    diag = jnp.where(same, jnp.tile(small, (1, 1, exp_dev)), jnp.zeros((), BF))

    mine = lax.dynamic_slice(x, (0, me_m * block), (total, block))
    left = jnp.concatenate([gate_left.reshape(ranks, block), up_left.reshape(ranks, block)])
    inner = lax.psum(dot_nt(mine, left), "mp").astype(BF)

    gate_w = jnp.swapaxes(w_gate, 1, 2).reshape(hid, width)
    up_w = jnp.swapaxes(w_up, 1, 2).reshape(hid, width)
    gate_act = dot_nt(x, gate_w) + dot_nn(inner[:, :ranks], diag[0])
    up_act = dot_nt(x, up_w) + dot_nn(inner[:, ranks:], diag[1])
    scale = jnp.repeat(weight, cols, axis=1)
    hidden = (jax.nn.silu(gate_act) * up_act * scale).astype(BF)
    bottom = lax.psum(dot_nt(hidden, diag[2]), "mp").astype(BF)
    out = dot_nn(hidden, w_down.reshape(hid, width))
    extra = dot_nn(bottom, down_right.reshape(ranks, block))
    out = lax.dynamic_update_slice(
        out, extra + lax.dynamic_slice(out, (0, me_m * block), (total, block)), (0, me_m * block)
    )
    return lax.psum_scatter(out.astype(BF), ("expert", "mp"), scatter_dimension=0, tiled=True)


def solution(mesh):
    return jax.shard_map(
        local,
        mesh=mesh,
        in_specs=(
            P(("groups", "expert", "mp"), None),
            P(("groups", "expert", "mp"), None),
            P(("groups", "expert", "mp"), None),
            P("expert", None, "mp"),
            P("expert", None, "mp"),
            P("expert", "mp", None),
            P("expert", None, "mp"),
            P("expert", "mp", None),
            P("expert", None, "mp"),
            P("expert", "mp", None),
            P("expert", "mp", None),
            P("expert", None, "mp"),
        ),
        out_specs=P(("groups", "expert", "mp"), None),
        check_vma=False,
    )
```

```python
import jax
import jax.numpy as jnp
from jax import lax
from jax.sharding import PartitionSpec as P

BF = jnp.bfloat16
F32 = jnp.float32


def dot_nt(a, b):
    return lax.dot_general(a, b, (((1,), (1,)), ((), ())), preferred_element_type=F32)


def dot_nn(a, b):
    return lax.dot_general(a, b, (((1,), (0,)), ((), ())), preferred_element_type=F32)


def local(
    tokens,
    routes,
    probs,
    w_gate,
    w_up,
    w_down,
    gate_left,
    gate_right,
    up_left,
    up_right,
    down_left,
    down_right,
):
    rows, width = tokens.shape
    exp_dev, _, cols = w_gate.shape
    rank = gate_left.shape[1]
    piece = gate_right.shape[1]
    block = gate_left.shape[2]
    groups = lax.axis_size("expert")
    parts = lax.axis_size("mp")
    chips = groups // 2
    experts = exp_dev * groups
    me_g = lax.axis_index("expert")
    me_m = lax.axis_index("mp")
    ranks = exp_dev * rank
    hid = exp_dev * cols

    def along_z(value, step):
        return lax.ppermute(value, "mp", [(i, (i + step) % parts) for i in range(parts)])

    def along_y(value, step):
        pairs = [(i, (i // 2 + step) % chips * 2 + i % 2) for i in range(groups)]
        return lax.ppermute(value, "expert", pairs)

    def other_core(value):
        return lax.ppermute(value, "expert", [(i, i ^ 1) for i in range(groups)])

    chosen = routes[:, :, None] == jnp.arange(experts, dtype=jnp.int32)
    weight = jnp.sum(jnp.where(chosen, probs[:, :, None], 0.0), axis=1)
    high = lax.reduce_precision(weight, 8, 7)
    low = (weight - high).astype(BF)
    side = jnp.concatenate([high.astype(BF), low], axis=1)
    pad = -(2 * experts) % 128
    sent = jnp.concatenate([tokens, jnp.pad(side, ((0, 0), (0, pad)))], axis=1)

    own = [sent] + [along_z(sent, k) for k in range(1, parts)]
    near = [own] + [[along_y(p, s) for p in own] for s in range(1, chips)]
    far = [[other_core(p) for p in line] for line in near]
    every = jnp.concatenate([p for half in (near, far) for line in half for p in line])
    total = every.shape[0]
    x = every[:, :width]
    side = every[:, width : width + 2 * experts].astype(F32)
    weight = side[:, :experts] + side[:, experts:]
    weight = lax.dynamic_slice(weight, (0, me_g * exp_dev), (total, exp_dev))

    small = jnp.stack([gate_right, up_right, down_left])
    small = small.reshape(3 * exp_dev * piece, parts, cols).swapaxes(0, 1)
    small = jnp.concatenate([small, small])
    small = [
        lax.dynamic_index_in_dim(small, me_m + k, 0, keepdims=False) for k in range(parts)
    ]
    small = [small[0]] + [along_z(small[k], k) for k in range(1, parts)]
    small = jnp.stack([small[-k % parts] for k in range(parts)] * 2)
    small = lax.dynamic_slice_in_dim(small, parts - me_m, parts, 0)
    small = small.reshape(parts, 3, exp_dev, piece, cols).transpose(1, 2, 0, 3, 4)
    small = small.reshape(3, ranks, cols)
    same = (jnp.arange(ranks) // rank)[:, None] == (jnp.arange(hid) // cols)[None, :]
    diag = jnp.where(same, jnp.tile(small, (1, 1, exp_dev)), jnp.zeros((), BF))

    def sum_parts(value):
        value = value.astype(BF)
        result = value.astype(F32)
        lines = value.reshape(-1, parts, rows, value.shape[1])
        for k in range(1, parts):
            result += along_z(jnp.roll(lines, k, axis=1).reshape(value.shape), k).astype(F32)
        return result.astype(BF)

    mine = lax.dynamic_slice(x, (0, me_m * block), (total, block))
    left = jnp.concatenate([gate_left.reshape(ranks, block), up_left.reshape(ranks, block)])
    inner = sum_parts(dot_nt(mine, left))

    gate_w = jnp.swapaxes(w_gate, 1, 2).reshape(hid, width)
    up_w = jnp.swapaxes(w_up, 1, 2).reshape(hid, width)
    gate_act = dot_nt(x, gate_w) + dot_nn(inner[:, :ranks], diag[0])
    up_act = dot_nt(x, up_w) + dot_nn(inner[:, ranks:], diag[1])
    scale = jnp.repeat(weight, cols, axis=1)
    hidden = (jax.nn.silu(gate_act) * up_act * scale).astype(BF)
    bottom = sum_parts(dot_nt(hidden, diag[2]))
    out = dot_nn(hidden, w_down.reshape(hid, width))
    extra = dot_nn(bottom, down_right.reshape(ranks, block))
    out = lax.dynamic_update_slice(
        out, extra + lax.dynamic_slice(out, (0, me_m * block), (total, block)), (0, me_m * block)
    ).astype(BF)

    out = out.reshape(2, chips, parts, rows, width)
    out = out[0].astype(F32) + other_core(out[1]).astype(F32)
    out = out.astype(BF)
    lines = []
    for k in range(parts):
        line = out[0, k].astype(F32)
        for s in range(1, chips):
            line += along_y(out[s, k], -s).astype(F32)
        lines.append(line)
    result = lines[0]
    for k in range(1, parts):
        result += along_z(lines[k].astype(BF), -k).astype(F32)
    return result.astype(BF)


def solution(mesh):
    return jax.shard_map(
        local,
        mesh=mesh,
        in_specs=(
            P(("groups", "expert", "mp"), None),
            P(("groups", "expert", "mp"), None),
            P(("groups", "expert", "mp"), None),
            P("expert", None, "mp"),
            P("expert", None, "mp"),
            P("expert", "mp", None),
            P("expert", None, "mp"),
            P("expert", "mp", None),
            P("expert", None, "mp"),
            P("expert", "mp", None),
            P("expert", "mp", None),
            P("expert", None, "mp"),
        ),
        out_specs=P(("groups", "expert", "mp"), None),
        check_vma=False,
    )
```

```python
import jax
import jax.numpy as jnp
from jax import lax
from jax.sharding import PartitionSpec as P

BF = jnp.bfloat16
F32 = jnp.float32


def dot_nt(a, b):
    return lax.dot_general(a, b, (((1,), (1,)), ((), ())), preferred_element_type=F32)


def dot_nn(a, b):
    return lax.dot_general(a, b, (((1,), (0,)), ((), ())), preferred_element_type=F32)


def local(
    tokens,
    routes,
    probs,
    w_gate,
    w_up,
    w_down,
    gate_left,
    gate_right,
    up_left,
    up_right,
    down_left,
    down_right,
):
    rows, width = tokens.shape
    exp_dev, _, cols = w_gate.shape
    rank = gate_left.shape[1]
    piece = gate_right.shape[1]
    block = gate_left.shape[2]
    parts = lax.axis_size("mp")
    chips = lax.axis_size("y")
    groups = chips * 2
    experts = exp_dev * groups
    me_g = lax.axis_index("y") * 2 + lax.axis_index("core")
    me_m = lax.axis_index("mp")
    ranks = exp_dev * rank
    hid = exp_dev * cols

    def along_z(value, step):
        return lax.ppermute(value, "mp", [(i, (i + step) % parts) for i in range(parts)])

    def other_core(value):
        return lax.ppermute(value, "core", [(0, 1), (1, 0)])

    def swap(value):
        return lax.all_to_all(value, ("y", "mp"), split_axis=0, concat_axis=0, tiled=True)

    chosen = routes[:, :, None] == jnp.arange(experts, dtype=jnp.int32)
    weight = jnp.sum(jnp.where(chosen, probs[:, :, None], 0.0), axis=1)
    high = lax.reduce_precision(weight, 8, 7)
    low = (weight - high).astype(BF)
    side = jnp.concatenate([high.astype(BF), low], axis=1)
    pad = -(2 * experts) % 128
    sent = jnp.concatenate([tokens, jnp.pad(side, ((0, 0), (0, pad)))], axis=1)

    near = swap(jnp.broadcast_to(sent, (chips * parts,) + sent.shape)).reshape(-1, sent.shape[1])
    every = jnp.concatenate([near, other_core(near)])
    total = every.shape[0]
    x = every[:, :width]
    side = every[:, width : width + 2 * experts].astype(F32)
    weight = side[:, :experts] + side[:, experts:]
    weight = lax.dynamic_slice(weight, (0, me_g * exp_dev), (total, exp_dev))

    small = jnp.stack([gate_right, up_right, down_left])
    small = small.reshape(3 * exp_dev * piece, parts, cols).swapaxes(0, 1)
    small = jnp.concatenate([small, small])
    small = [
        lax.dynamic_index_in_dim(small, me_m + k, 0, keepdims=False) for k in range(parts)
    ]
    small = [small[0]] + [along_z(small[k], k) for k in range(1, parts)]
    small = jnp.stack([small[-k % parts] for k in range(parts)] * 2)
    small = lax.dynamic_slice_in_dim(small, parts - me_m, parts, 0)
    small = small.reshape(parts, 3, exp_dev, piece, cols).transpose(1, 2, 0, 3, 4)
    small = small.reshape(3, ranks, cols)
    same = (jnp.arange(ranks) // rank)[:, None] == (jnp.arange(hid) // cols)[None, :]
    diag = jnp.where(same, jnp.tile(small, (1, 1, exp_dev)), jnp.zeros((), BF))

    def sum_parts(value):
        value = value.astype(BF)
        result = value.astype(F32)
        for k in range(1, parts):
            result += along_z(value, k).astype(F32)
        return result.astype(BF)

    mine = lax.dynamic_slice(x, (0, me_m * block), (total, block))
    left = jnp.concatenate([gate_left.reshape(ranks, block), up_left.reshape(ranks, block)])
    inner = sum_parts(dot_nt(mine, left))

    gate_w = jnp.swapaxes(w_gate, 1, 2).reshape(hid, width)
    up_w = jnp.swapaxes(w_up, 1, 2).reshape(hid, width)
    gate_act, up_act = lax.optimization_barrier((dot_nt(x, gate_w), dot_nt(x, up_w)))
    gate_act += dot_nn(inner[:, :ranks], diag[0])
    up_act += dot_nn(inner[:, ranks:], diag[1])
    scale = jnp.repeat(weight, cols, axis=1)
    hidden = (jax.nn.silu(gate_act) * up_act * scale).astype(BF)
    bottom = sum_parts(dot_nt(hidden, diag[2]))
    out = dot_nn(hidden, w_down.reshape(hid, width))
    extra = dot_nn(bottom, down_right.reshape(ranks, block))
    out = lax.dynamic_update_slice(
        out, extra + lax.dynamic_slice(out, (0, me_m * block), (total, block)), (0, me_m * block)
    ).astype(BF)

    out = out.reshape(2, chips * parts, rows, width)
    out = out[0].astype(F32) + other_core(out[1]).astype(F32)
    return jnp.sum(swap(out.astype(BF)).astype(F32), axis=0).astype(BF)


def solution(mesh):
    count = mesh.shape
    fine = jax.sharding.Mesh(
        mesh.devices.reshape(count["groups"], count["expert"] // 2, 2, count["mp"]),
        ("groups", "y", "core", "mp"),
    )
    expert = ("y", "core")
    return jax.shard_map(
        local,
        mesh=fine,
        in_specs=(
            P(("groups", "y", "core", "mp"), None),
            P(("groups", "y", "core", "mp"), None),
            P(("groups", "y", "core", "mp"), None),
            P(expert, None, "mp"),
            P(expert, None, "mp"),
            P(expert, "mp", None),
            P(expert, None, "mp"),
            P(expert, "mp", None),
            P(expert, None, "mp"),
            P(expert, "mp", None),
            P(expert, "mp", None),
            P(expert, None, "mp"),
        ),
        out_specs=P(("groups", "y", "core", "mp"), None),
        check_vma=False,
    )
```

```python
import functools

import jax
import jax.numpy as jnp
from jax import lax
from jax.experimental import pallas as pl
from jax.experimental.pallas import tpu as pltpu
from jax.sharding import PartitionSpec as P

BF = jnp.bfloat16
F32 = jnp.float32


def dot_nt(a, b):
    return lax.dot_general(a, b, (((1,), (1,)), ((), ())), preferred_element_type=F32)


def dot_nn(a, b):
    return lax.dot_general(a, b, (((1,), (0,)), ((), ())), preferred_element_type=F32)


def attach_kernel(experts, tokens_ref, routes_ref, probs_ref, out_ref):
    rows, width = tokens_ref.shape
    half = (out_ref.shape[1] - width) // 2
    out_ref[:, :width] = tokens_ref[...]
    routes = routes_ref[...]
    probs = probs_ref[...]
    ids = lax.broadcasted_iota(jnp.int32, (rows, half), 1)
    weight = jnp.zeros((rows, half), F32)
    for k in range(routes.shape[1]):
        weight += jnp.where(ids == routes[:, k : k + 1], probs[:, k : k + 1], 0.0)
    high = weight.astype(BF)
    low = (weight - high.astype(F32)).astype(BF)
    out_ref[:, width : width + half] = high
    out_ref[:, width + half :] = low


def attach(tokens, routes, probs, experts):
    rows, width = tokens.shape
    half = -(-experts // 128) * 128
    return pl.pallas_call(
        functools.partial(attach_kernel, experts),
        out_shape=jax.ShapeDtypeStruct((rows, width + 2 * half), BF),
        name="attach",
    )(tokens, routes, probs)


def after(value, earlier):
    return lax.optimization_barrier((value, earlier))[0]


def local(
    tokens,
    routes,
    probs,
    w_gate,
    w_up,
    w_down,
    gate_left,
    gate_right,
    up_left,
    up_right,
    down_left,
    down_right,
):
    rows, width = tokens.shape
    exp_dev, _, cols = w_gate.shape
    rank = gate_left.shape[1]
    piece = gate_right.shape[1]
    block = gate_left.shape[2]
    parts = lax.axis_size("mp")
    chips = lax.axis_size("y")
    groups = chips * 2
    experts = exp_dev * groups
    me_g = lax.axis_index("y") * 2 + lax.axis_index("core")
    me_m = lax.axis_index("mp")
    ranks = exp_dev * rank
    hid = exp_dev * cols

    def along_z(value, step):
        return lax.ppermute(value, "mp", [(i, (i + step) % parts) for i in range(parts)])

    def other_core(value):
        return lax.ppermute(value, "core", [(0, 1), (1, 0)])

    def along_y(value, step):
        return lax.ppermute(value, "y", [(i, (i + step) % chips) for i in range(chips)])

    sent = attach(tokens, routes, probs, experts)
    rest = jnp.concatenate([along_z(sent, k) for k in range(1, parts)])
    first = [sent] + [along_y(sent, s) for s in range(1, chips)]
    lines = [jnp.concatenate([sent, rest])]
    partner = [other_core(lines[0])]
    for s in range(1, chips):
        lines.append(jnp.concatenate([first[s], along_y(rest, s)]))
        partner.append(other_core(lines[s]))
    every = jnp.concatenate(lines + partner)
    total = every.shape[0]
    x = every[:, :width]
    half = (every.shape[1] - width) // 2
    weight = every[:, width : width + half].astype(F32) + every[:, width + half :].astype(F32)
    weight = lax.dynamic_slice(weight, (0, me_g * exp_dev), (total, exp_dev))

    small = jnp.stack([gate_right, up_right, down_left])
    small = small.reshape(3 * exp_dev * piece, parts, cols).swapaxes(0, 1)
    small = jnp.concatenate([small, small])
    small = [
        lax.dynamic_index_in_dim(small, me_m + k, 0, keepdims=False) for k in range(parts)
    ]
    small = after(small, partner[0])
    small = [small[0]] + [along_z(small[k], k) for k in range(1, parts)]
    small = jnp.stack([small[-k % parts] for k in range(parts)] * 2)
    small = lax.dynamic_slice_in_dim(small, parts - me_m, parts, 0)
    small = small.reshape(parts, 3, exp_dev, piece, cols).transpose(1, 2, 0, 3, 4)
    small = small.reshape(3, ranks, cols)
    same = (jnp.arange(ranks) // rank)[:, None] == (jnp.arange(hid) // cols)[None, :]
    diag = jnp.where(same, jnp.tile(small, (1, 1, exp_dev)), jnp.zeros((), BF))

    def sum_parts(value):
        value = value.astype(BF)
        result = value.astype(F32)
        lines = value.reshape(-1, parts, rows, value.shape[1])
        for k in range(1, parts):
            result += along_z(jnp.roll(lines, k, axis=1).reshape(value.shape), k).astype(F32)
        return result.astype(BF)

    mine = lax.dynamic_slice(x, (0, me_m * block), (total, block))
    left = jnp.concatenate([gate_left.reshape(ranks, block), up_left.reshape(ranks, block)])
    inner = sum_parts(dot_nt(mine, left))

    gate_w = jnp.swapaxes(w_gate, 1, 2).reshape(hid, width)
    up_w = jnp.swapaxes(w_up, 1, 2).reshape(hid, width)
    gate_act, up_act = lax.optimization_barrier((dot_nt(x, gate_w), dot_nt(x, up_w)))
    gate_act += dot_nn(inner[:, :ranks], diag[0])
    up_act += dot_nn(inner[:, ranks:], diag[1])
    scale = jnp.repeat(weight, cols, axis=1)
    hidden = (jax.nn.silu(gate_act) * up_act * scale).astype(BF)
    bottom = sum_parts(dot_nt(hidden, diag[2]))
    out = dot_nn(hidden, w_down.reshape(hid, width))
    extra = dot_nn(bottom, down_right.reshape(ranks, block))
    out = lax.dynamic_update_slice(
        out, extra + lax.dynamic_slice(out, (0, me_m * block), (total, block)), (0, me_m * block)
    ).astype(BF)

    out = out.reshape(2, chips, parts, rows, width)
    out = (out[0].astype(F32) + other_core(out[1]).astype(F32)).astype(BF)
    rest = out[0, 1:].astype(F32)
    back = [along_y(out[s, 1:], -s) for s in range(1, chips)]
    for piece in back:
        rest += piece.astype(F32)
    rest = rest.astype(BF)
    result = out[0, 0].astype(F32)
    for s in range(1, chips):
        result += along_y(after(out[s, 0], back[s - 1]), -s).astype(F32)
    for k in range(1, parts):
        result += along_z(rest[k - 1], -k).astype(F32)
    return result.astype(BF)


def solution(mesh):
    count = mesh.shape
    fine = jax.sharding.Mesh(
        mesh.devices.reshape(count["groups"], count["expert"] // 2, 2, count["mp"]),
        ("groups", "y", "core", "mp"),
    )
    expert = ("y", "core")
    return jax.shard_map(
        local,
        mesh=fine,
        in_specs=(
            P(("groups", "y", "core", "mp"), None),
            P(("groups", "y", "core", "mp"), None),
            P(("groups", "y", "core", "mp"), None),
            P(expert, None, "mp"),
            P(expert, None, "mp"),
            P(expert, "mp", None),
            P(expert, None, "mp"),
            P(expert, "mp", None),
            P(expert, None, "mp"),
            P(expert, "mp", None),
            P(expert, "mp", None),
            P(expert, None, "mp"),
        ),
        out_specs=P(("groups", "y", "core", "mp"), None),
        check_vma=False,
    )
```

```python
import functools

import jax
import jax.numpy as jnp
from jax import lax
from jax.experimental import pallas as pl
from jax.experimental.pallas import tpu as pltpu
from jax.sharding import PartitionSpec as P

BF = jnp.bfloat16
F32 = jnp.float32
VMEM_LIMIT = 40 * 1024 * 1024


def dot_nt(a, b):
    return lax.dot_general(a, b, (((1,), (1,)), ((), ())), preferred_element_type=F32)


def dot_nn(a, b):
    return lax.dot_general(a, b, (((1,), (0,)), ((), ())), preferred_element_type=F32)


def after(value, earlier):
    return lax.optimization_barrier((value, earlier))[0]


def half_of(part, parts):
    return lax.rem(part, parts) // (parts // 2)


def rotated(value, rows, parts, step):
    if step == 0:
        return value
    span = rows * parts
    lines = []
    for start in range(0, value.shape[0], span):
        cut = start + span - step * rows
        lines += [value[cut : start + span], value[start:cut]]
    return jnp.concatenate(lines)


def attach_kernel(parts, tokens_ref, routes_ref, probs_ref, *out_refs):
    rows, width = tokens_ref.shape
    wide = width // 2
    pair = out_refs[-1].shape[1] - wide
    me = lax.axis_index("mp")
    routes = routes_ref[...]
    probs = probs_ref[...]
    lane = lax.broadcasted_iota(jnp.int32, (rows, pair), 1)
    ids = jnp.where(lane < pair // 2, lane, lane - pair // 2)
    weight = jnp.zeros((rows, pair), F32)
    for k in range(routes.shape[1]):
        weight += jnp.where(ids == routes[:, k : k + 1], probs[:, k : k + 1], 0.0)
    high = weight.astype(BF).astype(F32)
    side = jnp.where(lane < pair // 2, high, weight - high).astype(BF)
    for k in range(parts):
        half = half_of(me + k, parts)
        one = pl.multiple_of(half * wide, 128)
        two = pl.multiple_of((1 - half) * wide, 128)
        out_refs[k][...] = tokens_ref[:, pl.ds(one, wide)]
        out_refs[parts + k][:, :wide] = tokens_ref[:, pl.ds(two, wide)]
        out_refs[parts + k][:, wide:] = side


def attach(tokens, routes, probs, experts, parts):
    rows, width = tokens.shape
    pair = 2 * (-(-experts // 64) * 64)
    outs = pl.pallas_call(
        functools.partial(attach_kernel, parts),
        out_shape=[jax.ShapeDtypeStruct((rows, width // 2), BF)] * parts
        + [jax.ShapeDtypeStruct((rows, width // 2 + pair), BF)] * parts,
        name="attach",
    )(tokens, routes, probs)
    return outs[:parts], outs[parts:]


def inner_kernel(parts, rows, count, *refs):
    lines, (gate_ref, up_ref), outs = refs[:count], refs[count : count + 2], refs[count + 2 :]
    exp_dev, rank, block = gate_ref.shape
    offset = pl.multiple_of(lax.rem(lax.axis_index("mp"), parts // 2) * block, 128)
    x = jnp.concatenate([line[:, pl.ds(offset, block)] for line in lines])
    left = jnp.concatenate(
        [ref[...].reshape(exp_dev * rank, block) for ref in (gate_ref, up_ref)]
    )
    value = dot_nt(x, left)
    for k in range(parts):
        outs[k][...] = rotated(value, rows, parts, k).astype(BF)


def inner_products(lines, gate_left, up_left, parts, rows):
    total = sum(line.shape[0] for line in lines)
    ranks = 2 * gate_left.shape[0] * gate_left.shape[1]
    return pl.pallas_call(
        functools.partial(inner_kernel, parts, rows, len(lines)),
        out_shape=[jax.ShapeDtypeStruct((total, ranks), BF)] * parts,
        compiler_params=pltpu.CompilerParams(vmem_limit_bytes=VMEM_LIMIT),
        name="inner",
    )(*lines, gate_left, up_left)


def raw_kernel(count, wide, half_ref, *refs):
    lines, (gate_ref, up_ref), rest = refs[:count], refs[count : count + 2], refs[count + 2 :]
    x = jnp.concatenate([line[:, :wide] for line in lines])
    gate, up = dot_nt(x, gate_ref[...]), dot_nt(x, up_ref[...])
    if len(rest) == 4:
        gate += rest[0][...]
        up += rest[1][...]
    rest[-2][...] = gate
    rest[-1][...] = up


def raw_products(half, lines, gate_w, up_w, earlier):
    hid, width = gate_w.shape
    wide = width // 2
    total = sum(line.shape[0] for line in lines)
    tile = hid // 3 if hid % 384 == 0 else hid
    weights = pl.BlockSpec((tile, wide), lambda i, half: (i, half[0]))
    result = pl.BlockSpec((total, tile), lambda i, half: (0, i))
    return pl.pallas_call(
        functools.partial(raw_kernel, len(lines), wide),
        grid_spec=pltpu.PrefetchScalarGridSpec(
            num_scalar_prefetch=1,
            grid=(hid // tile,),
            in_specs=[pl.BlockSpec(line.shape, lambda i, half: (0, 0)) for line in lines]
            + [weights] * 2
            + [result] * len(earlier),
            out_specs=[result] * 2,
        ),
        out_shape=[jax.ShapeDtypeStruct((total, hid), F32)] * 2,
        compiler_params=pltpu.CompilerParams(vmem_limit_bytes=VMEM_LIMIT),
        name="raw",
    )(half, *lines, gate_w, up_w, *earlier)


def hidden_kernel(parts, rows, count, exp_dev, pair, place_ref, *refs):
    lines, inner, rest = refs[:count], refs[count : count + parts], refs[count + parts :]
    gate_ref, up_ref, diag_ref, hidden_ref = rest[:4]
    outs = rest[4:]
    hid = gate_ref.shape[1]
    ranks = diag_ref.shape[1]
    wide = lines[0].shape[1] - pair
    total = sum(ref[...].astype(F32) for ref in inner).astype(BF)
    gate = gate_ref[...] + dot_nn(total[:, :ranks], diag_ref[0])
    up = up_ref[...] + dot_nn(total[:, ranks:], diag_ref[1])
    lane = lax.broadcasted_iota(jnp.int32, (pair, hid), 0)
    lane = jnp.where(lane < pair // 2, lane, lane - pair // 2)
    owner = lax.broadcasted_iota(jnp.int32, (pair, hid), 1) // (hid // exp_dev)
    pick = (lane == owner + place_ref[0]).astype(F32).astype(BF)
    scale = dot_nn(jnp.concatenate([line[:, wide:] for line in lines]), pick)
    hidden = (gate / (1.0 + jnp.exp(-gate)) * up * scale).astype(BF)
    hidden_ref[...] = hidden
    value = dot_nt(hidden, diag_ref[2])
    for k in range(parts):
        outs[k][...] = rotated(value, rows, parts, k).astype(BF)


def hidden_units(place, lines, inner, raw, diag, parts, rows, exp_dev, pair):
    total, hid = raw[0].shape
    ranks = diag.shape[1]
    vmem = pl.BlockSpec(memory_space=pltpu.VMEM)
    return pl.pallas_call(
        functools.partial(hidden_kernel, parts, rows, len(lines), exp_dev, pair),
        in_specs=[pl.BlockSpec(memory_space=pltpu.SMEM)]
        + [vmem] * (len(lines) + len(inner) + 3),
        out_shape=[jax.ShapeDtypeStruct((total, hid), BF)]
        + [jax.ShapeDtypeStruct((total, ranks), BF)] * parts,
        compiler_params=pltpu.CompilerParams(vmem_limit_bytes=VMEM_LIMIT),
        name="hidden",
    )(place, *lines, *inner, *raw, diag)


def down_kernel(place_ref, hidden_ref, down_ref, *refs):
    near_ref, far_ref = refs[-2:]
    near = near_ref.shape[0]
    value = dot_nn(hidden_ref[...], down_ref[...])
    near_ref[...] = value[:near]
    far_ref[...] = value[near:].astype(BF)
    if len(refs) > 2:
        right_ref, bottom = refs[0], refs[1:-2]
        step = pl.program_id(0) - place_ref[1]

        @pl.when((step >= 0) & (step < place_ref[2]))
        def _():
            low = sum(ref[...].astype(F32) for ref in bottom).astype(BF)
            extra = value + dot_nn(low, right_ref[...])
            near_ref[...] = extra[:near]
            far_ref[...] = extra[near:].astype(BF)


def down_products(place, hidden, down_w, right, bottom):
    total, hid = hidden.shape
    wide = down_w.shape[1] // 2
    tile = min(512, right.shape[1])
    steps = wide // tile
    last = right.shape[1] // tile - 1
    specs = [
        pl.BlockSpec((total, hid), lambda i, place: (0, 0)),
        pl.BlockSpec((hid, tile), lambda i, place: (0, place[0] * steps + i)),
    ]
    args = [hidden, down_w]
    if bottom:
        specs.append(
            pl.BlockSpec(
                (right.shape[0], tile),
                lambda i, place: (0, jnp.minimum(jnp.maximum(i - place[1], 0), last)),
            )
        )
        specs += [pl.BlockSpec(b.shape, lambda i, place: (0, 0)) for b in bottom]
        args += [right, *bottom]
    return pl.pallas_call(
        down_kernel,
        grid_spec=pltpu.PrefetchScalarGridSpec(
            num_scalar_prefetch=1,
            grid=(steps,),
            in_specs=specs,
            out_specs=[pl.BlockSpec((total // 2, tile), lambda i, place: (0, i))] * 2,
        ),
        out_shape=[
            jax.ShapeDtypeStruct((total // 2, wide), F32),
            jax.ShapeDtypeStruct((total // 2, wide), BF),
        ],
        compiler_params=pltpu.CompilerParams(vmem_limit_bytes=VMEM_LIMIT),
        name="down",
    )(place, *args)


def local(
    tokens,
    routes,
    probs,
    w_gate,
    w_up,
    w_down,
    gate_left,
    gate_right,
    up_left,
    up_right,
    down_left,
    down_right,
):
    rows, width = tokens.shape
    exp_dev, _, cols = w_gate.shape
    rank = gate_left.shape[1]
    piece = gate_right.shape[1]
    block = gate_left.shape[2]
    parts = lax.axis_size("mp")
    chips = lax.axis_size("y")
    experts = exp_dev * chips * 2
    me_g = lax.axis_index("y") * 2 + lax.axis_index("core")
    me_m = lax.axis_index("mp")
    ranks = exp_dev * rank
    hid = exp_dev * cols
    wide = width // 2

    def along_z(value, step):
        return lax.ppermute(value, "mp", [(i, (i + step) % parts) for i in range(parts)])

    def along_y(value, step):
        return lax.ppermute(value, "y", [(i, (i + step) % chips) for i in range(chips)])

    def other_core(value):
        return lax.ppermute(value, "core", [(0, 1), (1, 0)])

    def gather(own, pieces):
        line = jnp.concatenate([own] + pieces)
        lines = [line] + [along_y(line, s) for s in range(1, chips)]
        return lines + [other_core(line) for line in lines]

    one, two = attach(tokens, routes, probs, experts, parts)
    pieces = [along_z(one[k], k) for k in range(1, parts)]
    two = [two[0]] + list(after(tuple(two[1:]), pieces[0]))
    lines = gather(one[0], pieces)
    pieces = [along_z(two[k], k) for k in range(1, parts)]
    lines_two = gather(two[0], pieces)

    small = jnp.stack([gate_right, up_right, down_left])
    small = small.reshape(3 * exp_dev * piece, parts, cols).swapaxes(0, 1)
    small = jnp.concatenate([small, small])
    small = [
        lax.dynamic_index_in_dim(small, me_m + k, 0, keepdims=False) for k in range(parts)
    ]
    small = after(tuple(small), pieces[-1])
    small = [small[0]] + [along_z(small[k], k) for k in range(1, parts)]
    small = jnp.stack([small[-k % parts] for k in range(parts)] * 2)
    small = lax.dynamic_slice_in_dim(small, parts - me_m, parts, 0)
    small = small.reshape(parts, 3, exp_dev, piece, cols).transpose(1, 2, 0, 3, 4)
    small = small.reshape(3, ranks, cols)
    same = (jnp.arange(ranks) // rank)[:, None] == (jnp.arange(hid) // cols)[None, :]
    diag = jnp.where(same, jnp.tile(small, (1, 1, exp_dev)), jnp.zeros((), BF))

    half = half_of(me_m, parts)
    inner = inner_products(lines, gate_left, up_left, parts, rows)
    inner = [inner[0]] + [along_z(inner[k], k) for k in range(1, parts)]
    gate_w = jnp.swapaxes(w_gate, 1, 2).reshape(hid, width)
    up_w = jnp.swapaxes(w_up, 1, 2).reshape(hid, width)
    raw = raw_products(half[None], lines, gate_w, up_w, ())
    raw = raw_products(1 - half[None], lines_two, gate_w, up_w, raw)
    first_expert = (me_g * exp_dev)[None]
    hidden, *bottom = hidden_units(
        first_expert, lines_two, inner, raw, diag, parts, rows, exp_dev, two[0].shape[1] - wide
    )
    bottom = [bottom[0]] + [along_z(bottom[k], k) for k in range(1, parts)]

    down_w = w_down.reshape(hid, width)
    right = down_right.reshape(ranks, block)
    tile = min(512, block)
    tiles = block // tile
    start = lax.rem(me_m, parts // 2) * tiles

    def combine(near, far):
        out = (near + other_core(far).astype(F32)).reshape(chips, parts, rows, wide)
        line = out[0]
        for s in range(1, chips):
            line += along_y(out[s].astype(BF), -s).astype(F32)
        return [line[0]] + [along_z(line[k].astype(BF), -k).astype(F32) for k in range(1, parts)]

    tiles = jnp.int32(tiles)
    got_one = combine(*down_products(jnp.stack([1 - half, start, tiles]), hidden, down_w, right, ()))
    got_two = combine(*down_products(jnp.stack([half, start, tiles]), hidden, down_w, right, bottom))
    result = []
    for side in range(2):
        total = jnp.zeros((rows, wide), F32)
        for k in range(parts):
            total += jnp.where(half_of(me_m + k, parts) == side, got_two[k], got_one[k])
        result.append(total)
    return jnp.concatenate(result, axis=1).astype(BF)


def solution(mesh):
    count = mesh.shape
    fine = jax.sharding.Mesh(
        mesh.devices.reshape(count["groups"], count["expert"] // 2, 2, count["mp"]),
        ("groups", "y", "core", "mp"),
    )
    expert = ("y", "core")
    return jax.shard_map(
        local,
        mesh=fine,
        in_specs=(
            P(("groups", "y", "core", "mp"), None),
            P(("groups", "y", "core", "mp"), None),
            P(("groups", "y", "core", "mp"), None),
            P(expert, None, "mp"),
            P(expert, None, "mp"),
            P(expert, "mp", None),
            P(expert, None, "mp"),
            P(expert, "mp", None),
            P(expert, None, "mp"),
            P(expert, "mp", None),
            P(expert, "mp", None),
            P(expert, None, "mp"),
        ),
        out_specs=P(("groups", "y", "core", "mp"), None),
        check_vma=False,
    )
```

```python
import functools

import jax
import jax.numpy as jnp
from jax import lax
from jax.experimental import pallas as pl
from jax.experimental.pallas import tpu as pltpu
from jax.sharding import PartitionSpec as P

BF = jnp.bfloat16
F32 = jnp.float32
VMEM_LIMIT = 24 * 1024 * 1024
STREAM_LIMIT = 56 * 1024 * 1024


def dot_nt(a, b):
    return lax.dot_general(a, b, (((1,), (1,)), ((), ())), preferred_element_type=F32)


def dot_nn(a, b):
    return lax.dot_general(a, b, (((1,), (0,)), ((), ())), preferred_element_type=F32)


def after(value, earlier):
    return lax.optimization_barrier((value, earlier))[0]


def rotated(value, rows, parts, step):
    if step == 0:
        return value
    span = rows * parts
    lines = []
    for start in range(0, value.shape[0], span):
        cut = start + span - step * rows
        lines += [value[cut : start + span], value[start:cut]]
    return jnp.concatenate(lines)


def attach_kernel(tokens_ref, routes_ref, probs_ref, out_ref):
    rows, width = tokens_ref.shape
    pair = out_ref.shape[1] - width
    out_ref[:, :width] = tokens_ref[...]
    routes = routes_ref[...]
    probs = probs_ref[...]
    lane = lax.broadcasted_iota(jnp.int32, (rows, pair), 1)
    ids = jnp.where(lane < pair // 2, lane, lane - pair // 2)
    weight = jnp.zeros((rows, pair), F32)
    for k in range(routes.shape[1]):
        weight += jnp.where(ids == routes[:, k : k + 1], probs[:, k : k + 1], 0.0)
    high = weight.astype(BF).astype(F32)
    out_ref[:, width:] = jnp.where(lane < pair // 2, high, weight - high).astype(BF)


def attach(tokens, routes, probs, pair):
    rows, width = tokens.shape
    return pl.pallas_call(
        attach_kernel,
        out_shape=jax.ShapeDtypeStruct((rows, width + pair), BF),
        name="attach",
    )(tokens, routes, probs)


def cut_kernel(parts, *refs):
    ins, outs = refs[:3], refs[3:]
    exp_dev, piece, hid = ins[0].shape
    cols = hid // parts
    me = lax.axis_index("mp")
    for n, ref in enumerate(ins):
        value = ref[...].reshape(exp_dev * piece, hid).astype(F32)
        blocks = [value[:, j * cols : (j + 1) * cols] for j in range(parts)]
        for k in range(parts):
            target = lax.rem(me + k, parts)
            block = blocks[0]
            for j in range(1, parts):
                block = jnp.where(target == j, blocks[j], block)
            outs[k][n] = block.astype(BF)


def cut(factors, parts):
    exp_dev, piece, hid = factors[0].shape
    return pl.pallas_call(
        functools.partial(cut_kernel, parts),
        out_shape=[jax.ShapeDtypeStruct((3, exp_dev * piece, hid // parts), BF)] * parts,
        name="cut",
    )(*factors)


def spread_kernel(parts, exp_dev, *refs):
    pieces, out_ref = refs[:-1], refs[-1]
    _, ranks, hid = out_ref.shape
    rank = ranks // exp_dev
    piece = rank // parts
    me = lax.axis_index("mp")
    row = lax.broadcasted_iota(jnp.int32, (ranks, ranks), 0)
    col = lax.broadcasted_iota(jnp.int32, (ranks, ranks), 1)
    step = lax.rem(me - row % rank // piece + parts, parts)
    source = (step * exp_dev + row // rank) * piece + row % piece
    order = (col == source).astype(F32).astype(BF)
    own = (
        lax.broadcasted_iota(jnp.int32, (ranks, hid), 0) // rank
        == lax.broadcasted_iota(jnp.int32, (ranks, hid), 1) // (hid // exp_dev)
    )
    for n in range(3):
        value = dot_nn(order, jnp.concatenate([p[n].astype(F32) for p in pieces]).astype(BF))
        value = jnp.concatenate([value] * exp_dev, axis=1)
        out_ref[n] = jnp.where(own, value, 0.0).astype(BF)


def spread(pieces, parts, exp_dev):
    _, span, cols = pieces[0].shape
    return pl.pallas_call(
        functools.partial(spread_kernel, parts, exp_dev),
        out_shape=jax.ShapeDtypeStruct((3, span * parts, cols * exp_dev), BF),
        name="spread",
    )(*pieces)


def inner_kernel(parts, rows, count, *refs):
    lines, (gate_ref, up_ref), outs = refs[:count], refs[count : count + 2], refs[count + 2 :]
    exp_dev, rank, block = gate_ref.shape
    offset = pl.multiple_of(lax.axis_index("mp") * block, 128)
    x = jnp.concatenate([line[:, pl.ds(offset, block)] for line in lines])
    left = jnp.concatenate(
        [ref[...].reshape(exp_dev * rank, block) for ref in (gate_ref, up_ref)]
    )
    value = dot_nt(x, left)
    for k in range(parts):
        outs[k][...] = rotated(value, rows, parts, k).astype(BF)


def inner_products(lines, gate_left, up_left, parts, rows):
    total = sum(line.shape[0] for line in lines)
    ranks = 2 * gate_left.shape[0] * gate_left.shape[1]
    return pl.pallas_call(
        functools.partial(inner_kernel, parts, rows, len(lines)),
        out_shape=[jax.ShapeDtypeStruct((total, ranks), BF)] * parts,
        compiler_params=pltpu.CompilerParams(vmem_limit_bytes=VMEM_LIMIT),
        name="inner",
    )(*lines, gate_left, up_left)


def raw_kernel(count, *refs):
    lines, (gate_w, up_w, gate_ref, up_ref) = refs[:count], refs[count:]
    x = jnp.concatenate([line[:, : gate_w.shape[1]] for line in lines])
    gate_ref[...] = dot_nt(x, gate_w[...])
    up_ref[...] = dot_nt(x, up_w[...])


def raw_products(lines, gate_w, up_w):
    hid, width = gate_w.shape
    total = sum(line.shape[0] for line in lines)
    tile = hid // 3 if hid % 384 == 0 else hid
    weights = pl.BlockSpec((tile, width), lambda i: (i, 0))
    result = pl.BlockSpec((total, tile), lambda i: (0, i))
    return pl.pallas_call(
        functools.partial(raw_kernel, len(lines)),
        grid=(hid // tile,),
        in_specs=[pl.BlockSpec(line.shape, lambda i: (0, 0)) for line in lines] + [weights] * 2,
        out_specs=[result] * 2,
        out_shape=[jax.ShapeDtypeStruct((total, hid), F32)] * 2,
        compiler_params=pltpu.CompilerParams(vmem_limit_bytes=STREAM_LIMIT),
        name="raw",
    )(*lines, gate_w, up_w)


def hidden_kernel(parts, rows, count, exp_dev, pair, place_ref, *refs):
    lines, inner, rest = refs[:count], refs[count : count + parts], refs[count + parts :]
    gate_ref, up_ref, diag_ref, hidden_ref = rest[:4]
    outs = rest[4:]
    hid = gate_ref.shape[1]
    ranks = diag_ref.shape[1]
    wide = lines[0].shape[1] - pair
    total = sum(ref[...].astype(F32) for ref in inner).astype(BF)
    gate = gate_ref[...] + dot_nn(total[:, :ranks], diag_ref[0])
    up = up_ref[...] + dot_nn(total[:, ranks:], diag_ref[1])
    lane = lax.broadcasted_iota(jnp.int32, (pair, hid), 0)
    lane = jnp.where(lane < pair // 2, lane, lane - pair // 2)
    owner = lax.broadcasted_iota(jnp.int32, (pair, hid), 1) // (hid // exp_dev)
    pick = (lane == owner + place_ref[0]).astype(F32).astype(BF)
    scale = dot_nn(jnp.concatenate([line[:, wide:] for line in lines]), pick)
    hidden = (gate / (1.0 + jnp.exp(-gate)) * up * scale).astype(BF)
    hidden_ref[...] = hidden
    value = dot_nt(hidden, diag_ref[2])
    for k in range(parts):
        outs[k][...] = rotated(value, rows, parts, k).astype(BF)


def hidden_units(place, lines, inner, raw, diag, parts, rows, exp_dev, pair):
    total, hid = raw[0].shape
    ranks = diag.shape[1]
    vmem = pl.BlockSpec(memory_space=pltpu.VMEM)
    return pl.pallas_call(
        functools.partial(hidden_kernel, parts, rows, len(lines), exp_dev, pair),
        in_specs=[pl.BlockSpec(memory_space=pltpu.SMEM)]
        + [vmem] * (len(lines) + len(inner) + 3),
        out_shape=[jax.ShapeDtypeStruct((total, hid), BF)]
        + [jax.ShapeDtypeStruct((total, ranks), BF)] * parts,
        compiler_params=pltpu.CompilerParams(vmem_limit_bytes=VMEM_LIMIT),
        name="hidden",
    )(place, *lines, *inner, *raw, diag)


def down_kernel(hidden_ref, down_ref, near_ref, far_ref):
    near = near_ref.shape[0]
    value = dot_nn(hidden_ref[...], down_ref[...])
    near_ref[...] = value[:near]
    far_ref[...] = value[near:].astype(BF)


def down_products(hidden, down_w):
    total, hid = hidden.shape
    width = down_w.shape[1]
    tile = 1024
    return pl.pallas_call(
        down_kernel,
        grid=(width // tile,),
        in_specs=[
            pl.BlockSpec((total, hid), lambda i: (0, 0)),
            pl.BlockSpec((hid, tile), lambda i: (0, i)),
        ],
        out_specs=[pl.BlockSpec((total // 2, tile), lambda i: (0, i))] * 2,
        out_shape=[
            jax.ShapeDtypeStruct((total // 2, width), F32),
            jax.ShapeDtypeStruct((total // 2, width), BF),
        ],
        compiler_params=pltpu.CompilerParams(vmem_limit_bytes=STREAM_LIMIT),
        name="down",
    )(hidden, down_w)


def extra_kernel(right_ref, *refs):
    bottom, (near_ref, far_ref) = refs[:-2], refs[-2:]
    near = near_ref.shape[0]
    low = sum(ref[...].astype(F32) for ref in bottom).astype(BF)
    value = dot_nn(low, right_ref[...])
    near_ref[...] = value[:near]
    far_ref[...] = value[near:].astype(BF)


def extra_products(right, bottom):
    total = bottom[0].shape[0]
    block = right.shape[1]
    return pl.pallas_call(
        extra_kernel,
        out_shape=[
            jax.ShapeDtypeStruct((total // 2, block), F32),
            jax.ShapeDtypeStruct((total // 2, block), BF),
        ],
        compiler_params=pltpu.CompilerParams(vmem_limit_bytes=VMEM_LIMIT),
        name="extra",
    )(right, *bottom)


def merge_kernel(own_ref, back_ref, extra_ref, *out_refs):
    block = extra_ref.shape[2]
    offset = pl.multiple_of(lax.axis_index("mp") * block, 128)
    for k, out_ref in enumerate(out_refs):
        total = own_ref[k]
        if k > 0:
            total += back_ref[k - 1]
        out_ref[...] = total.astype(out_ref.dtype)
        low = own_ref[k, :, pl.ds(offset, block)] + extra_ref[k]
        if k > 0:
            low += back_ref[k - 1, :, pl.ds(offset, block)]
        out_ref[:, pl.ds(offset, block)] = low.astype(out_ref.dtype)


def merge(own, back, extra):
    parts, rows, width = own.shape
    return pl.pallas_call(
        merge_kernel,
        out_shape=[jax.ShapeDtypeStruct((rows, width), F32)]
        + [jax.ShapeDtypeStruct((rows, width), BF)] * (parts - 1),
        compiler_params=pltpu.CompilerParams(vmem_limit_bytes=VMEM_LIMIT),
        name="merge",
    )(own, back, extra)


def local(
    tokens,
    routes,
    probs,
    w_gate,
    w_up,
    w_down,
    gate_left,
    gate_right,
    up_left,
    up_right,
    down_left,
    down_right,
):
    rows, width = tokens.shape
    exp_dev, _, cols = w_gate.shape
    rank = gate_left.shape[1]
    block = gate_left.shape[2]
    parts = lax.axis_size("mp")
    chips = lax.axis_size("y")
    experts = exp_dev * chips * 2
    me_g = lax.axis_index("y") * 2 + lax.axis_index("core")
    ranks = exp_dev * rank
    hid = exp_dev * cols

    def along_z(value, step):
        return lax.ppermute(value, "mp", [(i, (i + step) % parts) for i in range(parts)])

    def along_y(value, step):
        return lax.ppermute(value, "y", [(i, (i + step) % chips) for i in range(chips)])

    def other_core(value):
        return lax.ppermute(value, "core", [(0, 1), (1, 0)])

    pair = 2 * (-(-experts // 64) * 64)
    sent = attach(tokens, routes, probs, pair)
    arrived = [along_z(sent, k) for k in range(1, parts)]
    first = [along_y(sent, s) for s in range(1, chips)]
    rest = jnp.concatenate(arrived)
    lines = [jnp.concatenate([sent, rest])]
    partner = [other_core(lines[0])]
    for s in range(1, chips):
        lines.append(jnp.concatenate([first[s - 1], along_y(rest, s)]))
        partner.append(other_core(lines[s]))
    lines += partner

    small = cut((gate_right, up_right, down_left), parts)
    small = after(tuple(small), arrived[-1])
    small = [small[0]] + [along_z(small[k], k) for k in range(1, parts)]

    inner = inner_products(lines, gate_left, up_left, parts, rows)
    inner = [inner[0]] + [along_z(inner[k], k) for k in range(1, parts)]
    gate_w = jnp.swapaxes(w_gate, 1, 2).reshape(hid, width)
    up_w = jnp.swapaxes(w_up, 1, 2).reshape(hid, width)
    raw = raw_products(lines, gate_w, up_w)
    diag = spread(after(tuple(small), raw[0]), parts, exp_dev)
    first_expert = (me_g * exp_dev)[None]
    hidden, *bottom = hidden_units(
        first_expert, lines, inner, raw, diag, parts, rows, exp_dev, pair
    )
    bottom = [bottom[0]] + [along_z(bottom[k], k) for k in range(1, parts)]

    near, far = down_products(hidden, w_down.reshape(hid, width))
    out = (near + other_core(far).astype(F32)).reshape(chips, parts, rows, width)
    back = [along_y(out[s, 1:].astype(BF), -s) for s in range(1, chips)]

    bottom = after(tuple(bottom), out)
    near, far = extra_products(down_right.reshape(ranks, block), bottom)
    extra = (near + other_core(far).astype(F32)).reshape(chips, parts, rows, block)
    total = extra[0]
    for s in range(1, chips):
        total += along_y(extra[s].astype(BF), -s).astype(F32)

    own = [along_y(after(out[s, 0].astype(BF), back[s - 1]), -s) for s in range(1, chips)]
    back = sum(piece.astype(F32) for piece in back)
    result, *pieces = merge(out[0], back, total)
    for piece in own:
        result += piece.astype(F32)
    for k in range(1, parts):
        result += along_z(pieces[k - 1], -k).astype(F32)
    return result.astype(BF)


def solution(mesh):
    count = mesh.shape
    fine = jax.sharding.Mesh(
        mesh.devices.reshape(count["groups"], count["expert"] // 2, 2, count["mp"]),
        ("groups", "y", "core", "mp"),
    )
    expert = ("y", "core")
    return jax.shard_map(
        local,
        mesh=fine,
        in_specs=(
            P(("groups", "y", "core", "mp"), None),
            P(("groups", "y", "core", "mp"), None),
            P(("groups", "y", "core", "mp"), None),
            P(expert, None, "mp"),
            P(expert, None, "mp"),
            P(expert, "mp", None),
            P(expert, None, "mp"),
            P(expert, "mp", None),
            P(expert, None, "mp"),
            P(expert, "mp", None),
            P(expert, "mp", None),
            P(expert, None, "mp"),
        ),
        out_specs=P(("groups", "y", "core", "mp"), None),
        check_vma=False,
    )
```

```python
import functools

import jax
import jax.numpy as jnp
from jax import lax
from jax.experimental import pallas as pl
from jax.experimental.pallas import tpu as pltpu
from jax.sharding import PartitionSpec as P

BF = jnp.bfloat16
F32 = jnp.float32
PIECES = 4
VMEM_LIMIT = 16 * 1024 * 1024
BRIEF = pl.CostEstimate(flops=1, bytes_accessed=1, transcendentals=0)


def dot_nt(a, b):
    return lax.dot_general(a, b, (((1,), (1,)), ((), ())), preferred_element_type=F32)


def dot_nn(a, b):
    return lax.dot_general(a, b, (((1,), (0,)), ((), ())), preferred_element_type=F32)


def in_hbm(*values):
    return [pltpu.with_memory_space_constraint(v, pltpu.HBM) for v in values]


def after(value, earlier):
    return lax.optimization_barrier((value, earlier))[0]


def rotated(value, rows, parts, step):
    if step == 0:
        return value
    span = rows * parts
    lines = []
    for start in range(0, value.shape[0], span):
        cut = start + span - step * rows
        lines += [value[cut : start + span], value[start:cut]]
    return jnp.concatenate(lines)


def attach_kernel(tokens_ref, routes_ref, probs_ref, out_ref):
    rows, width = tokens_ref.shape
    pair = out_ref.shape[1] - width
    out_ref[:, :width] = tokens_ref[...]
    routes = routes_ref[...]
    probs = probs_ref[...]
    lane = lax.broadcasted_iota(jnp.int32, (rows, pair), 1)
    ids = jnp.where(lane < pair // 2, lane, lane - pair // 2)
    weight = jnp.zeros((rows, pair), F32)
    for k in range(routes.shape[1]):
        weight += jnp.where(ids == routes[:, k : k + 1], probs[:, k : k + 1], 0.0)
    high = weight.astype(BF).astype(F32)
    out_ref[:, width:] = jnp.where(lane < pair // 2, high, weight - high).astype(BF)


def attach(tokens, routes, probs, pair):
    rows, width = tokens.shape
    return pl.pallas_call(
        attach_kernel,
        out_shape=jax.ShapeDtypeStruct((rows, width + pair), BF),
        cost_estimate=BRIEF,
        name="attach",
    )(*in_hbm(tokens, routes, probs))


def cut_kernel(parts, *refs):
    ins, outs = refs[:3], refs[3:]
    exp_dev, piece, hid = ins[0].shape
    cols = hid // parts
    me = lax.axis_index("mp")
    for n, ref in enumerate(ins):
        value = ref[...].reshape(exp_dev * piece, hid).astype(F32)
        blocks = [value[:, j * cols : (j + 1) * cols] for j in range(parts)]
        for k in range(parts):
            target = lax.rem(me + k, parts)
            block = blocks[0]
            for j in range(1, parts):
                block = jnp.where(target == j, blocks[j], block)
            outs[k][n] = block.astype(BF)


def cut(factors, parts):
    exp_dev, piece, hid = factors[0].shape
    return pl.pallas_call(
        functools.partial(cut_kernel, parts),
        out_shape=[jax.ShapeDtypeStruct((3, exp_dev * piece, hid // parts), BF)] * parts,
        cost_estimate=BRIEF,
        name="cut",
    )(*in_hbm(*factors))


def spread_kernel(parts, exp_dev, *refs):
    pieces, out_ref = refs[:-1], refs[-1]
    _, ranks, hid = out_ref.shape
    rank = ranks // exp_dev
    piece = rank // parts
    me = lax.axis_index("mp")
    row = lax.broadcasted_iota(jnp.int32, (ranks, ranks), 0)
    col = lax.broadcasted_iota(jnp.int32, (ranks, ranks), 1)
    step = lax.rem(me - row % rank // piece + parts, parts)
    source = (step * exp_dev + row // rank) * piece + row % piece
    order = (col == source).astype(F32).astype(BF)
    own = (
        lax.broadcasted_iota(jnp.int32, (ranks, hid), 0) // rank
        == lax.broadcasted_iota(jnp.int32, (ranks, hid), 1) // (hid // exp_dev)
    )
    for n in range(3):
        value = dot_nn(order, jnp.concatenate([p[n].astype(F32) for p in pieces]).astype(BF))
        value = jnp.concatenate([value] * exp_dev, axis=1)
        out_ref[n] = jnp.where(own, value, 0.0).astype(BF)


def spread(pieces, parts, exp_dev):
    _, span, cols = pieces[0].shape
    return pl.pallas_call(
        functools.partial(spread_kernel, parts, exp_dev),
        out_shape=jax.ShapeDtypeStruct((3, span * parts, cols * exp_dev), BF),
        cost_estimate=BRIEF,
        name="spread",
    )(*pieces)


def inner_kernel(parts, rows, count, *refs):
    lines, (gate_ref, up_ref), outs = refs[:count], refs[count : count + 2], refs[count + 2 :]
    exp_dev, rank, block = gate_ref.shape
    offset = pl.multiple_of(lax.axis_index("mp") * block, 128)
    x = jnp.concatenate([line[:, pl.ds(offset, block)] for line in lines])
    left = jnp.concatenate(
        [ref[...].reshape(exp_dev * rank, block) for ref in (gate_ref, up_ref)]
    )
    value = dot_nt(x, left)
    for k in range(parts):
        outs[k][...] = rotated(value, rows, parts, k).astype(BF)


def inner_products(lines, gate_left, up_left, parts, rows):
    total = sum(line.shape[0] for line in lines)
    ranks = 2 * gate_left.shape[0] * gate_left.shape[1]
    return pl.pallas_call(
        functools.partial(inner_kernel, parts, rows, len(lines)),
        out_shape=[jax.ShapeDtypeStruct((total, ranks), BF)] * parts,
        compiler_params=pltpu.CompilerParams(vmem_limit_bytes=VMEM_LIMIT),
        cost_estimate=BRIEF,
        name="inner",
    )(*lines, gate_left, up_left)


def load_kernel(count, *refs):
    sources, targets, sems = refs[:count], refs[count:-1], refs[-1]
    copies = []
    for n in range(count):
        step = sources[n].shape[0] // PIECES
        for i in range(PIECES):
            span = pl.ds(i * step, step)
            copies.append(
                pltpu.make_async_copy(
                    sources[n].at[span], targets[n].at[span], sems.at[n * PIECES + i]
                )
            )
    for copy in copies:
        copy.start()
    for copy in copies:
        copy.wait()


def load(*weights):
    count = len(weights)
    return pl.pallas_call(
        functools.partial(load_kernel, count),
        in_specs=[pl.BlockSpec(memory_space=pltpu.HBM)] * count,
        out_specs=[pl.BlockSpec(memory_space=pltpu.VMEM)] * count,
        out_shape=[pltpu.VMEM(w.shape, w.dtype) for w in weights],
        scratch_shapes=[pltpu.SemaphoreType.DMA((count * PIECES,))],
        compiler_params=pltpu.CompilerParams(vmem_limit_bytes=VMEM_LIMIT),
        cost_estimate=BRIEF,
        name="load",
    )(*in_hbm(*weights))


def raw_kernel(count, *refs):
    lines, (gate_w, up_w, gate_ref, up_ref) = refs[:count], refs[count:]
    hid, width = gate_w.shape
    x = jnp.concatenate([line[:, :width] for line in lines])
    tile = hid // 3 if hid % 384 == 0 else hid
    for i in range(hid // tile):
        span = slice(i * tile, (i + 1) * tile)
        gate_ref[:, span] = dot_nt(x, gate_w[span])
        up_ref[:, span] = dot_nt(x, up_w[span])


def raw_products(lines, gate_w, up_w):
    hid = gate_w.shape[0]
    total = sum(line.shape[0] for line in lines)
    return pl.pallas_call(
        functools.partial(raw_kernel, len(lines)),
        out_shape=[jax.ShapeDtypeStruct((total, hid), F32)] * 2,
        compiler_params=pltpu.CompilerParams(vmem_limit_bytes=VMEM_LIMIT),
        cost_estimate=BRIEF,
        name="raw",
    )(*lines, gate_w, up_w)


def hidden_kernel(parts, rows, count, exp_dev, pair, place_ref, *refs):
    lines, inner, rest = refs[:count], refs[count : count + parts], refs[count + parts :]
    gate_ref, up_ref, diag_ref, hidden_ref = rest[:4]
    outs = rest[4:]
    hid = gate_ref.shape[1]
    ranks = diag_ref.shape[1]
    wide = lines[0].shape[1] - pair
    total = sum(ref[...].astype(F32) for ref in inner).astype(BF)
    gate = gate_ref[...] + dot_nn(total[:, :ranks], diag_ref[0])
    up = up_ref[...] + dot_nn(total[:, ranks:], diag_ref[1])
    lane = lax.broadcasted_iota(jnp.int32, (pair, hid), 0)
    lane = jnp.where(lane < pair // 2, lane, lane - pair // 2)
    owner = lax.broadcasted_iota(jnp.int32, (pair, hid), 1) // (hid // exp_dev)
    pick = (lane == owner + place_ref[0]).astype(F32).astype(BF)
    scale = dot_nn(jnp.concatenate([line[:, wide:] for line in lines]), pick)
    hidden = (gate / (1.0 + jnp.exp(-gate)) * up * scale).astype(BF)
    hidden_ref[...] = hidden
    value = dot_nt(hidden, diag_ref[2])
    for k in range(parts):
        outs[k][...] = rotated(value, rows, parts, k).astype(BF)


def hidden_units(place, lines, inner, raw, diag, parts, rows, exp_dev, pair):
    total, hid = raw[0].shape
    ranks = diag.shape[1]
    vmem = pl.BlockSpec(memory_space=pltpu.VMEM)
    return pl.pallas_call(
        functools.partial(hidden_kernel, parts, rows, len(lines), exp_dev, pair),
        in_specs=[pl.BlockSpec(memory_space=pltpu.SMEM)]
        + [vmem] * (len(lines) + len(inner) + 3),
        out_shape=[jax.ShapeDtypeStruct((total, hid), BF)]
        + [jax.ShapeDtypeStruct((total, ranks), BF)] * parts,
        compiler_params=pltpu.CompilerParams(vmem_limit_bytes=VMEM_LIMIT),
        cost_estimate=BRIEF,
        name="hidden",
    )(place, *lines, *inner, *raw, diag)


def down_kernel(hidden_ref, down_ref, near_ref, far_ref):
    near, width = near_ref.shape
    hidden = hidden_ref[...]
    tile = min(1024, width)
    for i in range(width // tile):
        span = slice(i * tile, (i + 1) * tile)
        value = dot_nn(hidden, down_ref[:, span])
        near_ref[:, span] = value[:near]
        far_ref[:, span] = value[near:].astype(BF)


def down_products(hidden, down_w):
    total, width = hidden.shape[0], down_w.shape[1]
    return pl.pallas_call(
        down_kernel,
        out_shape=[
            jax.ShapeDtypeStruct((total // 2, width), F32),
            jax.ShapeDtypeStruct((total // 2, width), BF),
        ],
        compiler_params=pltpu.CompilerParams(vmem_limit_bytes=VMEM_LIMIT),
        cost_estimate=BRIEF,
        name="down",
    )(hidden, down_w)


def extra_kernel(right_ref, *refs):
    bottom, (near_ref, far_ref) = refs[:-2], refs[-2:]
    near = near_ref.shape[0]
    low = sum(ref[...].astype(F32) for ref in bottom).astype(BF)
    value = dot_nn(low, right_ref[...])
    near_ref[...] = value[:near]
    far_ref[...] = value[near:].astype(BF)


def extra_products(right, bottom):
    total = bottom[0].shape[0]
    block = right.shape[1]
    return pl.pallas_call(
        extra_kernel,
        out_shape=[
            jax.ShapeDtypeStruct((total // 2, block), F32),
            jax.ShapeDtypeStruct((total // 2, block), BF),
        ],
        compiler_params=pltpu.CompilerParams(vmem_limit_bytes=VMEM_LIMIT),
        cost_estimate=BRIEF,
        name="extra",
    )(right, *bottom)


def fold_kernel(head, near_ref, far_ref, own_ref, *out_refs):
    span = own_ref.shape[0]
    total = near_ref[...] + far_ref[...].astype(F32)
    own_ref[...] = total[:span]
    per = 2 if head else 1
    for n in range(len(out_refs) // per):
        line = total[(n + 1) * span : (n + 2) * span]
        if head:
            out_refs[2 * n][...] = line[:head].astype(BF)
            out_refs[2 * n + 1][...] = line[head:].astype(BF)
        else:
            out_refs[n][...] = line.astype(BF)


def fold(near, far, chips, head):
    total, width = near.shape
    span = total // chips
    cuts = [head, span - head] if head else [span]
    return pl.pallas_call(
        functools.partial(fold_kernel, head),
        out_shape=[jax.ShapeDtypeStruct((span, width), F32)]
        + [jax.ShapeDtypeStruct((rows, width), BF) for rows in cuts] * (chips - 1),
        compiler_params=pltpu.CompilerParams(vmem_limit_bytes=VMEM_LIMIT),
        cost_estimate=BRIEF,
        name="fold",
    )(near, far)


def merge_kernel(count, own_ref, low_ref, *refs):
    backs, lows, outs = refs[:count], refs[count : 2 * count], refs[2 * count :]
    rows = outs[0].shape[0]
    block = low_ref.shape[1]
    offset = pl.multiple_of(lax.axis_index("mp") * block, 128)
    low = low_ref[...]
    for ref in lows:
        low += ref[...].astype(F32)
    total = own_ref[rows:]
    part = own_ref[:, pl.ds(offset, block)] + low
    after_own = part[rows:]
    for ref in backs:
        total += ref[...].astype(F32)
        after_own += ref[:, pl.ds(offset, block)].astype(F32)
    outs[0][...] = own_ref[:rows]
    outs[0][:, pl.ds(offset, block)] = part[:rows]
    for k in range(1, len(outs)):
        span = slice((k - 1) * rows, k * rows)
        outs[k][...] = total[span].astype(BF)
        outs[k][:, pl.ds(offset, block)] = after_own[span].astype(BF)


def merge(own, low, backs, lows, rows):
    total, width = own.shape
    return pl.pallas_call(
        functools.partial(merge_kernel, len(backs)),
        out_shape=[jax.ShapeDtypeStruct((rows, width), F32)]
        + [jax.ShapeDtypeStruct((rows, width), BF)] * (total // rows - 1),
        compiler_params=pltpu.CompilerParams(vmem_limit_bytes=VMEM_LIMIT),
        cost_estimate=BRIEF,
        name="merge",
    )(own, low, *backs, *lows)


def local(
    tokens,
    routes,
    probs,
    w_gate,
    w_up,
    w_down,
    gate_left,
    gate_right,
    up_left,
    up_right,
    down_left,
    down_right,
):
    rows, width = tokens.shape
    exp_dev, _, cols = w_gate.shape
    rank = gate_left.shape[1]
    block = gate_left.shape[2]
    parts = lax.axis_size("mp")
    chips = lax.axis_size("y")
    experts = exp_dev * chips * 2
    me_g = lax.axis_index("y") * 2 + lax.axis_index("core")
    ranks = exp_dev * rank
    hid = exp_dev * cols

    def along_z(value, step):
        return lax.ppermute(value, "mp", [(i, (i + step) % parts) for i in range(parts)])

    def along_y(value, step):
        return lax.ppermute(value, "y", [(i, (i + step) % chips) for i in range(chips)])

    def other_core(value):
        return lax.ppermute(value, "core", [(0, 1), (1, 0)])

    pair = 2 * (-(-experts // 64) * 64)
    sent = attach(tokens, routes, probs, pair)
    arrived = [along_z(sent, k) for k in range(1, parts)]
    first = [along_y(sent, s) for s in range(1, chips)]
    gate_w = jnp.swapaxes(w_gate, 1, 2).reshape(hid, width)
    up_w = jnp.swapaxes(w_up, 1, 2).reshape(hid, width)
    gate_w, up_w, gate_left, up_left = load(
        *after((gate_w, up_w, gate_left, up_left), first)
    )
    small = cut((gate_right, up_right, down_left), parts)
    rest = after(jnp.concatenate(arrived), (gate_w, up_w, small))
    lines = [jnp.concatenate([sent, rest])]
    partner = [other_core(lines[0])]
    down_w, right = load(*after((w_down.reshape(hid, width), down_right), rest))
    small = after(tuple(small), rest)
    small = [small[0]] + [along_z(small[k], k) for k in range(1, parts)]
    for s in range(1, chips):
        line = jnp.concatenate([first[s - 1], along_y(rest, s)])
        line = after(line, (down_w, tuple(small)))
        lines.append(line)
        partner.append(other_core(line))
    lines += partner
    diag = spread(small, parts, exp_dev)

    inner = inner_products(lines, gate_left, up_left, parts, rows)
    inner = [inner[0]] + [along_z(inner[k], k) for k in range(1, parts)]
    raw = raw_products(lines, gate_w, up_w)
    first_expert = (me_g * exp_dev)[None]
    hidden, *bottom = hidden_units(
        first_expert, lines, inner, raw, diag, parts, rows, exp_dev, pair
    )
    bottom = [bottom[0]] + [along_z(bottom[k], k) for k in range(1, parts)]

    near, far = down_products(hidden, down_w)
    out, *others = fold(near, other_core(far), chips, rows)
    backs = [along_y(others[2 * s - 1], -s) for s in range(1, chips)]

    bottom = after(tuple(bottom), out)
    near, far = extra_products(right.reshape(ranks, block), bottom)
    low, *lows = fold(near, other_core(far), chips, 0)
    lows = [along_y(lows[s - 1], -s) for s in range(1, chips)]

    heads = [along_y(after(others[2 * s - 2], backs[s - 1]), -s) for s in range(1, chips)]
    result, *pieces = merge(out, low, backs, lows, rows)
    for piece in heads:
        result += piece.astype(F32)
    for k in range(1, parts):
        result += along_z(pieces[k - 1], -k).astype(F32)
    return result.astype(BF)


def solution(mesh):
    count = mesh.shape
    fine = jax.sharding.Mesh(
        mesh.devices.reshape(count["groups"], count["expert"] // 2, 2, count["mp"]),
        ("groups", "y", "core", "mp"),
    )
    expert = ("y", "core")
    return jax.shard_map(
        local,
        mesh=fine,
        in_specs=(
            P(("groups", "y", "core", "mp"), None),
            P(("groups", "y", "core", "mp"), None),
            P(("groups", "y", "core", "mp"), None),
            P(expert, None, "mp"),
            P(expert, None, "mp"),
            P(expert, "mp", None),
            P(expert, None, "mp"),
            P(expert, "mp", None),
            P(expert, None, "mp"),
            P(expert, "mp", None),
            P(expert, "mp", None),
            P(expert, None, "mp"),
        ),
        out_specs=P(("groups", "y", "core", "mp"), None),
        check_vma=False,
    )
```

```python
import functools

import jax
import jax.numpy as jnp
from jax import lax
from jax.experimental import pallas as pl
from jax.experimental.pallas import tpu as pltpu
from jax.sharding import PartitionSpec as P

BF = jnp.bfloat16
F32 = jnp.float32
VMEM_LIMIT = 16 * 1024 * 1024
STREAM_LIMIT = 24 * 1024 * 1024
BRIEF = pl.CostEstimate(flops=1, bytes_accessed=1, transcendentals=0)


def dot_nt(a, b):
    return lax.dot_general(a, b, (((1,), (1,)), ((), ())), preferred_element_type=F32)


def dot_nn(a, b):
    return lax.dot_general(a, b, (((1,), (0,)), ((), ())), preferred_element_type=F32)


def in_hbm(*values):
    return [pltpu.with_memory_space_constraint(v, pltpu.HBM) for v in values]


def after(value, earlier):
    return lax.optimization_barrier((value, earlier))[0]


def rotated(value, rows, parts, step):
    if step == 0:
        return value
    span = rows * parts
    lines = []
    for start in range(0, value.shape[0], span):
        cut = start + span - step * rows
        lines += [value[cut : start + span], value[start:cut]]
    return jnp.concatenate(lines)


def attach_kernel(tokens_ref, routes_ref, probs_ref, out_ref):
    rows, width = tokens_ref.shape
    pair = out_ref.shape[1] - width
    out_ref[:, :width] = tokens_ref[...]
    routes = routes_ref[...]
    probs = probs_ref[...]
    lane = lax.broadcasted_iota(jnp.int32, (rows, pair), 1)
    ids = jnp.where(lane < pair // 2, lane, lane - pair // 2)
    weight = jnp.zeros((rows, pair), F32)
    for k in range(routes.shape[1]):
        weight += jnp.where(ids == routes[:, k : k + 1], probs[:, k : k + 1], 0.0)
    high = weight.astype(BF).astype(F32)
    out_ref[:, width:] = jnp.where(lane < pair // 2, high, weight - high).astype(BF)


def attach(tokens, routes, probs, pair):
    rows, width = tokens.shape
    return pl.pallas_call(
        attach_kernel,
        out_shape=jax.ShapeDtypeStruct((rows, width + pair), BF),
        cost_estimate=BRIEF,
        name="attach",
    )(*in_hbm(tokens, routes, probs))


def cut_kernel(parts, *refs):
    ins, lefts, left_ref, outs = refs[:3], refs[3:5], refs[5], refs[6:]
    exp_dev, piece, hid = ins[0].shape
    half = left_ref.shape[0] // 2
    for n, ref in enumerate(lefts):
        left_ref[n * half : (n + 1) * half] = ref[...].reshape(half, left_ref.shape[1])
    cols = hid // parts
    me = lax.axis_index("mp")
    for n, ref in enumerate(ins):
        value = ref[...].reshape(exp_dev * piece, hid).astype(F32)
        blocks = [value[:, j * cols : (j + 1) * cols] for j in range(parts)]
        for k in range(parts):
            target = lax.rem(me + k, parts)
            block = blocks[0]
            for j in range(1, parts):
                block = jnp.where(target == j, blocks[j], block)
            outs[k][n] = block.astype(BF)


def cut(factors, lefts, parts):
    exp_dev, piece, hid = factors[0].shape
    _, rank, block = lefts[0].shape
    return pl.pallas_call(
        functools.partial(cut_kernel, parts),
        out_shape=[jax.ShapeDtypeStruct((2 * exp_dev * rank, block), BF)]
        + [jax.ShapeDtypeStruct((3, exp_dev * piece, hid // parts), BF)] * parts,
        cost_estimate=BRIEF,
        name="cut",
    )(*in_hbm(*factors, *lefts))


def spread_kernel(parts, exp_dev, *refs):
    pieces, out_ref = refs[:-1], refs[-1]
    _, ranks, hid = out_ref.shape
    rank = ranks // exp_dev
    piece = rank // parts
    me = lax.axis_index("mp")
    row = lax.broadcasted_iota(jnp.int32, (ranks, ranks), 0)
    col = lax.broadcasted_iota(jnp.int32, (ranks, ranks), 1)
    step = lax.rem(me - row % rank // piece + parts, parts)
    source = (step * exp_dev + row // rank) * piece + row % piece
    order = (col == source).astype(F32).astype(BF)
    cols = hid // exp_dev
    place = lax.broadcasted_iota(jnp.int32, (ranks, hid), 1)
    place -= lax.broadcasted_iota(jnp.int32, (ranks, hid), 0) // rank * cols
    own = (place >= 0) & (place < cols)
    for n in range(3):
        value = dot_nn(order, jnp.concatenate([p[n].astype(F32) for p in pieces]).astype(BF))
        value = jnp.concatenate([value] * exp_dev, axis=1)
        out_ref[n] = jnp.where(own, value, 0.0).astype(BF)


def spread(pieces, parts, exp_dev):
    _, span, cols = pieces[0].shape
    return pl.pallas_call(
        functools.partial(spread_kernel, parts, exp_dev),
        out_shape=jax.ShapeDtypeStruct((3, span * parts, cols * exp_dev), BF),
        cost_estimate=BRIEF,
        name="spread",
    )(*pieces)


def inner_kernel(parts, rows, count, *refs):
    lines, left_ref, outs = refs[:count], refs[count], refs[count + 1 :]
    block = left_ref.shape[1]
    offset = pl.multiple_of(lax.axis_index("mp") * block, 128)
    x = jnp.concatenate([line[:, pl.ds(offset, block)] for line in lines])
    value = dot_nt(x, left_ref[...])
    for k in range(parts):
        outs[k][...] = rotated(value, rows, parts, k).astype(BF)


def inner_products(lines, left, parts, rows):
    total = sum(line.shape[0] for line in lines)
    ranks = left.shape[0]
    return pl.pallas_call(
        functools.partial(inner_kernel, parts, rows, len(lines)),
        out_shape=[jax.ShapeDtypeStruct((total, ranks), BF)] * parts,
        compiler_params=pltpu.CompilerParams(vmem_limit_bytes=VMEM_LIMIT),
        cost_estimate=BRIEF,
        name="inner",
    )(*lines, left)


def raw_kernel(count, tiles, *refs):
    lines, weights, outs = refs[:count], refs[count : count + 2], refs[count + 2 : count + 4]
    scratch, sems = refs[count + 4 : count + 6], refs[count + 6]
    hid, width = weights[0].shape
    tile = hid // tiles
    copies = []
    for i in range(tiles):
        for n in range(2):
            span = pl.ds(i * tile, tile)
            copy = pltpu.make_async_copy(
                weights[n].at[span], scratch[n].at[span], sems.at[2 * i + n]
            )
            copy.start()
            copies.append(copy)
    x = jnp.concatenate([line[:, :width] for line in lines])
    for i in range(tiles):
        span = slice(i * tile, (i + 1) * tile)
        for n in range(2):
            copies[2 * i + n].wait()
            outs[n][:, span] = dot_nt(x, scratch[n][span])


def raw_products(lines, gate_w, up_w):
    hid = gate_w.shape[0]
    total = sum(line.shape[0] for line in lines)
    tiles = hid // 128
    vmem = pl.BlockSpec(memory_space=pltpu.VMEM)
    return pl.pallas_call(
        functools.partial(raw_kernel, len(lines), tiles),
        in_specs=[vmem] * len(lines) + [pl.BlockSpec(memory_space=pltpu.HBM)] * 2,
        out_specs=[vmem] * 2,
        out_shape=[jax.ShapeDtypeStruct((total, hid), F32)] * 2,
        scratch_shapes=[pltpu.VMEM(gate_w.shape, BF)] * 2
        + [pltpu.SemaphoreType.DMA((2 * tiles,))],
        compiler_params=pltpu.CompilerParams(vmem_limit_bytes=STREAM_LIMIT),
        cost_estimate=BRIEF,
        name="raw",
    )(*lines, *in_hbm(gate_w, up_w))


def hidden_kernel(parts, count, exp_dev, pair, place_ref, *refs):
    lines, inner, rest = refs[:count], refs[count : count + parts], refs[count + parts :]
    gate_ref, up_ref, diag_ref, hidden_ref, near_ref, far_ref = rest
    hid = gate_ref.shape[1]
    ranks = diag_ref.shape[1]
    wide = lines[0].shape[1] - pair
    total = sum(ref[...].astype(F32) for ref in inner).astype(BF)
    gate = gate_ref[...] + dot_nn(total[:, :ranks], diag_ref[0])
    up = up_ref[...] + dot_nn(total[:, ranks:], diag_ref[1])
    lane = lax.broadcasted_iota(jnp.int32, (pair, hid), 0)
    lane = jnp.where(lane < pair // 2, lane, lane - pair // 2)
    cols = hid // exp_dev
    place = lax.broadcasted_iota(jnp.int32, (pair, hid), 1) - (lane - place_ref[0]) * cols
    pick = ((place >= 0) & (place < cols)).astype(F32).astype(BF)
    scale = dot_nn(jnp.concatenate([line[:, wide:] for line in lines]), pick)
    hidden = (gate / (1.0 + jnp.exp(-gate)) * up * scale).astype(BF)
    hidden_ref[...] = hidden
    value = dot_nt(hidden, diag_ref[2])
    near = near_ref.shape[0]
    near_ref[...] = value[:near].astype(BF)
    far_ref[...] = value[near:].astype(BF)


def hidden_units(place, lines, inner, raw, diag, parts, exp_dev, pair):
    total, hid = raw[0].shape
    ranks = diag.shape[1]
    vmem = pl.BlockSpec(memory_space=pltpu.VMEM)
    return pl.pallas_call(
        functools.partial(hidden_kernel, parts, len(lines), exp_dev, pair),
        in_specs=[pl.BlockSpec(memory_space=pltpu.SMEM)]
        + [vmem] * (len(lines) + len(inner) + 3),
        out_shape=[jax.ShapeDtypeStruct((total, hid), BF)]
        + [jax.ShapeDtypeStruct((total // 2, ranks), BF)] * 2,
        compiler_params=pltpu.CompilerParams(vmem_limit_bytes=VMEM_LIMIT),
        cost_estimate=BRIEF,
        name="hidden",
    )(place, *lines, *inner, *raw, diag)


def down_kernel(hidden_ref, down_ref, near_ref, far_ref):
    near, width = near_ref.shape
    hidden = hidden_ref[...]
    tile = min(1024, width)
    for i in range(width // tile):
        span = slice(i * tile, (i + 1) * tile)
        value = dot_nn(hidden, down_ref[:, span])
        near_ref[:, span] = value[:near]
        far_ref[:, span] = value[near:].astype(BF)


def down_products(hidden, down_w):
    total, width = hidden.shape[0], down_w.shape[1]
    return pl.pallas_call(
        down_kernel,
        out_shape=[
            jax.ShapeDtypeStruct((total // 2, width), F32),
            jax.ShapeDtypeStruct((total // 2, width), BF),
        ],
        compiler_params=pltpu.CompilerParams(vmem_limit_bytes=VMEM_LIMIT),
        cost_estimate=BRIEF,
        name="down",
    )(hidden, down_w)


def turn_kernel(rows, near_ref, far_ref, *out_refs):
    value = jnp.concatenate([near_ref[...].astype(F32), far_ref[...].astype(F32)], axis=1)
    for k, out_ref in enumerate(out_refs):
        out_ref[...] = rotated(value, rows, len(out_refs), k).astype(BF)


def turn(near, far, parts, rows):
    total, ranks = near.shape
    return pl.pallas_call(
        functools.partial(turn_kernel, rows),
        out_shape=[jax.ShapeDtypeStruct((total, 2 * ranks), BF)] * parts,
        cost_estimate=BRIEF,
        name="turn",
    )(near, far)


def extra_kernel(chips, near_ref, far_ref, *refs):
    bottom, own_ref, outs = refs[: -chips], refs[-chips], refs[len(refs) - chips + 1 :]
    ranks, span = near_ref.shape[0], own_ref.shape[0]
    low = sum(ref[...].astype(F32) for ref in bottom).astype(BF)
    value = dot_nn(low[:, :ranks], near_ref[...]) + dot_nn(low[:, ranks:], far_ref[...])
    own_ref[...] = value[:span]
    for n, out_ref in enumerate(outs):
        out_ref[...] = value[(n + 1) * span : (n + 2) * span].astype(BF)


def extra_products(near, far, bottom, chips):
    span = bottom[0].shape[0] // chips
    block = near.shape[1]
    return pl.pallas_call(
        functools.partial(extra_kernel, chips),
        out_shape=[jax.ShapeDtypeStruct((span, block), F32)]
        + [jax.ShapeDtypeStruct((span, block), BF)] * (chips - 1),
        compiler_params=pltpu.CompilerParams(vmem_limit_bytes=VMEM_LIMIT),
        cost_estimate=BRIEF,
        name="extra",
    )(near, far, *bottom)


def fold_kernel(head, near_ref, far_ref, own_ref, *out_refs):
    span = own_ref.shape[0]
    total = near_ref[...] + far_ref[...].astype(F32)
    own_ref[...] = total[:span]
    for n in range(len(out_refs) // 2):
        line = total[(n + 1) * span : (n + 2) * span]
        out_refs[2 * n][...] = line[:head].astype(BF)
        out_refs[2 * n + 1][...] = line[head:].astype(BF)


def fold(near, far, chips, head):
    total, width = near.shape
    span = total // chips
    cuts = [head, span - head]
    return pl.pallas_call(
        functools.partial(fold_kernel, head),
        out_shape=[jax.ShapeDtypeStruct((span, width), F32)]
        + [jax.ShapeDtypeStruct((rows, width), BF) for rows in cuts] * (chips - 1),
        compiler_params=pltpu.CompilerParams(vmem_limit_bytes=VMEM_LIMIT),
        cost_estimate=BRIEF,
        name="fold",
    )(near, far)


def merge_kernel(count, own_ref, low_ref, *refs):
    backs, lows, outs = refs[:count], refs[count : 2 * count], refs[2 * count :]
    rows = outs[0].shape[0]
    block = low_ref.shape[1]
    offset = pl.multiple_of(lax.axis_index("mp") * block, 128)
    low = low_ref[...]
    for ref in lows:
        low += ref[...].astype(F32)
    total = own_ref[rows:]
    part = own_ref[:, pl.ds(offset, block)] + low
    after_own = part[rows:]
    for ref in backs:
        total += ref[...].astype(F32)
        after_own += ref[:, pl.ds(offset, block)].astype(F32)
    outs[0][...] = own_ref[:rows]
    outs[0][:, pl.ds(offset, block)] = part[:rows]
    for k in range(1, len(outs)):
        span = slice((k - 1) * rows, k * rows)
        outs[k][...] = total[span].astype(BF)
        outs[k][:, pl.ds(offset, block)] = after_own[span].astype(BF)


def merge(own, low, backs, lows, rows):
    total, width = own.shape
    return pl.pallas_call(
        functools.partial(merge_kernel, len(backs)),
        out_shape=[jax.ShapeDtypeStruct((rows, width), F32)]
        + [jax.ShapeDtypeStruct((rows, width), BF)] * (total // rows - 1),
        compiler_params=pltpu.CompilerParams(vmem_limit_bytes=VMEM_LIMIT),
        cost_estimate=BRIEF,
        name="merge",
    )(own, low, *backs, *lows)


def local(
    tokens,
    routes,
    probs,
    w_gate,
    w_up,
    w_down,
    gate_left,
    gate_right,
    up_left,
    up_right,
    down_left,
    down_right,
):
    rows, width = tokens.shape
    exp_dev, _, cols = w_gate.shape
    rank = gate_left.shape[1]
    block = gate_left.shape[2]
    parts = lax.axis_size("mp")
    chips = lax.axis_size("y")
    experts = exp_dev * chips * 2
    me_g = lax.axis_index("y") * 2 + lax.axis_index("core")
    ranks = exp_dev * rank
    hid = exp_dev * cols

    def along_z(value, step):
        return lax.ppermute(value, "mp", [(i, (i + step) % parts) for i in range(parts)])

    def along_y(value, step):
        return lax.ppermute(value, "y", [(i, (i + step) % chips) for i in range(chips)])

    def other_core(value):
        return lax.ppermute(value, "core", [(0, 1), (1, 0)])

    pair = 2 * (-(-experts // 64) * 64)
    sent = attach(tokens, routes, probs, pair)
    arrived = [along_z(sent, k) for k in range(1, parts)]
    first = [along_y(sent, s) for s in range(1, chips)]
    left, *small = cut((gate_right, up_right, down_left), (gate_left, up_left), parts)
    rest = after(jnp.concatenate(arrived), (left, small))
    lines = [jnp.concatenate([sent, rest])]
    partner = [other_core(lines[0])]
    small = after(tuple(small), rest)
    small = [small[0]] + [along_z(small[k], k) for k in range(1, parts)]
    right = after(down_right.reshape(ranks, block), rest)
    partner_right = other_core(right)
    for s in range(1, chips):
        line = jnp.concatenate([first[s - 1], along_y(rest, s)])
        line = after(line, (tuple(small), partner_right))
        lines.append(line)
        partner.append(other_core(line))
    lines += partner
    diag = spread(small, parts, exp_dev)

    inner = inner_products(lines, left, parts, rows)
    inner = [inner[0]] + [along_z(inner[k], k) for k in range(1, parts)]
    gate_w = jnp.swapaxes(w_gate, 1, 2).reshape(hid, width)
    up_w = jnp.swapaxes(w_up, 1, 2).reshape(hid, width)
    raw = raw_products(lines, gate_w, up_w)
    first_expert = (me_g * exp_dev)[None]
    hidden, near, far = hidden_units(
        first_expert, lines, inner, raw, diag, parts, exp_dev, pair
    )
    swapped = other_core(far)
    bottom = turn(near, swapped, parts, rows)
    bottom = [bottom[0]] + [along_z(bottom[k], k) for k in range(1, parts)]

    near, far = down_products(hidden, w_down.reshape(hid, width))
    out, *others = fold(near, other_core(after(far, swapped)), chips, rows)
    backs = [along_y(others[2 * s - 1], -s) for s in range(1, chips)]

    low, *lows = extra_products(right, partner_right, bottom, chips)
    lows = [along_y(lows[s - 1], -s) for s in range(1, chips)]

    heads = [along_y(after(others[2 * s - 2], backs[s - 1]), -s) for s in range(1, chips)]
    result, *pieces = merge(out, low, backs, lows, rows)
    for piece in heads:
        result += piece.astype(F32)
    for k in range(1, parts):
        result += along_z(pieces[k - 1], -k).astype(F32)
    return result.astype(BF)


def solution(mesh):
    count = mesh.shape
    fine = jax.sharding.Mesh(
        mesh.devices.reshape(count["groups"], count["expert"] // 2, 2, count["mp"]),
        ("groups", "y", "core", "mp"),
    )
    expert = ("y", "core")
    return jax.shard_map(
        local,
        mesh=fine,
        in_specs=(
            P(("groups", "y", "core", "mp"), None),
            P(("groups", "y", "core", "mp"), None),
            P(("groups", "y", "core", "mp"), None),
            P(expert, None, "mp"),
            P(expert, None, "mp"),
            P(expert, "mp", None),
            P(expert, None, "mp"),
            P(expert, "mp", None),
            P(expert, None, "mp"),
            P(expert, "mp", None),
            P(expert, "mp", None),
            P(expert, None, "mp"),
        ),
        out_specs=P(("groups", "y", "core", "mp"), None),
        check_vma=False,
    )
```

```python
import functools

import jax
import jax.numpy as jnp
from jax import lax
from jax.experimental import pallas as pl
from jax.experimental.pallas import tpu as pltpu
from jax.sharding import PartitionSpec as P

BF = jnp.bfloat16
F32 = jnp.float32
SMALL_LIMIT = 4 * 1024 * 1024
VMEM_LIMIT = 12 * 1024 * 1024
STREAM_LIMIT = 16 * 1024 * 1024
PIECES = 4
BRIEF = pl.CostEstimate(flops=1, bytes_accessed=1, transcendentals=0)


def dot_nt(a, b):
    return lax.dot_general(a, b, (((1,), (1,)), ((), ())), preferred_element_type=F32)


def dot_nn(a, b):
    return lax.dot_general(a, b, (((1,), (0,)), ((), ())), preferred_element_type=F32)


def in_hbm(*values):
    return [pltpu.with_memory_space_constraint(v, pltpu.HBM) for v in values]


def after(value, earlier):
    return lax.optimization_barrier((value, earlier))[0]


def rotated(value, rows, parts, step):
    if step == 0:
        return value
    span = rows * parts
    lines = []
    for start in range(0, value.shape[0], span):
        cut = start + span - step * rows
        lines += [value[cut : start + span], value[start:cut]]
    return jnp.concatenate(lines)


def attach_kernel(tokens_ref, routes_ref, probs_ref, out_ref):
    rows, width = tokens_ref.shape
    pair = out_ref.shape[1] - width
    out_ref[:, :width] = tokens_ref[...]
    routes = routes_ref[...]
    probs = probs_ref[...]
    lane = lax.broadcasted_iota(jnp.int32, (rows, pair), 1)
    ids = jnp.where(lane < pair // 2, lane, lane - pair // 2)
    weight = jnp.zeros((rows, pair), F32)
    for k in range(routes.shape[1]):
        weight += jnp.where(ids == routes[:, k : k + 1], probs[:, k : k + 1], 0.0)
    high = weight.astype(BF).astype(F32)
    out_ref[:, width:] = jnp.where(lane < pair // 2, high, weight - high).astype(BF)


def attach(tokens, routes, probs, pair):
    rows, width = tokens.shape
    return pl.pallas_call(
        attach_kernel,
        out_shape=jax.ShapeDtypeStruct((rows, width + pair), BF),
        compiler_params=pltpu.CompilerParams(vmem_limit_bytes=SMALL_LIMIT),
        cost_estimate=BRIEF,
        name="attach",
    )(*in_hbm(tokens, routes, probs))


def cut_kernel(parts, *refs):
    ins, lefts, left_ref, outs = refs[:3], refs[3:5], refs[5], refs[6:]
    exp_dev, piece, hid = ins[0].shape
    half = left_ref.shape[0] // 2
    for n, ref in enumerate(lefts):
        left_ref[n * half : (n + 1) * half] = ref[...].reshape(half, left_ref.shape[1])
    cols = hid // parts
    me = lax.axis_index("mp")
    for n, ref in enumerate(ins):
        value = ref[...].reshape(exp_dev * piece, hid).astype(F32)
        blocks = [value[:, j * cols : (j + 1) * cols] for j in range(parts)]
        for k in range(parts):
            target = lax.rem(me + k, parts)
            block = blocks[0]
            for j in range(1, parts):
                block = jnp.where(target == j, blocks[j], block)
            outs[k][n] = block.astype(BF)


def cut(factors, lefts, parts):
    exp_dev, piece, hid = factors[0].shape
    _, rank, block = lefts[0].shape
    return pl.pallas_call(
        functools.partial(cut_kernel, parts),
        out_shape=[jax.ShapeDtypeStruct((2 * exp_dev * rank, block), BF)]
        + [jax.ShapeDtypeStruct((3, exp_dev * piece, hid // parts), BF)] * parts,
        compiler_params=pltpu.CompilerParams(vmem_limit_bytes=SMALL_LIMIT),
        cost_estimate=BRIEF,
        name="cut",
    )(*in_hbm(*factors, *lefts))


def spread_kernel(parts, exp_dev, *refs):
    pieces, out_ref = refs[:-1], refs[-1]
    _, ranks, hid = out_ref.shape
    rank = ranks // exp_dev
    piece = rank // parts
    me = lax.axis_index("mp")
    row = lax.broadcasted_iota(jnp.int32, (ranks, ranks), 0)
    col = lax.broadcasted_iota(jnp.int32, (ranks, ranks), 1)
    step = lax.rem(me - row % rank // piece + parts, parts)
    source = (step * exp_dev + row // rank) * piece + row % piece
    order = (col == source).astype(F32).astype(BF)
    cols = hid // exp_dev
    place = lax.broadcasted_iota(jnp.int32, (ranks, hid), 1)
    place -= lax.broadcasted_iota(jnp.int32, (ranks, hid), 0) // rank * cols
    own = (place >= 0) & (place < cols)
    for n in range(3):
        value = dot_nn(order, jnp.concatenate([p[n].astype(F32) for p in pieces]).astype(BF))
        value = jnp.concatenate([value] * exp_dev, axis=1)
        out_ref[n] = jnp.where(own, value, 0.0).astype(BF)


def spread(pieces, parts, exp_dev):
    _, span, cols = pieces[0].shape
    return pl.pallas_call(
        functools.partial(spread_kernel, parts, exp_dev),
        out_shape=jax.ShapeDtypeStruct((3, span * parts, cols * exp_dev), BF),
        compiler_params=pltpu.CompilerParams(vmem_limit_bytes=SMALL_LIMIT),
        cost_estimate=BRIEF,
        name="spread",
    )(*pieces)


def inner_kernel(parts, rows, count, *refs):
    lines, left_ref, outs = refs[:count], refs[count], refs[count + 1 :]
    block = left_ref.shape[1]
    offset = pl.multiple_of(lax.axis_index("mp") * block, 128)
    x = jnp.concatenate([line[:, pl.ds(offset, block)] for line in lines])
    value = dot_nt(x, left_ref[...])
    for k in range(parts):
        outs[k][...] = rotated(value, rows, parts, k).astype(BF)


def inner_products(lines, left, parts, rows):
    total = sum(line.shape[0] for line in lines)
    ranks = left.shape[0]
    return pl.pallas_call(
        functools.partial(inner_kernel, parts, rows, len(lines)),
        out_shape=[jax.ShapeDtypeStruct((total, ranks), BF)] * parts,
        compiler_params=pltpu.CompilerParams(vmem_limit_bytes=VMEM_LIMIT),
        cost_estimate=BRIEF,
        name="inner",
    )(*lines, left)


def load_kernel(source, target, sems):
    step = source.shape[0] // PIECES
    copies = []
    for i in range(PIECES):
        span = pl.ds(i * step, step)
        copies.append(pltpu.make_async_copy(source.at[span], target.at[span], sems.at[i]))
    for copy in copies:
        copy.start()
    for copy in copies:
        copy.wait()


def load(weights):
    return pl.pallas_call(
        load_kernel,
        in_specs=[pl.BlockSpec(memory_space=pltpu.HBM)],
        out_specs=pl.BlockSpec(memory_space=pltpu.VMEM),
        out_shape=pltpu.VMEM(weights.shape, weights.dtype),
        scratch_shapes=[pltpu.SemaphoreType.DMA((PIECES,))],
        compiler_params=pltpu.CompilerParams(vmem_limit_bytes=SMALL_LIMIT),
        cost_estimate=BRIEF,
        name="load",
    )(*in_hbm(weights))


def raw_kernel(count, tile, *refs):
    lines, (gate_w, up_w, gate_ref, up_ref, scratch, sems) = refs[:count], refs[count:]
    hid, width = gate_w.shape
    spans = [pl.ds(i * tile, tile) for i in range(hid // tile)]
    copies = [
        pltpu.make_async_copy(up_w.at[span], scratch.at[span], sems.at[i])
        for i, span in enumerate(spans)
    ]
    for copy in copies:
        copy.start()
    x = jnp.concatenate([line[:, :width] for line in lines])
    for span in spans:
        gate_ref[:, span] = dot_nt(x, gate_w[span])
    for span, copy in zip(spans, copies):
        copy.wait()
        up_ref[:, span] = dot_nt(x, scratch[span])


def raw_products(lines, gate_w, up_w):
    hid = gate_w.shape[0]
    total = sum(line.shape[0] for line in lines)
    tile = 256 if hid % 256 == 0 else 128
    vmem = pl.BlockSpec(memory_space=pltpu.VMEM)
    return pl.pallas_call(
        functools.partial(raw_kernel, len(lines), tile),
        in_specs=[vmem] * (len(lines) + 1) + [pl.BlockSpec(memory_space=pltpu.HBM)],
        out_specs=[vmem] * 2,
        out_shape=[jax.ShapeDtypeStruct((total, hid), F32)] * 2,
        scratch_shapes=[pltpu.VMEM(up_w.shape, BF), pltpu.SemaphoreType.DMA((hid // tile,))],
        compiler_params=pltpu.CompilerParams(vmem_limit_bytes=STREAM_LIMIT),
        cost_estimate=BRIEF,
        name="raw",
    )(*lines, gate_w, *in_hbm(up_w))


def hidden_kernel(parts, count, exp_dev, pair, place_ref, *refs):
    lines, inner, rest = refs[:count], refs[count : count + parts], refs[count + parts :]
    gate_ref, up_ref, diag_ref, hidden_ref, near_ref, far_ref = rest
    hid = gate_ref.shape[1]
    ranks = diag_ref.shape[1]
    wide = lines[0].shape[1] - pair
    total = sum(ref[...].astype(F32) for ref in inner).astype(BF)
    gate = gate_ref[...] + dot_nn(total[:, :ranks], diag_ref[0])
    up = up_ref[...] + dot_nn(total[:, ranks:], diag_ref[1])
    lane = lax.broadcasted_iota(jnp.int32, (pair, hid), 0)
    lane = jnp.where(lane < pair // 2, lane, lane - pair // 2)
    cols = hid // exp_dev
    place = lax.broadcasted_iota(jnp.int32, (pair, hid), 1) - (lane - place_ref[0]) * cols
    pick = ((place >= 0) & (place < cols)).astype(F32).astype(BF)
    scale = dot_nn(jnp.concatenate([line[:, wide:] for line in lines]), pick)
    hidden = (gate / (1.0 + jnp.exp(-gate)) * up * scale).astype(BF)
    hidden_ref[...] = hidden
    value = dot_nt(hidden, diag_ref[2])
    near = near_ref.shape[0]
    near_ref[...] = value[:near].astype(BF)
    far_ref[...] = value[near:].astype(BF)


def hidden_units(place, lines, inner, raw, diag, parts, exp_dev, pair):
    total, hid = raw[0].shape
    ranks = diag.shape[1]
    vmem = pl.BlockSpec(memory_space=pltpu.VMEM)
    return pl.pallas_call(
        functools.partial(hidden_kernel, parts, len(lines), exp_dev, pair),
        in_specs=[pl.BlockSpec(memory_space=pltpu.SMEM)]
        + [vmem] * (len(lines) + len(inner) + 3),
        out_shape=[jax.ShapeDtypeStruct((total, hid), BF)]
        + [jax.ShapeDtypeStruct((total // 2, ranks), BF)] * 2,
        compiler_params=pltpu.CompilerParams(vmem_limit_bytes=VMEM_LIMIT),
        cost_estimate=BRIEF,
        name="hidden",
    )(place, *lines, *inner, *raw, diag)


def down_kernel(hidden_ref, down_ref, near_ref, far_ref):
    near, width = near_ref.shape
    hidden = hidden_ref[...]
    tile = min(1024, width)
    for i in range(width // tile):
        span = slice(i * tile, (i + 1) * tile)
        value = dot_nn(hidden, down_ref[:, span])
        near_ref[:, span] = value[:near]
        far_ref[:, span] = value[near:].astype(BF)


def down_products(hidden, down_w):
    total, width = hidden.shape[0], down_w.shape[1]
    return pl.pallas_call(
        down_kernel,
        out_shape=[
            jax.ShapeDtypeStruct((total // 2, width), F32),
            jax.ShapeDtypeStruct((total // 2, width), BF),
        ],
        compiler_params=pltpu.CompilerParams(vmem_limit_bytes=VMEM_LIMIT),
        cost_estimate=BRIEF,
        name="down",
    )(hidden, down_w)


def turn_kernel(rows, near_ref, far_ref, *out_refs):
    value = jnp.concatenate([near_ref[...].astype(F32), far_ref[...].astype(F32)], axis=1)
    for k, out_ref in enumerate(out_refs):
        out_ref[...] = rotated(value, rows, len(out_refs), k).astype(BF)


def turn(near, far, parts, rows):
    total, ranks = near.shape
    return pl.pallas_call(
        functools.partial(turn_kernel, rows),
        out_shape=[jax.ShapeDtypeStruct((total, 2 * ranks), BF)] * parts,
        compiler_params=pltpu.CompilerParams(vmem_limit_bytes=SMALL_LIMIT),
        cost_estimate=BRIEF,
        name="turn",
    )(near, far)


def extra_kernel(chips, near_ref, far_ref, *refs):
    bottom, own_ref, outs = refs[: -chips], refs[-chips], refs[len(refs) - chips + 1 :]
    ranks, span = near_ref.shape[0], own_ref.shape[0]
    low = sum(ref[...].astype(F32) for ref in bottom).astype(BF)
    value = dot_nn(low[:, :ranks], near_ref[...]) + dot_nn(low[:, ranks:], far_ref[...])
    own_ref[...] = value[:span]
    for n, out_ref in enumerate(outs):
        out_ref[...] = value[(n + 1) * span : (n + 2) * span].astype(BF)


def extra_products(near, far, bottom, chips):
    span = bottom[0].shape[0] // chips
    block = near.shape[1]
    return pl.pallas_call(
        functools.partial(extra_kernel, chips),
        out_shape=[jax.ShapeDtypeStruct((span, block), F32)]
        + [jax.ShapeDtypeStruct((span, block), BF)] * (chips - 1),
        compiler_params=pltpu.CompilerParams(vmem_limit_bytes=VMEM_LIMIT),
        cost_estimate=BRIEF,
        name="extra",
    )(near, far, *bottom)


def fold_kernel(head, near_ref, far_ref, own_ref, *out_refs):
    span = own_ref.shape[0]
    total = near_ref[...] + far_ref[...].astype(F32)
    own_ref[...] = total[:span]
    for n in range(len(out_refs) // 2):
        line = total[(n + 1) * span : (n + 2) * span]
        out_refs[2 * n][...] = line[:head].astype(BF)
        out_refs[2 * n + 1][...] = line[head:].astype(BF)


def fold(near, far, chips, head):
    total, width = near.shape
    span = total // chips
    cuts = [head, span - head]
    return pl.pallas_call(
        functools.partial(fold_kernel, head),
        out_shape=[jax.ShapeDtypeStruct((span, width), F32)]
        + [jax.ShapeDtypeStruct((rows, width), BF) for rows in cuts] * (chips - 1),
        compiler_params=pltpu.CompilerParams(vmem_limit_bytes=VMEM_LIMIT),
        cost_estimate=BRIEF,
        name="fold",
    )(near, far)


def merge_kernel(count, own_ref, low_ref, *refs):
    backs, lows, outs = refs[:count], refs[count : 2 * count], refs[2 * count :]
    rows = outs[0].shape[0]
    block = low_ref.shape[1]
    offset = pl.multiple_of(lax.axis_index("mp") * block, 128)
    low = low_ref[...]
    for ref in lows:
        low += ref[...].astype(F32)
    total = own_ref[rows:]
    part = own_ref[:, pl.ds(offset, block)] + low
    after_own = part[rows:]
    for ref in backs:
        total += ref[...].astype(F32)
        after_own += ref[:, pl.ds(offset, block)].astype(F32)
    outs[0][...] = own_ref[:rows]
    outs[0][:, pl.ds(offset, block)] = part[:rows]
    for k in range(1, len(outs)):
        span = slice((k - 1) * rows, k * rows)
        outs[k][...] = total[span].astype(BF)
        outs[k][:, pl.ds(offset, block)] = after_own[span].astype(BF)


def merge(own, low, backs, lows, rows):
    total, width = own.shape
    return pl.pallas_call(
        functools.partial(merge_kernel, len(backs)),
        out_shape=[jax.ShapeDtypeStruct((rows, width), F32)]
        + [jax.ShapeDtypeStruct((rows, width), BF)] * (total // rows - 1),
        compiler_params=pltpu.CompilerParams(vmem_limit_bytes=VMEM_LIMIT),
        cost_estimate=BRIEF,
        name="merge",
    )(own, low, *backs, *lows)


def local(
    tokens,
    routes,
    probs,
    w_gate,
    w_up,
    w_down,
    gate_left,
    gate_right,
    up_left,
    up_right,
    down_left,
    down_right,
):
    rows, width = tokens.shape
    exp_dev, _, cols = w_gate.shape
    rank = gate_left.shape[1]
    block = gate_left.shape[2]
    parts = lax.axis_size("mp")
    chips = lax.axis_size("y")
    experts = exp_dev * chips * 2
    me_g = lax.axis_index("y") * 2 + lax.axis_index("core")
    ranks = exp_dev * rank
    hid = exp_dev * cols

    def along_z(value, step):
        return lax.ppermute(value, "mp", [(i, (i + step) % parts) for i in range(parts)])

    def along_y(value, step):
        return lax.ppermute(value, "y", [(i, (i + step) % chips) for i in range(chips)])

    def other_core(value):
        return lax.ppermute(value, "core", [(0, 1), (1, 0)])

    pair = 2 * (-(-experts // 64) * 64)
    sent = attach(tokens, routes, probs, pair)
    arrived = [along_z(sent, k) for k in range(1, parts)]
    first = [along_y(sent, s) for s in range(1, chips)]
    left, *small = cut((gate_right, up_right, down_left), (gate_left, up_left), parts)
    gate_w = load(jnp.swapaxes(w_gate, 1, 2).reshape(hid, width))
    rest = after(jnp.concatenate(arrived), (left, small, gate_w))
    lines = [jnp.concatenate([sent, rest])]
    partner = [other_core(lines[0])]
    small = after(tuple(small), rest)
    small = [small[0]] + [along_z(small[k], k) for k in range(1, parts)]
    right = after(down_right.reshape(ranks, block), rest)
    partner_right = other_core(right)
    for s in range(1, chips):
        line = jnp.concatenate([first[s - 1], along_y(rest, s)])
        line = after(line, (tuple(small), partner_right))
        lines.append(line)
        partner.append(other_core(line))
    lines += partner
    diag = spread(small, parts, exp_dev)

    lines = after(tuple(lines), diag)
    inner = inner_products(lines, left, parts, rows)
    inner = [inner[0]] + [along_z(inner[k], k) for k in range(1, parts)]
    up_w = jnp.swapaxes(w_up, 1, 2).reshape(hid, width)
    raw = raw_products(lines, gate_w, up_w)
    first_expert = (me_g * exp_dev)[None]
    hidden, near, far = hidden_units(
        first_expert, lines, inner, raw, diag, parts, exp_dev, pair
    )
    swapped = other_core(far)
    bottom = turn(near, swapped, parts, rows)
    bottom = [bottom[0]] + [along_z(bottom[k], k) for k in range(1, parts)]

    near, far = down_products(hidden, w_down.reshape(hid, width))
    out, *others = fold(near, other_core(after(far, swapped)), chips, rows)
    backs = [along_y(others[2 * s - 1], -s) for s in range(1, chips)]

    low, *lows = extra_products(right, partner_right, bottom, chips)
    lows = [along_y(lows[s - 1], -s) for s in range(1, chips)]

    heads = [along_y(after(others[2 * s - 2], backs[s - 1]), -s) for s in range(1, chips)]
    result, *pieces = merge(out, low, backs, lows, rows)
    for piece in heads:
        result += piece.astype(F32)
    for k in range(1, parts):
        result += along_z(pieces[k - 1], -k).astype(F32)
    return result.astype(BF)


def solution(mesh):
    count = mesh.shape
    fine = jax.sharding.Mesh(
        mesh.devices.reshape(count["groups"], count["expert"] // 2, 2, count["mp"]),
        ("groups", "y", "core", "mp"),
    )
    expert = ("y", "core")
    return jax.shard_map(
        local,
        mesh=fine,
        in_specs=(
            P(("groups", "y", "core", "mp"), None),
            P(("groups", "y", "core", "mp"), None),
            P(("groups", "y", "core", "mp"), None),
            P(expert, None, "mp"),
            P(expert, None, "mp"),
            P(expert, "mp", None),
            P(expert, None, "mp"),
            P(expert, "mp", None),
            P(expert, None, "mp"),
            P(expert, "mp", None),
            P(expert, "mp", None),
            P(expert, None, "mp"),
        ),
        out_specs=P(("groups", "y", "core", "mp"), None),
        check_vma=False,
    )
```

```python
import functools

import jax
import jax.numpy as jnp
from jax import lax
from jax.experimental import pallas as pl
from jax.experimental.pallas import tpu as pltpu
from jax.sharding import PartitionSpec as P

BF = jnp.bfloat16
F32 = jnp.float32
SMALL_LIMIT = 4 * 1024 * 1024
VMEM_LIMIT = 12 * 1024 * 1024
PIECES = 8
BRIEF = pl.CostEstimate(flops=1, bytes_accessed=1, transcendentals=0)


def dot_nt(a, b):
    return lax.dot_general(a, b, (((1,), (1,)), ((), ())), preferred_element_type=F32)


def dot_nn(a, b):
    return lax.dot_general(a, b, (((1,), (0,)), ((), ())), preferred_element_type=F32)


def in_hbm(*values):
    return [pltpu.with_memory_space_constraint(v, pltpu.HBM) for v in values]


def after(value, earlier):
    return lax.optimization_barrier((value, earlier))[0]


def rotated(value, rows, parts, step):
    if step == 0:
        return value
    span = rows * parts
    lines = []
    for start in range(0, value.shape[0], span):
        cut = start + span - step * rows
        lines += [value[cut : start + span], value[start:cut]]
    return jnp.concatenate(lines)


def attach_kernel(tokens_ref, routes_ref, probs_ref, out_ref):
    rows, width = tokens_ref.shape
    pair = out_ref.shape[1] - width
    out_ref[:, :width] = tokens_ref[...]
    routes = routes_ref[...]
    probs = probs_ref[...]
    lane = lax.broadcasted_iota(jnp.int32, (rows, pair), 1)
    ids = jnp.where(lane < pair // 2, lane, lane - pair // 2)
    weight = jnp.zeros((rows, pair), F32)
    for k in range(routes.shape[1]):
        weight += jnp.where(ids == routes[:, k : k + 1], probs[:, k : k + 1], 0.0)
    high = weight.astype(BF).astype(F32)
    out_ref[:, width:] = jnp.where(lane < pair // 2, high, weight - high).astype(BF)


def attach(tokens, routes, probs, pair):
    rows, width = tokens.shape
    return pl.pallas_call(
        attach_kernel,
        out_shape=jax.ShapeDtypeStruct((rows, width + pair), BF),
        compiler_params=pltpu.CompilerParams(vmem_limit_bytes=SMALL_LIMIT),
        cost_estimate=BRIEF,
        name="attach",
    )(*in_hbm(tokens, routes, probs))


def prepare_kernel(parts, *refs):
    ins, lefts, weights = refs[:3], refs[3:5], refs[5:7]
    loaded, left_ref, outs, sems = refs[7:9], refs[9], refs[10:-1], refs[-1]
    step = weights[0].shape[0] // PIECES
    copies = []
    for n in range(2):
        for i in range(PIECES):
            span = pl.ds(i * step, step)
            copies.append(
                pltpu.make_async_copy(
                    weights[n].at[span], loaded[n].at[span], sems.at[n * PIECES + i]
                )
            )
    for copy in copies:
        copy.start()
    half = left_ref.shape[0] // 2
    for n, ref in enumerate(lefts):
        left_ref[n * half : (n + 1) * half] = ref[...].reshape(half, left_ref.shape[1])
    exp_dev, piece, hid = ins[0].shape
    cols = hid // parts
    me = lax.axis_index("mp")
    for n, ref in enumerate(ins):
        value = ref[...].reshape(exp_dev * piece, hid).astype(F32)
        blocks = [value[:, j * cols : (j + 1) * cols] for j in range(parts)]
        for k in range(parts):
            target = lax.rem(me + k, parts)
            block = blocks[0]
            for j in range(1, parts):
                block = jnp.where(target == j, blocks[j], block)
            outs[k][n] = block.astype(BF)
    for copy in copies:
        copy.wait()


def prepare(factors, lefts, weights, parts):
    exp_dev, piece, hid = factors[0].shape
    _, rank, block = lefts[0].shape
    vmem = pl.BlockSpec(memory_space=pltpu.VMEM)
    return pl.pallas_call(
        functools.partial(prepare_kernel, parts),
        in_specs=[vmem] * 5 + [pl.BlockSpec(memory_space=pltpu.HBM)] * 2,
        out_specs=[vmem] * (3 + parts),
        out_shape=[pltpu.VMEM(w.shape, w.dtype) for w in weights]
        + [jax.ShapeDtypeStruct((2 * exp_dev * rank, block), BF)]
        + [jax.ShapeDtypeStruct((3, exp_dev * piece, hid // parts), BF)] * parts,
        scratch_shapes=[pltpu.SemaphoreType.DMA((2 * PIECES,))],
        compiler_params=pltpu.CompilerParams(vmem_limit_bytes=SMALL_LIMIT),
        cost_estimate=BRIEF,
        name="prepare",
    )(*in_hbm(*factors, *lefts, *weights))


def spread_kernel(parts, exp_dev, *refs):
    pieces, out_ref = refs[:-1], refs[-1]
    _, ranks, hid = out_ref.shape
    rank = ranks // exp_dev
    piece = rank // parts
    me = lax.axis_index("mp")
    row = lax.broadcasted_iota(jnp.int32, (ranks, ranks), 0)
    col = lax.broadcasted_iota(jnp.int32, (ranks, ranks), 1)
    step = lax.rem(me - row % rank // piece + parts, parts)
    source = (step * exp_dev + row // rank) * piece + row % piece
    order = (col == source).astype(F32).astype(BF)
    cols = hid // exp_dev
    place = lax.broadcasted_iota(jnp.int32, (ranks, hid), 1)
    place -= lax.broadcasted_iota(jnp.int32, (ranks, hid), 0) // rank * cols
    own = (place >= 0) & (place < cols)
    for n in range(3):
        value = dot_nn(order, jnp.concatenate([p[n].astype(F32) for p in pieces]).astype(BF))
        value = jnp.concatenate([value] * exp_dev, axis=1)
        out_ref[n] = jnp.where(own, value, 0.0).astype(BF)


def spread(pieces, parts, exp_dev):
    _, span, cols = pieces[0].shape
    return pl.pallas_call(
        functools.partial(spread_kernel, parts, exp_dev),
        out_shape=jax.ShapeDtypeStruct((3, span * parts, cols * exp_dev), BF),
        compiler_params=pltpu.CompilerParams(vmem_limit_bytes=SMALL_LIMIT),
        cost_estimate=BRIEF,
        name="spread",
    )(*pieces)


def inner_kernel(parts, rows, count, *refs):
    lines, left_ref, outs = refs[:count], refs[count], refs[count + 1 :]
    block = left_ref.shape[1]
    offset = pl.multiple_of(lax.axis_index("mp") * block, 128)
    x = jnp.concatenate([line[:, pl.ds(offset, block)] for line in lines])
    value = dot_nt(x, left_ref[...])
    for k in range(parts):
        outs[k][...] = rotated(value, rows, parts, k).astype(BF)


def inner_products(lines, left, parts, rows):
    total = sum(line.shape[0] for line in lines)
    ranks = left.shape[0]
    return pl.pallas_call(
        functools.partial(inner_kernel, parts, rows, len(lines)),
        out_shape=[jax.ShapeDtypeStruct((total, ranks), BF)] * parts,
        compiler_params=pltpu.CompilerParams(vmem_limit_bytes=VMEM_LIMIT),
        cost_estimate=BRIEF,
        name="inner",
    )(*lines, left)


def raw_kernel(count, tile, *refs):
    lines, (gate_w, up_w, gate_ref, up_ref) = refs[:count], refs[count:]
    hid, width = gate_w.shape
    x = jnp.concatenate([line[:, :width] for line in lines])
    for i in range(hid // tile):
        span = pl.ds(i * tile, tile)
        gate_ref[:, span] = dot_nt(x, gate_w[span])
        up_ref[:, span] = dot_nt(x, up_w[span])


def raw_products(lines, gate_w, up_w):
    hid = gate_w.shape[0]
    total = sum(line.shape[0] for line in lines)
    tile = 256 if hid % 256 == 0 else 128
    return pl.pallas_call(
        functools.partial(raw_kernel, len(lines), tile),
        out_shape=[jax.ShapeDtypeStruct((total, hid), F32)] * 2,
        compiler_params=pltpu.CompilerParams(vmem_limit_bytes=VMEM_LIMIT),
        cost_estimate=BRIEF,
        name="raw",
    )(*lines, gate_w, up_w)


def hidden_kernel(parts, count, exp_dev, pair, *refs):
    lines, inner, rest = refs[:count], refs[count : count + parts], refs[count + parts :]
    gate_ref, up_ref, diag_ref, hidden_ref, near_ref, far_ref = rest
    hid = gate_ref.shape[1]
    ranks = diag_ref.shape[1]
    wide = lines[0].shape[1] - pair
    total = sum(ref[...].astype(F32) for ref in inner).astype(BF)
    gate = gate_ref[...] + dot_nn(total[:, :ranks], diag_ref[0])
    up = up_ref[...] + dot_nn(total[:, ranks:], diag_ref[1])
    lane = lax.broadcasted_iota(jnp.int32, (pair, hid), 0)
    lane = jnp.where(lane < pair // 2, lane, lane - pair // 2)
    cols = hid // exp_dev
    first = (lax.axis_index("y") * 2 + lax.axis_index("core")) * exp_dev
    place = lax.broadcasted_iota(jnp.int32, (pair, hid), 1) - (lane - first) * cols
    pick = ((place >= 0) & (place < cols)).astype(F32).astype(BF)
    scale = dot_nn(jnp.concatenate([line[:, wide:] for line in lines]), pick)
    hidden = (gate / (1.0 + jnp.exp(-gate)) * up * scale).astype(BF)
    hidden_ref[...] = hidden
    value = dot_nt(hidden, diag_ref[2])
    near = near_ref.shape[0]
    near_ref[...] = value[:near].astype(BF)
    far_ref[...] = value[near:].astype(BF)


def hidden_units(lines, inner, raw, diag, parts, exp_dev, pair):
    total, hid = raw[0].shape
    ranks = diag.shape[1]
    return pl.pallas_call(
        functools.partial(hidden_kernel, parts, len(lines), exp_dev, pair),
        out_shape=[jax.ShapeDtypeStruct((total, hid), BF)]
        + [jax.ShapeDtypeStruct((total // 2, ranks), BF)] * 2,
        compiler_params=pltpu.CompilerParams(vmem_limit_bytes=VMEM_LIMIT),
        cost_estimate=BRIEF,
        name="hidden",
    )(*lines, *inner, *raw, diag)


def down_kernel(hidden_ref, down_ref, near_ref, far_ref):
    near, width = near_ref.shape
    hidden = hidden_ref[...]
    tile = min(1024, width)
    for i in range(width // tile):
        span = slice(i * tile, (i + 1) * tile)
        value = dot_nn(hidden, down_ref[:, span])
        near_ref[:, span] = value[:near]
        far_ref[:, span] = value[near:].astype(BF)


def down_products(hidden, down_w):
    total, width = hidden.shape[0], down_w.shape[1]
    return pl.pallas_call(
        down_kernel,
        out_shape=[
            jax.ShapeDtypeStruct((total // 2, width), F32),
            jax.ShapeDtypeStruct((total // 2, width), BF),
        ],
        compiler_params=pltpu.CompilerParams(vmem_limit_bytes=VMEM_LIMIT),
        cost_estimate=BRIEF,
        name="down",
    )(hidden, down_w)


def turn_kernel(rows, near_ref, far_ref, *out_refs):
    value = jnp.concatenate([near_ref[...].astype(F32), far_ref[...].astype(F32)], axis=1)
    for k, out_ref in enumerate(out_refs):
        out_ref[...] = rotated(value, rows, len(out_refs), k).astype(BF)


def turn(near, far, parts, rows):
    total, ranks = near.shape
    return pl.pallas_call(
        functools.partial(turn_kernel, rows),
        out_shape=[jax.ShapeDtypeStruct((total, 2 * ranks), BF)] * parts,
        compiler_params=pltpu.CompilerParams(vmem_limit_bytes=SMALL_LIMIT),
        cost_estimate=BRIEF,
        name="turn",
    )(near, far)


def extra_kernel(chips, near_ref, far_ref, *refs):
    bottom, own_ref, outs = refs[: -chips], refs[-chips], refs[len(refs) - chips + 1 :]
    ranks, span = near_ref.shape[0], own_ref.shape[0]
    low = sum(ref[...].astype(F32) for ref in bottom).astype(BF)
    value = dot_nn(low[:, :ranks], near_ref[...]) + dot_nn(low[:, ranks:], far_ref[...])
    own_ref[...] = value[:span]
    for n, out_ref in enumerate(outs):
        out_ref[...] = value[(n + 1) * span : (n + 2) * span].astype(BF)


def extra_products(near, far, bottom, chips):
    span = bottom[0].shape[0] // chips
    block = near.shape[1]
    return pl.pallas_call(
        functools.partial(extra_kernel, chips),
        out_shape=[jax.ShapeDtypeStruct((span, block), F32)]
        + [jax.ShapeDtypeStruct((span, block), BF)] * (chips - 1),
        compiler_params=pltpu.CompilerParams(vmem_limit_bytes=VMEM_LIMIT),
        cost_estimate=BRIEF,
        name="extra",
    )(near, far, *bottom)


def fold_kernel(head, near_ref, far_ref, own_ref, *out_refs):
    span = own_ref.shape[0]
    total = near_ref[...] + far_ref[...].astype(F32)
    own_ref[...] = total[:span]
    for n in range(len(out_refs) // 2):
        line = total[(n + 1) * span : (n + 2) * span]
        out_refs[2 * n][...] = line[:head].astype(BF)
        out_refs[2 * n + 1][...] = line[head:].astype(BF)


def fold(near, far, chips, head):
    total, width = near.shape
    span = total // chips
    cuts = [head, span - head]
    return pl.pallas_call(
        functools.partial(fold_kernel, head),
        out_shape=[jax.ShapeDtypeStruct((span, width), F32)]
        + [jax.ShapeDtypeStruct((rows, width), BF) for rows in cuts] * (chips - 1),
        compiler_params=pltpu.CompilerParams(vmem_limit_bytes=VMEM_LIMIT),
        cost_estimate=BRIEF,
        name="fold",
    )(near, far)


def merge_kernel(count, own_ref, low_ref, *refs):
    backs, lows, outs = refs[:count], refs[count : 2 * count], refs[2 * count :]
    rows = outs[0].shape[0]
    block = low_ref.shape[1]
    offset = pl.multiple_of(lax.axis_index("mp") * block, 128)
    low = low_ref[...]
    for ref in lows:
        low += ref[...].astype(F32)
    total = own_ref[rows:]
    part = own_ref[:, pl.ds(offset, block)] + low
    after_own = part[rows:]
    for ref in backs:
        total += ref[...].astype(F32)
        after_own += ref[:, pl.ds(offset, block)].astype(F32)
    outs[0][...] = own_ref[:rows]
    outs[0][:, pl.ds(offset, block)] = part[:rows]
    for k in range(1, len(outs)):
        span = slice((k - 1) * rows, k * rows)
        outs[k][...] = total[span].astype(BF)
        outs[k][:, pl.ds(offset, block)] = after_own[span].astype(BF)


def merge(own, low, backs, lows, rows):
    total, width = own.shape
    return pl.pallas_call(
        functools.partial(merge_kernel, len(backs)),
        out_shape=[jax.ShapeDtypeStruct((rows, width), F32)]
        + [jax.ShapeDtypeStruct((rows, width), BF)] * (total // rows - 1),
        compiler_params=pltpu.CompilerParams(vmem_limit_bytes=VMEM_LIMIT),
        cost_estimate=BRIEF,
        name="merge",
    )(own, low, *backs, *lows)


def local(
    tokens,
    routes,
    probs,
    w_gate,
    w_up,
    w_down,
    gate_left,
    gate_right,
    up_left,
    up_right,
    down_left,
    down_right,
):
    rows, width = tokens.shape
    exp_dev, _, cols = w_gate.shape
    rank = gate_left.shape[1]
    block = gate_left.shape[2]
    parts = lax.axis_size("mp")
    chips = lax.axis_size("y")
    experts = exp_dev * chips * 2
    ranks = exp_dev * rank
    hid = exp_dev * cols

    def along_z(value, step):
        return lax.ppermute(value, "mp", [(i, (i + step) % parts) for i in range(parts)])

    def along_y(value, step):
        return lax.ppermute(value, "y", [(i, (i + step) % chips) for i in range(chips)])

    def other_core(value):
        return lax.ppermute(value, "core", [(0, 1), (1, 0)])

    pair = 2 * (-(-experts // 64) * 64)
    sent = attach(tokens, routes, probs, pair)
    arrived = [along_z(sent, k) for k in range(1, parts)]
    first = [along_y(sent, s) for s in range(1, chips)]
    weights = [jnp.swapaxes(w, 1, 2).reshape(hid, width) for w in (w_gate, w_up)]
    gate_w, up_w, left, *small = prepare(
        (gate_right, up_right, down_left), (gate_left, up_left), weights, parts
    )
    rest = after(jnp.concatenate(arrived), (left, small, gate_w, up_w))
    lines = [jnp.concatenate([sent, rest])]
    partner = [other_core(lines[0])]
    small = after(tuple(small), rest)
    small = [small[0]] + [along_z(small[k], k) for k in range(1, parts)]
    right = after(down_right.reshape(ranks, block), rest)
    partner_right = other_core(right)
    for s in range(1, chips):
        line = jnp.concatenate([first[s - 1], along_y(rest, s)])
        line = after(line, (tuple(small), partner_right))
        lines.append(line)
        partner.append(other_core(line))
    lines += partner
    diag = spread(small, parts, exp_dev)

    lines = after(tuple(lines), diag)
    inner = inner_products(lines, left, parts, rows)
    inner = [inner[0]] + [along_z(inner[k], k) for k in range(1, parts)]
    raw = raw_products(lines, gate_w, up_w)
    hidden, near, far = hidden_units(
        lines, inner, raw, diag, parts, exp_dev, pair
    )
    swapped = other_core(far)
    bottom = turn(near, swapped, parts, rows)
    bottom = [bottom[0]] + [along_z(bottom[k], k) for k in range(1, parts)]

    near, far = down_products(hidden, w_down.reshape(hid, width))
    out, *others = fold(near, other_core(after(far, swapped)), chips, rows)
    backs = [along_y(others[2 * s - 1], -s) for s in range(1, chips)]

    low, *lows = extra_products(right, partner_right, bottom, chips)
    lows = [along_y(lows[s - 1], -s) for s in range(1, chips)]

    heads = [along_y(after(others[2 * s - 2], backs[s - 1]), -s) for s in range(1, chips)]
    result, *pieces = merge(out, low, backs, lows, rows)
    for piece in heads:
        result += piece.astype(F32)
    for k in range(1, parts):
        result += along_z(pieces[k - 1], -k).astype(F32)
    return result.astype(BF)


def solution(mesh):
    count = mesh.shape
    fine = jax.sharding.Mesh(
        mesh.devices.reshape(count["groups"], count["expert"] // 2, 2, count["mp"]),
        ("groups", "y", "core", "mp"),
    )
    expert = ("y", "core")
    return jax.shard_map(
        local,
        mesh=fine,
        in_specs=(
            P(("groups", "y", "core", "mp"), None),
            P(("groups", "y", "core", "mp"), None),
            P(("groups", "y", "core", "mp"), None),
            P(expert, None, "mp"),
            P(expert, None, "mp"),
            P(expert, "mp", None),
            P(expert, None, "mp"),
            P(expert, "mp", None),
            P(expert, None, "mp"),
            P(expert, "mp", None),
            P(expert, "mp", None),
            P(expert, None, "mp"),
        ),
        out_specs=P(("groups", "y", "core", "mp"), None),
        check_vma=False,
    )
```

```python
import functools

import jax
import jax.numpy as jnp
from jax import lax
from jax.experimental import pallas as pl
from jax.experimental.pallas import tpu as pltpu
from jax.sharding import PartitionSpec as P

BF = jnp.bfloat16
F32 = jnp.float32
SMALL_LIMIT = 4 * 1024 * 1024
VMEM_LIMIT = 12 * 1024 * 1024
PIECES = 8
BRIEF = pl.CostEstimate(flops=1, bytes_accessed=1, transcendentals=0)


def dot_nt(a, b):
    return lax.dot_general(a, b, (((1,), (1,)), ((), ())), preferred_element_type=F32)


def dot_nn(a, b):
    return lax.dot_general(a, b, (((1,), (0,)), ((), ())), preferred_element_type=F32)


def in_hbm(*values):
    return [pltpu.with_memory_space_constraint(v, pltpu.HBM) for v in values]


def after(value, earlier):
    return lax.optimization_barrier((value, earlier))[0]


def rotated(value, rows, parts, step):
    if step == 0:
        return value
    blocks = []
    for start in range(0, value.shape[0], rows * parts):
        for k in range(parts):
            at = start + (k ^ step) * rows
            blocks.append(value[at : at + rows])
    return jnp.concatenate(blocks)


def attach_kernel(tokens_ref, routes_ref, probs_ref, out_ref):
    rows, width = tokens_ref.shape
    pair = out_ref.shape[1] - width
    out_ref[:, :width] = tokens_ref[...]
    routes = routes_ref[...]
    probs = probs_ref[...]
    lane = lax.broadcasted_iota(jnp.int32, (rows, pair), 1)
    ids = jnp.where(lane < pair // 2, lane, lane - pair // 2)
    weight = jnp.zeros((rows, pair), F32)
    for k in range(routes.shape[1]):
        weight += jnp.where(ids == routes[:, k : k + 1], probs[:, k : k + 1], 0.0)
    high = weight.astype(BF).astype(F32)
    out_ref[:, width:] = jnp.where(lane < pair // 2, high, weight - high).astype(BF)


def attach(tokens, routes, probs, pair):
    rows, width = tokens.shape
    return pl.pallas_call(
        attach_kernel,
        out_shape=jax.ShapeDtypeStruct((rows, width + pair), BF),
        compiler_params=pltpu.CompilerParams(vmem_limit_bytes=SMALL_LIMIT),
        cost_estimate=BRIEF,
        name="attach",
    )(*in_hbm(tokens, routes, probs))


def prepare_kernel(parts, *refs):
    ins, lefts, weights = refs[:3], refs[3:5], refs[5:7]
    loaded, left_ref, outs, sems = refs[7:9], refs[9], refs[10:-1], refs[-1]
    step = weights[0].shape[0] // PIECES
    copies = []
    for n in range(2):
        for i in range(PIECES):
            span = pl.ds(i * step, step)
            copies.append(
                pltpu.make_async_copy(
                    weights[n].at[span], loaded[n].at[span], sems.at[n * PIECES + i]
                )
            )
    for copy in copies:
        copy.start()
    half = left_ref.shape[0] // 2
    for n, ref in enumerate(lefts):
        left_ref[n * half : (n + 1) * half] = ref[...].reshape(half, left_ref.shape[1])
    exp_dev, piece, hid = ins[0].shape
    cols = hid // parts
    me = lax.axis_index("mp")
    for n, ref in enumerate(ins):
        value = ref[...].reshape(exp_dev * piece, hid).astype(F32)
        blocks = [value[:, j * cols : (j + 1) * cols] for j in range(parts)]
        for k in range(parts):
            target = me ^ k
            block = blocks[0]
            for j in range(1, parts):
                block = jnp.where(target == j, blocks[j], block)
            outs[k][n] = block.astype(BF)
    for copy in copies:
        copy.wait()


def prepare(factors, lefts, weights, parts):
    exp_dev, piece, hid = factors[0].shape
    _, rank, block = lefts[0].shape
    vmem = pl.BlockSpec(memory_space=pltpu.VMEM)
    return pl.pallas_call(
        functools.partial(prepare_kernel, parts),
        in_specs=[vmem] * 5 + [pl.BlockSpec(memory_space=pltpu.HBM)] * 2,
        out_specs=[vmem] * (3 + parts),
        out_shape=[pltpu.VMEM(w.shape, w.dtype) for w in weights]
        + [jax.ShapeDtypeStruct((2 * exp_dev * rank, block), BF)]
        + [jax.ShapeDtypeStruct((3, exp_dev * piece, hid // parts), BF)] * parts,
        scratch_shapes=[pltpu.SemaphoreType.DMA((2 * PIECES,))],
        compiler_params=pltpu.CompilerParams(vmem_limit_bytes=SMALL_LIMIT),
        cost_estimate=BRIEF,
        name="prepare",
    )(*in_hbm(*factors, *lefts, *weights))


def spread_kernel(parts, exp_dev, *refs):
    pieces, out_ref = refs[:-1], refs[-1]
    _, ranks, hid = out_ref.shape
    rank = ranks // exp_dev
    piece = rank // parts
    me = lax.axis_index("mp")
    row = lax.broadcasted_iota(jnp.int32, (ranks, ranks), 0)
    col = lax.broadcasted_iota(jnp.int32, (ranks, ranks), 1)
    step = me ^ (row % rank // piece)
    source = (step * exp_dev + row // rank) * piece + row % piece
    order = (col == source).astype(F32).astype(BF)
    cols = hid // exp_dev
    place = lax.broadcasted_iota(jnp.int32, (ranks, hid), 1)
    place -= lax.broadcasted_iota(jnp.int32, (ranks, hid), 0) // rank * cols
    own = (place >= 0) & (place < cols)
    for n in range(3):
        value = dot_nn(order, jnp.concatenate([p[n].astype(F32) for p in pieces]).astype(BF))
        value = jnp.concatenate([value] * exp_dev, axis=1)
        out_ref[n] = jnp.where(own, value, 0.0).astype(BF)


def spread(pieces, parts, exp_dev):
    _, span, cols = pieces[0].shape
    return pl.pallas_call(
        functools.partial(spread_kernel, parts, exp_dev),
        out_shape=jax.ShapeDtypeStruct((3, span * parts, cols * exp_dev), BF),
        compiler_params=pltpu.CompilerParams(vmem_limit_bytes=SMALL_LIMIT),
        cost_estimate=BRIEF,
        name="spread",
    )(*pieces)


def inner_kernel(parts, rows, count, *refs):
    lines, left_ref, outs = refs[:count], refs[count], refs[count + 1 :]
    block = left_ref.shape[1]
    offset = pl.multiple_of(lax.axis_index("mp") * block, 128)
    x = jnp.concatenate([line[:, pl.ds(offset, block)] for line in lines])
    value = dot_nt(x, left_ref[...])
    for k in range(parts):
        outs[k][...] = rotated(value, rows, parts, k).astype(BF)


def inner_products(lines, left, parts, rows):
    total = sum(line.shape[0] for line in lines)
    ranks = left.shape[0]
    return pl.pallas_call(
        functools.partial(inner_kernel, parts, rows, len(lines)),
        out_shape=[jax.ShapeDtypeStruct((total, ranks), BF)] * parts,
        compiler_params=pltpu.CompilerParams(vmem_limit_bytes=VMEM_LIMIT),
        cost_estimate=BRIEF,
        name="inner",
    )(*lines, left)


def raw_kernel(count, tile, *refs):
    lines, (gate_w, up_w, gate_ref, up_ref) = refs[:count], refs[count:]
    hid, width = gate_w.shape
    x = jnp.concatenate([line[:, :width] for line in lines])
    for i in range(hid // tile):
        span = pl.ds(i * tile, tile)
        gate_ref[:, span] = dot_nt(x, gate_w[span])
        up_ref[:, span] = dot_nt(x, up_w[span])


def raw_products(lines, gate_w, up_w):
    hid = gate_w.shape[0]
    total = sum(line.shape[0] for line in lines)
    tile = 256 if hid % 256 == 0 else 128
    return pl.pallas_call(
        functools.partial(raw_kernel, len(lines), tile),
        out_shape=[jax.ShapeDtypeStruct((total, hid), F32)] * 2,
        compiler_params=pltpu.CompilerParams(vmem_limit_bytes=VMEM_LIMIT),
        cost_estimate=BRIEF,
        name="raw",
    )(*lines, gate_w, up_w)


def hidden_kernel(parts, count, exp_dev, pair, *refs):
    lines, inner, rest = refs[:count], refs[count : count + parts], refs[count + parts :]
    gate_ref, up_ref, diag_ref, hidden_ref, near_ref, far_ref = rest
    hid = gate_ref.shape[1]
    ranks = diag_ref.shape[1]
    wide = lines[0].shape[1] - pair
    total = sum(ref[...].astype(F32) for ref in inner).astype(BF)
    gate = gate_ref[...] + dot_nn(total[:, :ranks], diag_ref[0])
    up = up_ref[...] + dot_nn(total[:, ranks:], diag_ref[1])
    lane = lax.broadcasted_iota(jnp.int32, (pair, hid), 0)
    lane = jnp.where(lane < pair // 2, lane, lane - pair // 2)
    cols = hid // exp_dev
    first = (lax.axis_index("y") * 2 + lax.axis_index("core")) * exp_dev
    place = lax.broadcasted_iota(jnp.int32, (pair, hid), 1) - (lane - first) * cols
    pick = ((place >= 0) & (place < cols)).astype(F32).astype(BF)
    scale = dot_nn(jnp.concatenate([line[:, wide:] for line in lines]), pick)
    hidden = (gate / (1.0 + jnp.exp(-gate)) * up * scale).astype(BF)
    hidden_ref[...] = hidden
    value = dot_nt(hidden, diag_ref[2])
    near = near_ref.shape[0]
    near_ref[...] = value[:near].astype(BF)
    far_ref[...] = value[near:].astype(BF)


def hidden_units(lines, inner, raw, diag, parts, exp_dev, pair):
    total, hid = raw[0].shape
    ranks = diag.shape[1]
    return pl.pallas_call(
        functools.partial(hidden_kernel, parts, len(lines), exp_dev, pair),
        out_shape=[jax.ShapeDtypeStruct((total, hid), BF)]
        + [jax.ShapeDtypeStruct((total // 2, ranks), BF)] * 2,
        compiler_params=pltpu.CompilerParams(vmem_limit_bytes=VMEM_LIMIT),
        cost_estimate=BRIEF,
        name="hidden",
    )(*lines, *inner, *raw, diag)


def down_kernel(hidden_ref, down_ref, near_ref, far_ref):
    near, width = near_ref.shape
    hidden = hidden_ref[...]
    tile = min(1024, width)
    for i in range(width // tile):
        span = slice(i * tile, (i + 1) * tile)
        value = dot_nn(hidden, down_ref[:, span])
        near_ref[:, span] = value[:near]
        far_ref[:, span] = value[near:].astype(BF)


def down_products(hidden, down_w):
    total, width = hidden.shape[0], down_w.shape[1]
    return pl.pallas_call(
        down_kernel,
        out_shape=[
            jax.ShapeDtypeStruct((total // 2, width), F32),
            jax.ShapeDtypeStruct((total // 2, width), BF),
        ],
        compiler_params=pltpu.CompilerParams(vmem_limit_bytes=VMEM_LIMIT),
        cost_estimate=BRIEF,
        name="down",
    )(hidden, down_w)


def pair_kernel(near_ref, far_ref, *out_refs):
    value = jnp.concatenate([near_ref[...].astype(F32), far_ref[...].astype(F32)], axis=1)
    span = out_refs[0].shape[0]
    for n, out_ref in enumerate(out_refs):
        out_ref[...] = value[n * span : (n + 1) * span].astype(BF)


def side_by_side(near, far, chips):
    total, ranks = near.shape
    return pl.pallas_call(
        pair_kernel,
        out_shape=[jax.ShapeDtypeStruct((total // chips, 2 * ranks), BF)] * chips,
        compiler_params=pltpu.CompilerParams(vmem_limit_bytes=SMALL_LIMIT),
        cost_estimate=BRIEF,
        name="pair",
    )(near, far)


def turn_kernel(rows, chips, *refs):
    ins, outs = refs[:chips], refs[chips:]
    value = jnp.concatenate([ref[...].astype(F32) for ref in ins], axis=1)
    for k, out_ref in enumerate(outs):
        out_ref[...] = rotated(value, rows, len(outs), k).astype(BF)


def turn(lines, parts, rows):
    span, ranks = lines[0].shape
    return pl.pallas_call(
        functools.partial(turn_kernel, rows, len(lines)),
        out_shape=[jax.ShapeDtypeStruct((span, len(lines) * ranks), BF)] * parts,
        compiler_params=pltpu.CompilerParams(vmem_limit_bytes=SMALL_LIMIT),
        cost_estimate=BRIEF,
        name="turn",
    )(*lines)


def fold_kernel(head, near_ref, far_ref, own_ref, *out_refs):
    span = own_ref.shape[0]
    total = near_ref[...] + far_ref[...].astype(F32)
    own_ref[...] = total[:span]
    for n in range(len(out_refs) // 2):
        line = total[(n + 1) * span : (n + 2) * span]
        out_refs[2 * n][...] = line[:head].astype(BF)
        out_refs[2 * n + 1][...] = line[head:].astype(BF)


def fold(near, far, chips, head):
    total, width = near.shape
    span = total // chips
    cuts = [head, span - head]
    return pl.pallas_call(
        functools.partial(fold_kernel, head),
        out_shape=[jax.ShapeDtypeStruct((span, width), F32)]
        + [jax.ShapeDtypeStruct((rows, width), BF) for rows in cuts] * (chips - 1),
        compiler_params=pltpu.CompilerParams(vmem_limit_bytes=VMEM_LIMIT),
        cost_estimate=BRIEF,
        name="fold",
    )(near, far)


def merge_kernel(chips, parts, *refs):
    own_ref, rights, refs = refs[0], refs[1 : 1 + 2 * chips], refs[1 + 2 * chips :]
    bottom, backs, outs = refs[:parts], refs[parts:-parts], refs[-parts:]
    rows = outs[0].shape[0]
    ranks, block = rights[0].shape
    offset = pl.multiple_of(lax.axis_index("mp") * block, 128)
    low = sum(ref[...].astype(F32) for ref in bottom).astype(BF)
    value = jnp.zeros((low.shape[0], block), F32)
    for n, ref in enumerate(rights):
        at = (2 * n if n < chips else 2 * (n - chips) + 1) * ranks
        value += dot_nn(low[:, at : at + ranks], ref[...])
    total = own_ref[rows:]
    value += own_ref[:, pl.ds(offset, block)]
    rest = value[rows:]
    for ref in backs:
        total += ref[...].astype(F32)
        rest += ref[:, pl.ds(offset, block)].astype(F32)
    outs[0][...] = own_ref[:rows]
    outs[0][:, pl.ds(offset, block)] = value[:rows]
    for k in range(1, parts):
        span = slice((k - 1) * rows, k * rows)
        outs[k][...] = total[span].astype(BF)
        outs[k][:, pl.ds(offset, block)] = rest[span].astype(BF)


def merge(own, rights, bottom, backs, rows):
    total, width = own.shape
    parts = total // rows
    return pl.pallas_call(
        functools.partial(merge_kernel, len(backs) + 1, parts),
        out_shape=[jax.ShapeDtypeStruct((rows, width), F32)]
        + [jax.ShapeDtypeStruct((rows, width), BF)] * (parts - 1),
        compiler_params=pltpu.CompilerParams(vmem_limit_bytes=VMEM_LIMIT),
        cost_estimate=BRIEF,
        name="merge",
    )(own, *rights, *bottom, *backs)


def local(
    tokens,
    routes,
    probs,
    w_gate,
    w_up,
    w_down,
    gate_left,
    gate_right,
    up_left,
    up_right,
    down_left,
    down_right,
):
    rows, width = tokens.shape
    exp_dev, _, cols = w_gate.shape
    rank = gate_left.shape[1]
    block = gate_left.shape[2]
    parts = lax.axis_size("mp")
    chips = lax.axis_size("y")
    experts = exp_dev * chips * 2
    ranks = exp_dev * rank
    hid = exp_dev * cols

    def along_z(value, step):
        return lax.ppermute(value, "mp", [(i, i ^ step) for i in range(parts)])

    def along_y(value, step):
        return lax.ppermute(value, "y", [(i, (i + step) % chips) for i in range(chips)])

    def other_core(value):
        return lax.ppermute(value, "core", [(0, 1), (1, 0)])

    pair = 2 * (-(-experts // 64) * 64)
    sent = attach(tokens, routes, probs, pair)
    arrived = [along_z(sent, k) for k in range(1, parts)]
    first = [along_y(sent, s) for s in range(1, chips)]
    weights = [jnp.swapaxes(w, 1, 2).reshape(hid, width) for w in (w_gate, w_up)]
    gate_w, up_w, left, *small = prepare(
        (gate_right, up_right, down_left), (gate_left, up_left), weights, parts
    )
    right = down_right.reshape(ranks, block)
    rest = after(jnp.concatenate(arrived), (left, small, gate_w, up_w))
    lines = [jnp.concatenate([sent, rest])]
    partner = [other_core(lines[0])]
    small = after(tuple(small), rest)
    small = [small[0]] + [along_z(small[k], k) for k in range(1, parts)]
    for s in range(1, chips):
        line = jnp.concatenate([first[s - 1], along_y(rest, s)])
        line = after(line, tuple(small))
        lines.append(line)
        partner.append(other_core(line))
    lines += partner
    diag = spread(small, parts, exp_dev)

    lines = after(tuple(lines), diag)
    inner = inner_products(lines, left, parts, rows)
    inner = [along_z(inner[k], k) for k in range(parts - 1, 0, -1)] + [inner[0]]
    raw = raw_products(lines, gate_w, up_w)
    right = after(right, lines[chips - 1])
    rights = [right] + [along_y(right, -s) for s in range(1, chips)]
    raw = after(tuple(raw), rights[1:])
    rights += [other_core(right) for right in rights]
    hidden, near, far = hidden_units(
        lines, inner, raw, diag, parts, exp_dev, pair
    )
    swapped = other_core(far)
    low, *lows = side_by_side(near, swapped, chips)
    lows = [along_y(lows[s - 1], -s) for s in range(1, chips)]
    bottom = turn([low] + lows, parts, rows)
    bottom = [along_z(bottom[k], k) for k in range(parts - 1, 0, -1)] + [bottom[0]]

    near, far = down_products(hidden, w_down.reshape(hid, width))
    far = after(other_core(after(far, swapped)), lows)
    out, *others = fold(near, far, chips, rows)
    backs = [along_y(others[2 * s - 1], -s) for s in range(1, chips)]
    heads = [along_y(after(others[2 * s - 2], bottom[0]), -s) for s in range(1, chips)]
    own, *pieces = merge(out, rights, bottom, backs, rows)
    result = along_z(pieces[-1], parts - 1).astype(F32)
    for k in range(parts - 2, 0, -1):
        result += along_z(pieces[k - 1], k).astype(F32)
    for piece in heads:
        result += piece.astype(F32)
    return (result + own).astype(BF)


def solution(mesh):
    count = mesh.shape
    fine = jax.sharding.Mesh(
        mesh.devices.reshape(count["groups"], count["expert"] // 2, 2, count["mp"]),
        ("groups", "y", "core", "mp"),
    )
    expert = ("y", "core")
    return jax.shard_map(
        local,
        mesh=fine,
        in_specs=(
            P(("groups", "y", "core", "mp"), None),
            P(("groups", "y", "core", "mp"), None),
            P(("groups", "y", "core", "mp"), None),
            P(expert, None, "mp"),
            P(expert, None, "mp"),
            P(expert, "mp", None),
            P(expert, None, "mp"),
            P(expert, "mp", None),
            P(expert, None, "mp"),
            P(expert, "mp", None),
            P(expert, "mp", None),
            P(expert, None, "mp"),
        ),
        out_specs=P(("groups", "y", "core", "mp"), None),
        check_vma=False,
    )
```

```python
import functools

import jax
import jax.numpy as jnp
from jax import lax
from jax.experimental import pallas as pl
from jax.experimental.pallas import tpu as pltpu
from jax.sharding import PartitionSpec as P

BF = jnp.bfloat16
F32 = jnp.float32
SMALL_LIMIT = 4 * 1024 * 1024
VMEM_LIMIT = 12 * 1024 * 1024
PIECES = 8
LONG = pl.CostEstimate(flops=100_000_000_000, bytes_accessed=12_000_000, transcendentals=0)
BRIEF = pl.CostEstimate(flops=1, bytes_accessed=1, transcendentals=0)


def dot_nt(a, b):
    return lax.dot_general(a, b, (((1,), (1,)), ((), ())), preferred_element_type=F32)


def dot_nn(a, b):
    return lax.dot_general(a, b, (((1,), (0,)), ((), ())), preferred_element_type=F32)


def in_hbm(*values):
    return [pltpu.with_memory_space_constraint(v, pltpu.HBM) for v in values]


def after(value, earlier):
    return lax.optimization_barrier((value, earlier))[0]


def rotated(value, rows, parts, step):
    if step == 0:
        return value
    span = rows * parts
    lines = []
    for start in range(0, value.shape[0], span):
        cut = start + span - step * rows
        lines += [value[cut : start + span], value[start:cut]]
    return jnp.concatenate(lines)


def attach_kernel(tokens_ref, routes_ref, probs_ref, out_ref):
    rows, width = tokens_ref.shape
    pair = out_ref.shape[1] - width
    out_ref[:, :width] = tokens_ref[...]
    routes = routes_ref[...]
    probs = probs_ref[...]
    lane = lax.broadcasted_iota(jnp.int32, (rows, pair), 1)
    ids = jnp.where(lane < pair // 2, lane, lane - pair // 2)
    weight = jnp.zeros((rows, pair), F32)
    for k in range(routes.shape[1]):
        weight += jnp.where(ids == routes[:, k : k + 1], probs[:, k : k + 1], 0.0)
    high = weight.astype(BF).astype(F32)
    out_ref[:, width:] = jnp.where(lane < pair // 2, high, weight - high).astype(BF)


def attach(tokens, routes, probs, pair):
    rows, width = tokens.shape
    return pl.pallas_call(
        attach_kernel,
        out_shape=jax.ShapeDtypeStruct((rows, width + pair), BF),
        compiler_params=pltpu.CompilerParams(vmem_limit_bytes=SMALL_LIMIT),
        cost_estimate=BRIEF,
        name="attach",
    )(*in_hbm(tokens, routes, probs))


def piece_copies(source, target, sems):
    step = source.shape[0] // PIECES
    spans = [pl.ds(i * step, step) for i in range(PIECES)]
    return [
        pltpu.make_async_copy(source.at[span], target.at[span], sems.at[i])
        for i, span in enumerate(spans)
    ]


def load_kernel(source, target, sems):
    copies = piece_copies(source, target, sems)
    for copy in copies:
        copy.start()
    for copy in copies:
        copy.wait()


def load(weights):
    return pl.pallas_call(
        load_kernel,
        in_specs=[pl.BlockSpec(memory_space=pltpu.HBM)],
        out_specs=pl.BlockSpec(memory_space=pltpu.VMEM),
        out_shape=pltpu.VMEM(weights.shape, weights.dtype),
        scratch_shapes=[pltpu.SemaphoreType.DMA((PIECES,))],
        compiler_params=pltpu.CompilerParams(vmem_limit_bytes=SMALL_LIMIT),
        cost_estimate=BRIEF,
        name="load",
    )(*in_hbm(weights))


def prepare_kernel(parts, *refs):
    ins, lefts, source = refs[:3], refs[3:5], refs[5]
    target, left_ref, outs, sems = refs[6], refs[7], refs[8:-1], refs[-1]
    copies = piece_copies(source, target, sems)
    for copy in copies:
        copy.start()
    half = left_ref.shape[0] // 2
    for n, ref in enumerate(lefts):
        left_ref[n * half : (n + 1) * half] = ref[...].reshape(half, left_ref.shape[1])
    exp_dev, piece, hid = ins[0].shape
    cols = hid // parts
    me = lax.axis_index("mp")
    for n, ref in enumerate(ins):
        value = ref[...].reshape(exp_dev * piece, hid).astype(F32)
        blocks = [value[:, j * cols : (j + 1) * cols] for j in range(parts)]
        for k in range(parts):
            device = lax.rem(me + k, parts)
            block = blocks[0]
            for j in range(1, parts):
                block = jnp.where(device == j, blocks[j], block)
            outs[k][n] = block.astype(BF)
    for copy in copies:
        copy.wait()


def prepare(factors, lefts, weights, parts):
    exp_dev, piece, hid = factors[0].shape
    _, rank, block = lefts[0].shape
    vmem = pl.BlockSpec(memory_space=pltpu.VMEM)
    return pl.pallas_call(
        functools.partial(prepare_kernel, parts),
        in_specs=[vmem] * 5 + [pl.BlockSpec(memory_space=pltpu.HBM)],
        out_specs=[vmem] * (2 + parts),
        out_shape=[pltpu.VMEM(weights.shape, weights.dtype)]
        + [jax.ShapeDtypeStruct((2 * exp_dev * rank, block), BF)]
        + [jax.ShapeDtypeStruct((3, exp_dev * piece, hid // parts), BF)] * parts,
        scratch_shapes=[pltpu.SemaphoreType.DMA((PIECES,))],
        compiler_params=pltpu.CompilerParams(vmem_limit_bytes=SMALL_LIMIT),
        cost_estimate=BRIEF,
        name="prepare",
    )(*in_hbm(*factors, *lefts, weights))


def spread_kernel(parts, exp_dev, *refs):
    pieces, out_ref = refs[:-1], refs[-1]
    _, ranks, hid = out_ref.shape
    rank = ranks // exp_dev
    piece = rank // parts
    me = lax.axis_index("mp")
    row = lax.broadcasted_iota(jnp.int32, (ranks, ranks), 0)
    col = lax.broadcasted_iota(jnp.int32, (ranks, ranks), 1)
    step = lax.rem(me - row % rank // piece + parts, parts)
    source = (step * exp_dev + row // rank) * piece + row % piece
    order = (col == source).astype(F32).astype(BF)
    cols = hid // exp_dev
    place = lax.broadcasted_iota(jnp.int32, (ranks, hid), 1)
    place -= lax.broadcasted_iota(jnp.int32, (ranks, hid), 0) // rank * cols
    own = (place >= 0) & (place < cols)
    for n in range(3):
        value = dot_nn(order, jnp.concatenate([p[n].astype(F32) for p in pieces]).astype(BF))
        value = jnp.concatenate([value] * exp_dev, axis=1)
        out_ref[n] = jnp.where(own, value, 0.0).astype(BF)


def spread(pieces, parts, exp_dev):
    _, span, cols = pieces[0].shape
    return pl.pallas_call(
        functools.partial(spread_kernel, parts, exp_dev),
        out_shape=jax.ShapeDtypeStruct((3, span * parts, cols * exp_dev), BF),
        compiler_params=pltpu.CompilerParams(vmem_limit_bytes=SMALL_LIMIT),
        cost_estimate=BRIEF,
        name="spread",
    )(*pieces)


def inner_kernel(parts, rows, count, *refs):
    lines, left_ref, outs = refs[:count], refs[count], refs[count + 1 :]
    block = left_ref.shape[1]
    offset = pl.multiple_of(lax.axis_index("mp") * block, 128)
    x = jnp.concatenate([line[:, pl.ds(offset, block)] for line in lines])
    value = dot_nt(x, left_ref[...])
    for k in range(parts):
        outs[k][...] = rotated(value, rows, parts, k).astype(BF)


def inner_products(lines, left, parts, rows):
    total = sum(line.shape[0] for line in lines)
    ranks = left.shape[0]
    return pl.pallas_call(
        functools.partial(inner_kernel, parts, rows, len(lines)),
        out_shape=[jax.ShapeDtypeStruct((total, ranks), BF)] * parts,
        compiler_params=pltpu.CompilerParams(vmem_limit_bytes=VMEM_LIMIT),
        cost_estimate=BRIEF,
        name="inner",
    )(*lines, left)


def raw_kernel(count, tile, *refs):
    lines, (gate_w, up_w, gate_ref, up_ref) = refs[:count], refs[count:]
    hid, width = gate_w.shape
    x = jnp.concatenate([line[:, :width] for line in lines])
    for i in range(hid // tile):
        span = pl.ds(i * tile, tile)
        gate_ref[:, span] = dot_nt(x, gate_w[span])
        up_ref[:, span] = dot_nt(x, up_w[span])


def raw_products(lines, gate_w, up_w):
    hid = gate_w.shape[0]
    total = sum(line.shape[0] for line in lines)
    tile = 256 if hid % 256 == 0 else 128
    return pl.pallas_call(
        functools.partial(raw_kernel, len(lines), tile),
        out_shape=[jax.ShapeDtypeStruct((total, hid), F32)] * 2,
        compiler_params=pltpu.CompilerParams(vmem_limit_bytes=VMEM_LIMIT),
        cost_estimate=BRIEF,
        name="raw",
    )(*lines, gate_w, up_w)


def hidden_kernel(parts, count, exp_dev, pair, *refs):
    lines, inner, rest = refs[:count], refs[count : count + parts], refs[count + parts :]
    gate_ref, up_ref, diag_ref, hidden_ref, near_ref, far_ref = rest
    hid = gate_ref.shape[1]
    ranks = diag_ref.shape[1]
    wide = lines[0].shape[1] - pair
    total = sum(ref[...].astype(F32) for ref in inner).astype(BF)
    gate = gate_ref[...] + dot_nn(total[:, :ranks], diag_ref[0])
    up = up_ref[...] + dot_nn(total[:, ranks:], diag_ref[1])
    lane = lax.broadcasted_iota(jnp.int32, (pair, hid), 0)
    lane = jnp.where(lane < pair // 2, lane, lane - pair // 2)
    cols = hid // exp_dev
    first = (lax.axis_index("y") * 2 + lax.axis_index("core")) * exp_dev
    place = lax.broadcasted_iota(jnp.int32, (pair, hid), 1) - (lane - first) * cols
    pick = ((place >= 0) & (place < cols)).astype(F32).astype(BF)
    scale = dot_nn(jnp.concatenate([line[:, wide:] for line in lines]), pick)
    hidden = (gate / (1.0 + jnp.exp(-gate)) * up * scale).astype(BF)
    hidden_ref[...] = hidden
    value = dot_nt(hidden, diag_ref[2])
    near = near_ref.shape[0]
    near_ref[...] = value[:near].astype(BF)
    far_ref[...] = value[near:].astype(BF)


def hidden_units(lines, inner, raw, diag, parts, exp_dev, pair):
    total, hid = raw[0].shape
    ranks = diag.shape[1]
    return pl.pallas_call(
        functools.partial(hidden_kernel, parts, len(lines), exp_dev, pair),
        out_shape=[jax.ShapeDtypeStruct((total, hid), BF)]
        + [jax.ShapeDtypeStruct((total // 2, ranks), BF)] * 2,
        compiler_params=pltpu.CompilerParams(vmem_limit_bytes=VMEM_LIMIT),
        cost_estimate=BRIEF,
        name="hidden",
    )(*lines, *inner, *raw, diag)


def down_kernel(hidden_ref, down_ref, near_ref, far_ref):
    near, width = near_ref.shape
    hidden = hidden_ref[...]
    tile = min(1024, width)
    for i in range(width // tile):
        span = slice(i * tile, (i + 1) * tile)
        value = dot_nn(hidden, down_ref[:, span])
        near_ref[:, span] = value[:near]
        far_ref[:, span] = value[near:].astype(BF)


def down_products(hidden, down_w):
    total, width = hidden.shape[0], down_w.shape[1]
    return pl.pallas_call(
        down_kernel,
        out_shape=[
            jax.ShapeDtypeStruct((total // 2, width), F32),
            jax.ShapeDtypeStruct((total // 2, width), BF),
        ],
        compiler_params=pltpu.CompilerParams(vmem_limit_bytes=VMEM_LIMIT),
        cost_estimate=BRIEF,
        name="down",
    )(hidden, down_w)


def turn_kernel(rows, near_ref, far_ref, *out_refs):
    value = jnp.concatenate([near_ref[...].astype(F32), far_ref[...].astype(F32)], axis=1)
    for k, out_ref in enumerate(out_refs):
        out_ref[...] = rotated(value, rows, len(out_refs), k).astype(BF)


def turn(near, far, parts, rows):
    total, ranks = near.shape
    return pl.pallas_call(
        functools.partial(turn_kernel, rows),
        out_shape=[jax.ShapeDtypeStruct((total, 2 * ranks), BF)] * parts,
        compiler_params=pltpu.CompilerParams(vmem_limit_bytes=SMALL_LIMIT),
        cost_estimate=BRIEF,
        name="turn",
    )(near, far)


def extra_kernel(chips, near_ref, far_ref, *refs):
    bottom, own_ref, outs = refs[: -chips], refs[-chips], refs[len(refs) - chips + 1 :]
    ranks, span = near_ref.shape[0], own_ref.shape[0]
    low = sum(ref[...].astype(F32) for ref in bottom).astype(BF)
    value = dot_nn(low[:, :ranks], near_ref[...]) + dot_nn(low[:, ranks:], far_ref[...])
    own_ref[...] = value[:span]
    for n, out_ref in enumerate(outs):
        out_ref[...] = value[(n + 1) * span : (n + 2) * span].astype(BF)


def extra_products(near, far, bottom, chips):
    span = bottom[0].shape[0] // chips
    block = near.shape[1]
    return pl.pallas_call(
        functools.partial(extra_kernel, chips),
        out_shape=[jax.ShapeDtypeStruct((span, block), F32)]
        + [jax.ShapeDtypeStruct((span, block), BF)] * (chips - 1),
        compiler_params=pltpu.CompilerParams(vmem_limit_bytes=VMEM_LIMIT),
        cost_estimate=LONG,
        name="extra",
    )(near, far, *bottom)


def fold_kernel(head, near_ref, far_ref, own_ref, *out_refs):
    span = own_ref.shape[0]
    total = near_ref[...] + far_ref[...].astype(F32)
    own_ref[...] = total[:span]
    for n in range(len(out_refs) // 2):
        line = total[(n + 1) * span : (n + 2) * span]
        out_refs[2 * n][...] = line[:head].astype(BF)
        out_refs[2 * n + 1][...] = line[head:].astype(BF)


def fold(near, far, chips, head):
    total, width = near.shape
    span = total // chips
    cuts = [head, span - head]
    return pl.pallas_call(
        functools.partial(fold_kernel, head),
        out_shape=[jax.ShapeDtypeStruct((span, width), F32)]
        + [jax.ShapeDtypeStruct((rows, width), BF) for rows in cuts] * (chips - 1),
        compiler_params=pltpu.CompilerParams(vmem_limit_bytes=VMEM_LIMIT),
        cost_estimate=BRIEF,
        name="fold",
    )(near, far)


def merge_kernel(count, own_ref, low_ref, *refs):
    backs, lows, outs = refs[:count], refs[count : 2 * count], refs[2 * count :]
    rows = outs[0].shape[0]
    block = low_ref.shape[1]
    offset = pl.multiple_of(lax.axis_index("mp") * block, 128)
    low = low_ref[...]
    for ref in lows:
        low += ref[...].astype(F32)
    total = own_ref[rows:]
    part = own_ref[:, pl.ds(offset, block)] + low
    after_own = part[rows:]
    for ref in backs:
        total += ref[...].astype(F32)
        after_own += ref[:, pl.ds(offset, block)].astype(F32)
    outs[0][...] = own_ref[:rows]
    outs[0][:, pl.ds(offset, block)] = part[:rows]
    for k in range(1, len(outs)):
        span = slice((k - 1) * rows, k * rows)
        outs[k][...] = total[span].astype(BF)
        outs[k][:, pl.ds(offset, block)] = after_own[span].astype(BF)


def merge(own, low, backs, lows, rows):
    total, width = own.shape
    return pl.pallas_call(
        functools.partial(merge_kernel, len(backs)),
        out_shape=[jax.ShapeDtypeStruct((rows, width), F32)]
        + [jax.ShapeDtypeStruct((rows, width), BF)] * (total // rows - 1),
        compiler_params=pltpu.CompilerParams(vmem_limit_bytes=VMEM_LIMIT),
        cost_estimate=BRIEF,
        name="merge",
    )(own, low, *backs, *lows)


def local(
    tokens,
    routes,
    probs,
    w_gate,
    w_up,
    w_down,
    gate_left,
    gate_right,
    up_left,
    up_right,
    down_left,
    down_right,
):
    rows, width = tokens.shape
    exp_dev, _, cols = w_gate.shape
    rank = gate_left.shape[1]
    block = gate_left.shape[2]
    parts = lax.axis_size("mp")
    chips = lax.axis_size("y")
    experts = exp_dev * chips * 2
    ranks = exp_dev * rank
    hid = exp_dev * cols

    def along_z(value, step):
        return lax.ppermute(value, "mp", [(i, (i + step) % parts) for i in range(parts)])

    def along_y(value, step):
        return lax.ppermute(value, "y", [(i, (i + step) % chips) for i in range(chips)])

    def other_core(value):
        return lax.ppermute(value, "core", [(0, 1), (1, 0)])

    pair = 2 * (-(-experts // 64) * 64)
    sent = attach(tokens, routes, probs, pair)
    arrived = [along_z(sent, k) for k in range(1, parts)]
    first = [along_y(sent, s) for s in range(1, chips)]
    gate_w, up_w = (jnp.swapaxes(w, 1, 2).reshape(hid, width) for w in (w_gate, w_up))
    gate_w, left, *small = prepare(
        (gate_right, up_right, down_left), (gate_left, up_left), gate_w, parts
    )
    rest = after(jnp.concatenate(arrived), (left, small, gate_w))
    up_w = load(after(up_w, rest))
    lines = [jnp.concatenate([sent, rest])]
    partner = [other_core(lines[0])]
    small = after(tuple(small), rest)
    small = [small[0]] + [along_z(small[k], k) for k in range(1, parts)]
    right = after(down_right.reshape(ranks, block), rest)
    partner_right = other_core(right)
    for s in range(1, chips):
        line = jnp.concatenate([first[s - 1], along_y(rest, s)])
        line = after(line, (tuple(small), partner_right, up_w))
        lines.append(line)
        partner.append(other_core(line))
    lines += partner
    diag = spread(small, parts, exp_dev)

    lines = after(tuple(lines), diag)
    inner = inner_products(lines, left, parts, rows)
    inner = [inner[0]] + [along_z(inner[k], k) for k in range(1, parts)]
    raw = raw_products(lines, gate_w, up_w)
    hidden, near, far = hidden_units(
        lines, inner, raw, diag, parts, exp_dev, pair
    )
    swapped = other_core(far)
    bottom = turn(near, swapped, parts, rows)
    bottom = [bottom[0]] + [along_z(bottom[k], k) for k in range(1, parts)]

    near, far = down_products(hidden, w_down.reshape(hid, width))
    out, *others = fold(near, other_core(after(far, swapped)), chips, rows)
    backs = [along_y(others[2 * s - 1], -s) for s in range(1, chips)]

    low, *lows = extra_products(right, partner_right, bottom, chips)
    lows = [along_y(lows[s - 1], -s) for s in range(1, chips)]

    heads = [along_y(after(others[2 * s - 2], low), -s) for s in range(1, chips)]
    result, *pieces = merge(out, low, backs, lows, rows)
    for piece in heads:
        result += piece.astype(F32)
    for k in range(1, parts):
        result += along_z(pieces[k - 1], -k).astype(F32)
    return result.astype(BF)


def solution(mesh):
    count = mesh.shape
    fine = jax.sharding.Mesh(
        mesh.devices.reshape(count["groups"], count["expert"] // 2, 2, count["mp"]),
        ("groups", "y", "core", "mp"),
    )
    expert = ("y", "core")
    return jax.shard_map(
        local,
        mesh=fine,
        in_specs=(
            P(("groups", "y", "core", "mp"), None),
            P(("groups", "y", "core", "mp"), None),
            P(("groups", "y", "core", "mp"), None),
            P(expert, None, "mp"),
            P(expert, None, "mp"),
            P(expert, "mp", None),
            P(expert, None, "mp"),
            P(expert, "mp", None),
            P(expert, None, "mp"),
            P(expert, "mp", None),
            P(expert, "mp", None),
            P(expert, None, "mp"),
        ),
        out_specs=P(("groups", "y", "core", "mp"), None),
        check_vma=False,
    )
```

```python
import functools

import jax
import jax.numpy as jnp
from jax import lax
from jax.experimental import pallas as pl
from jax.experimental.pallas import tpu as pltpu
from jax.sharding import PartitionSpec as P

BF = jnp.bfloat16
F32 = jnp.float32
SMALL_LIMIT = 4 * 1024 * 1024
VMEM_LIMIT = 12 * 1024 * 1024
PIECES = 8
BRIEF = pl.CostEstimate(flops=1, bytes_accessed=1, transcendentals=0)


def dot_nt(a, b):
    return lax.dot_general(a, b, (((1,), (1,)), ((), ())), preferred_element_type=F32)


def dot_nn(a, b):
    return lax.dot_general(a, b, (((1,), (0,)), ((), ())), preferred_element_type=F32)


def in_hbm(*values):
    return [pltpu.with_memory_space_constraint(v, pltpu.HBM) for v in values]


def after(value, earlier):
    return lax.optimization_barrier((value, earlier))[0]


def rotated(value, rows, parts, step):
    if step == 0:
        return value
    span = rows * parts
    lines = []
    for start in range(0, value.shape[0], span):
        cut = start + span - step * rows
        lines += [value[cut : start + span], value[start:cut]]
    return jnp.concatenate(lines)


def attach_kernel(tokens_ref, routes_ref, probs_ref, out_ref):
    rows, width = tokens_ref.shape
    pair = out_ref.shape[1] - width
    out_ref[:, :width] = tokens_ref[...]
    routes = routes_ref[...]
    probs = probs_ref[...]
    lane = lax.broadcasted_iota(jnp.int32, (rows, pair), 1)
    ids = jnp.where(lane < pair // 2, lane, lane - pair // 2)
    weight = jnp.zeros((rows, pair), F32)
    for k in range(routes.shape[1]):
        weight += jnp.where(ids == routes[:, k : k + 1], probs[:, k : k + 1], 0.0)
    high = weight.astype(BF).astype(F32)
    out_ref[:, width:] = jnp.where(lane < pair // 2, high, weight - high).astype(BF)


def attach(tokens, routes, probs, pair):
    rows, width = tokens.shape
    return pl.pallas_call(
        attach_kernel,
        out_shape=jax.ShapeDtypeStruct((rows, width + pair), BF),
        compiler_params=pltpu.CompilerParams(vmem_limit_bytes=SMALL_LIMIT),
        cost_estimate=BRIEF,
        name="attach",
    )(*in_hbm(tokens, routes, probs))


def piece_copies(source, target, sems):
    step = source.shape[0] // PIECES
    spans = [pl.ds(i * step, step) for i in range(PIECES)]
    return [
        pltpu.make_async_copy(source.at[span], target.at[span], sems.at[i])
        for i, span in enumerate(spans)
    ]


def load_kernel(source, target, sems):
    copies = piece_copies(source, target, sems)
    for copy in copies:
        copy.start()
    for copy in copies:
        copy.wait()


def load(weights):
    return pl.pallas_call(
        load_kernel,
        in_specs=[pl.BlockSpec(memory_space=pltpu.HBM)],
        out_specs=pl.BlockSpec(memory_space=pltpu.VMEM),
        out_shape=pltpu.VMEM(weights.shape, weights.dtype),
        scratch_shapes=[pltpu.SemaphoreType.DMA((PIECES,))],
        compiler_params=pltpu.CompilerParams(vmem_limit_bytes=SMALL_LIMIT),
        cost_estimate=BRIEF,
        name="load",
    )(*in_hbm(weights))


def prepare_kernel(parts, *refs):
    ins, lefts, source = refs[:3], refs[3:5], refs[5]
    target, left_ref, outs, sems = refs[6], refs[7], refs[8:-1], refs[-1]
    copies = piece_copies(source, target, sems)
    for copy in copies:
        copy.start()
    half = left_ref.shape[0] // 2
    for n, ref in enumerate(lefts):
        left_ref[n * half : (n + 1) * half] = ref[...].reshape(half, left_ref.shape[1])
    exp_dev, piece, hid = ins[0].shape
    cols = hid // parts
    me = lax.axis_index("mp")
    for n, ref in enumerate(ins):
        value = ref[...].reshape(exp_dev * piece, hid).astype(F32)
        blocks = [value[:, j * cols : (j + 1) * cols] for j in range(parts)]
        for k in range(parts):
            device = lax.rem(me + k, parts)
            block = blocks[0]
            for j in range(1, parts):
                block = jnp.where(device == j, blocks[j], block)
            outs[k][n] = block.astype(BF)
    for copy in copies:
        copy.wait()


def prepare(factors, lefts, weights, parts):
    exp_dev, piece, hid = factors[0].shape
    _, rank, block = lefts[0].shape
    vmem = pl.BlockSpec(memory_space=pltpu.VMEM)
    return pl.pallas_call(
        functools.partial(prepare_kernel, parts),
        in_specs=[vmem] * 5 + [pl.BlockSpec(memory_space=pltpu.HBM)],
        out_specs=[vmem] * (2 + parts),
        out_shape=[pltpu.VMEM(weights.shape, weights.dtype)]
        + [jax.ShapeDtypeStruct((2 * exp_dev * rank, block), BF)]
        + [jax.ShapeDtypeStruct((3, exp_dev * piece, hid // parts), BF)] * parts,
        scratch_shapes=[pltpu.SemaphoreType.DMA((PIECES,))],
        compiler_params=pltpu.CompilerParams(vmem_limit_bytes=SMALL_LIMIT),
        cost_estimate=BRIEF,
        name="prepare",
    )(*in_hbm(*factors, *lefts, weights))


def spread_kernel(parts, exp_dev, *refs):
    pieces, out_ref = refs[:-1], refs[-1]
    _, ranks, hid = out_ref.shape
    rank = ranks // exp_dev
    piece = rank // parts
    me = lax.axis_index("mp")
    row = lax.broadcasted_iota(jnp.int32, (ranks, ranks), 0)
    col = lax.broadcasted_iota(jnp.int32, (ranks, ranks), 1)
    step = lax.rem(me - row % rank // piece + parts, parts)
    source = (step * exp_dev + row // rank) * piece + row % piece
    order = (col == source).astype(F32).astype(BF)
    cols = hid // exp_dev
    place = lax.broadcasted_iota(jnp.int32, (ranks, hid), 1)
    place -= lax.broadcasted_iota(jnp.int32, (ranks, hid), 0) // rank * cols
    own = (place >= 0) & (place < cols)
    for n in range(3):
        value = dot_nn(order, jnp.concatenate([p[n].astype(F32) for p in pieces]).astype(BF))
        value = jnp.concatenate([value] * exp_dev, axis=1)
        out_ref[n] = jnp.where(own, value, 0.0).astype(BF)


def spread(pieces, parts, exp_dev):
    _, span, cols = pieces[0].shape
    return pl.pallas_call(
        functools.partial(spread_kernel, parts, exp_dev),
        out_shape=jax.ShapeDtypeStruct((3, span * parts, cols * exp_dev), BF),
        compiler_params=pltpu.CompilerParams(vmem_limit_bytes=SMALL_LIMIT),
        cost_estimate=BRIEF,
        name="spread",
    )(*pieces)


def inner_kernel(parts, rows, count, *refs):
    lines, left_ref, outs = refs[:count], refs[count], refs[count + 1 :]
    block = left_ref.shape[1]
    offset = pl.multiple_of(lax.axis_index("mp") * block, 128)
    x = jnp.concatenate([line[:, pl.ds(offset, block)] for line in lines])
    value = dot_nt(x, left_ref[...])
    for k in range(parts):
        outs[k][...] = rotated(value, rows, parts, k).astype(BF)


def inner_products(lines, left, parts, rows):
    total = sum(line.shape[0] for line in lines)
    ranks = left.shape[0]
    return pl.pallas_call(
        functools.partial(inner_kernel, parts, rows, len(lines)),
        out_shape=[jax.ShapeDtypeStruct((total, ranks), BF)] * parts,
        compiler_params=pltpu.CompilerParams(vmem_limit_bytes=VMEM_LIMIT),
        cost_estimate=BRIEF,
        name="inner",
    )(*lines, left)


def raw_kernel(count, tile, *refs):
    lines, (gate_w, up_w, gate_ref, up_ref) = refs[:count], refs[count:]
    hid, width = gate_w.shape
    x = jnp.concatenate([line[:, :width] for line in lines])
    for i in range(hid // tile):
        span = pl.ds(i * tile, tile)
        gate_ref[:, span] = dot_nt(x, gate_w[span])
        up_ref[:, span] = dot_nt(x, up_w[span])


def raw_products(lines, gate_w, up_w):
    hid = gate_w.shape[0]
    total = sum(line.shape[0] for line in lines)
    tile = 256 if hid % 256 == 0 else 128
    return pl.pallas_call(
        functools.partial(raw_kernel, len(lines), tile),
        out_shape=[jax.ShapeDtypeStruct((total, hid), F32)] * 2,
        compiler_params=pltpu.CompilerParams(vmem_limit_bytes=VMEM_LIMIT),
        cost_estimate=BRIEF,
        name="raw",
    )(*lines, gate_w, up_w)


def hidden_kernel(parts, count, exp_dev, pair, *refs):
    lines, inner, rest = refs[:count], refs[count : count + parts], refs[count + parts :]
    gate_ref, up_ref, diag_ref, hidden_ref, near_ref, far_ref = rest
    hid = gate_ref.shape[1]
    ranks = diag_ref.shape[1]
    wide = lines[0].shape[1] - pair
    total = sum(ref[...].astype(F32) for ref in inner).astype(BF)
    gate = gate_ref[...] + dot_nn(total[:, :ranks], diag_ref[0])
    up = up_ref[...] + dot_nn(total[:, ranks:], diag_ref[1])
    lane = lax.broadcasted_iota(jnp.int32, (pair, hid), 0)
    lane = jnp.where(lane < pair // 2, lane, lane - pair // 2)
    cols = hid // exp_dev
    first = (lax.axis_index("y") * 2 + lax.axis_index("core")) * exp_dev
    place = lax.broadcasted_iota(jnp.int32, (pair, hid), 1) - (lane - first) * cols
    pick = ((place >= 0) & (place < cols)).astype(F32).astype(BF)
    scale = dot_nn(jnp.concatenate([line[:, wide:] for line in lines]), pick)
    hidden = (gate / (1.0 + jnp.exp(-gate)) * up * scale).astype(BF)
    hidden_ref[...] = hidden
    value = dot_nt(hidden, diag_ref[2])
    near = near_ref.shape[0]
    near_ref[...] = value[:near].astype(BF)
    far_ref[...] = value[near:].astype(BF)


def hidden_units(lines, inner, raw, diag, parts, exp_dev, pair):
    total, hid = raw[0].shape
    ranks = diag.shape[1]
    return pl.pallas_call(
        functools.partial(hidden_kernel, parts, len(lines), exp_dev, pair),
        out_shape=[jax.ShapeDtypeStruct((total, hid), BF)]
        + [jax.ShapeDtypeStruct((total // 2, ranks), BF)] * 2,
        compiler_params=pltpu.CompilerParams(vmem_limit_bytes=VMEM_LIMIT),
        cost_estimate=BRIEF,
        name="hidden",
    )(*lines, *inner, *raw, diag)


def down_kernel(hidden_ref, down_ref, near_ref, far_ref):
    near, width = near_ref.shape
    hidden = hidden_ref[...]
    tile = min(1024, width)
    for i in range(width // tile):
        span = slice(i * tile, (i + 1) * tile)
        value = dot_nn(hidden, down_ref[:, span])
        near_ref[:, span] = value[:near]
        far_ref[:, span] = value[near:].astype(BF)


def down_products(hidden, down_w):
    total, width = hidden.shape[0], down_w.shape[1]
    return pl.pallas_call(
        down_kernel,
        out_shape=[
            jax.ShapeDtypeStruct((total // 2, width), F32),
            jax.ShapeDtypeStruct((total // 2, width), BF),
        ],
        compiler_params=pltpu.CompilerParams(vmem_limit_bytes=VMEM_LIMIT),
        cost_estimate=BRIEF,
        name="down",
    )(hidden, down_w)


def pair_kernel(near_ref, far_ref, *out_refs):
    value = jnp.concatenate([near_ref[...].astype(F32), far_ref[...].astype(F32)], axis=1)
    span = out_refs[0].shape[0]
    for n, out_ref in enumerate(out_refs):
        out_ref[...] = value[n * span : (n + 1) * span].astype(BF)


def side_by_side(near, far, chips):
    total, ranks = near.shape
    return pl.pallas_call(
        pair_kernel,
        out_shape=[jax.ShapeDtypeStruct((total // chips, 2 * ranks), BF)] * chips,
        compiler_params=pltpu.CompilerParams(vmem_limit_bytes=SMALL_LIMIT),
        cost_estimate=BRIEF,
        name="pair",
    )(near, far)


def turn_kernel(rows, chips, *refs):
    ins, outs = refs[:chips], refs[chips:]
    value = jnp.concatenate([ref[...].astype(F32) for ref in ins], axis=1)
    for k, out_ref in enumerate(outs):
        out_ref[...] = rotated(value, rows, len(outs), k).astype(BF)


def turn(lines, parts, rows):
    span, ranks = lines[0].shape
    return pl.pallas_call(
        functools.partial(turn_kernel, rows, len(lines)),
        out_shape=[jax.ShapeDtypeStruct((span, len(lines) * ranks), BF)] * parts,
        compiler_params=pltpu.CompilerParams(vmem_limit_bytes=SMALL_LIMIT),
        cost_estimate=BRIEF,
        name="turn",
    )(*lines)


def add_up_kernel(*refs):
    refs[-1][...] = sum(ref[...].astype(F32) for ref in refs[:-1]).astype(BF)


def add_up(pieces):
    return pl.pallas_call(
        add_up_kernel,
        out_shape=jax.ShapeDtypeStruct(pieces[0].shape, BF),
        compiler_params=pltpu.CompilerParams(vmem_limit_bytes=SMALL_LIMIT),
        cost_estimate=BRIEF,
        name="add_up",
    )(*pieces)


def fold_kernel(head, near_ref, far_ref, own_ref, *out_refs):
    span = own_ref.shape[0]
    total = near_ref[...] + far_ref[...].astype(F32)
    own_ref[...] = total[:span]
    for n in range(len(out_refs) // 2):
        line = total[(n + 1) * span : (n + 2) * span]
        out_refs[2 * n][...] = line[:head].astype(BF)
        out_refs[2 * n + 1][...] = line[head:].astype(BF)


def fold(near, far, chips, head):
    total, width = near.shape
    span = total // chips
    cuts = [head, span - head]
    return pl.pallas_call(
        functools.partial(fold_kernel, head),
        out_shape=[jax.ShapeDtypeStruct((span, width), F32)]
        + [jax.ShapeDtypeStruct((rows, width), BF) for rows in cuts] * (chips - 1),
        compiler_params=pltpu.CompilerParams(vmem_limit_bytes=VMEM_LIMIT),
        cost_estimate=BRIEF,
        name="fold",
    )(near, far)


def merge_kernel(chips, parts, *refs):
    own_ref, rights, refs = refs[0], refs[1 : 1 + 2 * chips], refs[1 + 2 * chips :]
    low, backs, outs = refs[0][...], refs[1:-parts], refs[-parts:]
    rows = outs[0].shape[0]
    ranks, block = rights[0].shape
    offset = pl.multiple_of(lax.axis_index("mp") * block, 128)
    value = jnp.zeros((low.shape[0], block), F32)
    for n, ref in enumerate(rights):
        at = (2 * n if n < chips else 2 * (n - chips) + 1) * ranks
        value += dot_nn(low[:, at : at + ranks], ref[...])
    total = own_ref[rows:]
    value += own_ref[:, pl.ds(offset, block)]
    rest = value[rows:]
    for ref in backs:
        total += ref[...].astype(F32)
        rest += ref[:, pl.ds(offset, block)].astype(F32)
    outs[0][...] = own_ref[:rows]
    outs[0][:, pl.ds(offset, block)] = value[:rows]
    for k in range(1, parts):
        span = slice((k - 1) * rows, k * rows)
        outs[k][...] = total[span].astype(BF)
        outs[k][:, pl.ds(offset, block)] = rest[span].astype(BF)


def merge(own, rights, low, backs, rows):
    total, width = own.shape
    parts = total // rows
    return pl.pallas_call(
        functools.partial(merge_kernel, len(backs) + 1, parts),
        out_shape=[jax.ShapeDtypeStruct((rows, width), F32)]
        + [jax.ShapeDtypeStruct((rows, width), BF)] * (parts - 1),
        compiler_params=pltpu.CompilerParams(vmem_limit_bytes=VMEM_LIMIT),
        cost_estimate=BRIEF,
        name="merge",
    )(own, *rights, low, *backs)


def local(
    tokens,
    routes,
    probs,
    w_gate,
    w_up,
    w_down,
    gate_left,
    gate_right,
    up_left,
    up_right,
    down_left,
    down_right,
):
    rows, width = tokens.shape
    exp_dev, _, cols = w_gate.shape
    rank = gate_left.shape[1]
    block = gate_left.shape[2]
    parts = lax.axis_size("mp")
    chips = lax.axis_size("y")
    experts = exp_dev * chips * 2
    ranks = exp_dev * rank
    hid = exp_dev * cols

    def along_z(value, step):
        return lax.ppermute(value, "mp", [(i, (i + step) % parts) for i in range(parts)])

    def along_y(value, step):
        return lax.ppermute(value, "y", [(i, (i + step) % chips) for i in range(chips)])

    def other_core(value):
        return lax.ppermute(value, "core", [(0, 1), (1, 0)])

    pair = 2 * (-(-experts // 64) * 64)
    sent = attach(tokens, routes, probs, pair)
    arrived = [along_z(sent, k) for k in range(1, parts)]
    first = [along_y(sent, s) for s in range(1, chips)]
    gate_w, up_w = (jnp.swapaxes(w, 1, 2).reshape(hid, width) for w in (w_gate, w_up))
    gate_w, left, *small = prepare(
        (gate_right, up_right, down_left), (gate_left, up_left), gate_w, parts
    )
    right = down_right.reshape(ranks, block)
    partner_right = other_core(right)
    rest = after(jnp.concatenate(arrived), (left, small, gate_w, partner_right))
    up_w = load(after(up_w, rest))
    lines = [jnp.concatenate([sent, rest])]
    partner = [other_core(lines[0])]
    small = after(tuple(small), rest)
    small = [small[0]] + [along_z(small[k], k) for k in range(1, parts)]
    for s in range(1, chips):
        line = jnp.concatenate([first[s - 1], along_y(rest, s)])
        arrival = line
        line = after(line, (tuple(small), up_w))
        lines.append(line)
        partner.append(other_core(line))
    lines += partner
    diag = spread(small, parts, exp_dev)

    lines = after(tuple(lines), diag)
    inner = inner_products(lines, left, parts, rows)
    inner = [inner[0]] + [along_z(inner[k], k) for k in range(1, parts)]
    raw = raw_products(lines, gate_w, up_w)
    right = after(right, arrival)
    rights = [right] + [along_y(right, -s) for s in range(1, chips)]
    raw = after(tuple(raw), rights[1:])
    hidden, near, far = hidden_units(
        lines, inner, raw, diag, parts, exp_dev, pair
    )
    swapped = other_core(far)
    low, *lows = side_by_side(near, swapped, chips)
    lows = [along_y(lows[s - 1], -s) for s in range(1, chips)]
    bottom = turn([low] + lows, parts, rows)
    bottom = [bottom[0]] + [along_z(bottom[k], k) for k in range(1, parts)]

    near, far = down_products(hidden, w_down.reshape(hid, width))
    far = after(other_core(after(far, swapped)), lows)
    out, *others = fold(near, far, chips, rows)
    backs = [along_y(others[2 * s - 1], -s) for s in range(1, chips)]
    rights += [partner_right] + [other_core(after(right, bottom[0])) for right in rights[1:]]
    own, *pieces = merge(out, rights, add_up(bottom[1:] + bottom[:1]), backs, rows)
    heads = [along_y(after(others[2 * s - 2], own), -s) for s in range(1, chips)]
    result = own
    for piece in heads:
        result += piece.astype(F32)
    for k in range(1, parts):
        result += along_z(pieces[k - 1], -k).astype(F32)
    return result.astype(BF)


def solution(mesh):
    count = mesh.shape
    fine = jax.sharding.Mesh(
        mesh.devices.reshape(count["groups"], count["expert"] // 2, 2, count["mp"]),
        ("groups", "y", "core", "mp"),
    )
    expert = ("y", "core")
    return jax.shard_map(
        local,
        mesh=fine,
        in_specs=(
            P(("groups", "y", "core", "mp"), None),
            P(("groups", "y", "core", "mp"), None),
            P(("groups", "y", "core", "mp"), None),
            P(expert, None, "mp"),
            P(expert, None, "mp"),
            P(expert, "mp", None),
            P(expert, None, "mp"),
            P(expert, "mp", None),
            P(expert, None, "mp"),
            P(expert, "mp", None),
            P(expert, "mp", None),
            P(expert, None, "mp"),
        ),
        out_specs=P(("groups", "y", "core", "mp"), None),
        check_vma=False,
    )
```

```python
import functools

import jax
import jax.numpy as jnp
from jax import lax
from jax.experimental import pallas as pl
from jax.experimental.pallas import tpu as pltpu
from jax.sharding import PartitionSpec as P

BF = jnp.bfloat16
F32 = jnp.float32
SMALL_LIMIT = 4 * 1024 * 1024
VMEM_LIMIT = 12 * 1024 * 1024
PIECES = 8
BRIEF = pl.CostEstimate(flops=1, bytes_accessed=1, transcendentals=0)


def dot_nt(a, b):
    return lax.dot_general(a, b, (((1,), (1,)), ((), ())), preferred_element_type=F32)


def dot_nn(a, b):
    return lax.dot_general(a, b, (((1,), (0,)), ((), ())), preferred_element_type=F32)


def in_hbm(*values):
    return [pltpu.with_memory_space_constraint(v, pltpu.HBM) for v in values]


def after(value, earlier):
    return lax.optimization_barrier((value, earlier))[0]


def rotated(value, rows, parts, step):
    if step == 0:
        return value
    span = rows * parts
    lines = []
    for start in range(0, value.shape[0], span):
        cut = start + span - step * rows
        lines += [value[cut : start + span], value[start:cut]]
    return jnp.concatenate(lines)


def attach_kernel(tokens_ref, routes_ref, probs_ref, out_ref):
    rows, width = tokens_ref.shape
    pair = out_ref.shape[1] - width
    out_ref[:, :width] = tokens_ref[...]
    routes = routes_ref[...]
    probs = probs_ref[...]
    lane = lax.broadcasted_iota(jnp.int32, (rows, pair), 1)
    ids = jnp.where(lane < pair // 2, lane, lane - pair // 2)
    weight = jnp.zeros((rows, pair), F32)
    for k in range(routes.shape[1]):
        weight += jnp.where(ids == routes[:, k : k + 1], probs[:, k : k + 1], 0.0)
    high = weight.astype(BF).astype(F32)
    out_ref[:, width:] = jnp.where(lane < pair // 2, high, weight - high).astype(BF)


def attach(tokens, routes, probs, pair):
    rows, width = tokens.shape
    return pl.pallas_call(
        attach_kernel,
        out_shape=jax.ShapeDtypeStruct((rows, width + pair), BF),
        compiler_params=pltpu.CompilerParams(vmem_limit_bytes=SMALL_LIMIT),
        cost_estimate=BRIEF,
        name="attach",
    )(*in_hbm(tokens, routes, probs))


def piece_copies(source, target, sems):
    step = source.shape[0] // PIECES
    spans = [pl.ds(i * step, step) for i in range(PIECES)]
    return [
        pltpu.make_async_copy(source.at[span], target.at[span], sems.at[i])
        for i, span in enumerate(spans)
    ]


def load_kernel(source, target, sems):
    copies = piece_copies(source, target, sems)
    for copy in copies:
        copy.start()
    for copy in copies:
        copy.wait()


def load(weights):
    return pl.pallas_call(
        load_kernel,
        in_specs=[pl.BlockSpec(memory_space=pltpu.HBM)],
        out_specs=pl.BlockSpec(memory_space=pltpu.VMEM),
        out_shape=pltpu.VMEM(weights.shape, weights.dtype),
        scratch_shapes=[pltpu.SemaphoreType.DMA((PIECES,))],
        compiler_params=pltpu.CompilerParams(vmem_limit_bytes=SMALL_LIMIT),
        cost_estimate=BRIEF,
        name="load",
    )(*in_hbm(weights))


def prepare_kernel(parts, *refs):
    ins, lefts, source = refs[:3], refs[3:5], refs[5]
    target, left_ref, outs, sems = refs[6], refs[7], refs[8:-1], refs[-1]
    copies = piece_copies(source, target, sems)
    for copy in copies:
        copy.start()
    half = left_ref.shape[0] // 2
    for n, ref in enumerate(lefts):
        left_ref[n * half : (n + 1) * half] = ref[...].reshape(half, left_ref.shape[1])
    exp_dev, piece, hid = ins[0].shape
    cols = hid // parts
    me = lax.axis_index("mp")
    for n, ref in enumerate(ins):
        value = ref[...].reshape(exp_dev * piece, hid).astype(F32)
        blocks = [value[:, j * cols : (j + 1) * cols] for j in range(parts)]
        for k in range(parts):
            device = lax.rem(me + k, parts)
            block = blocks[0]
            for j in range(1, parts):
                block = jnp.where(device == j, blocks[j], block)
            outs[k][n] = block.astype(BF)
    for copy in copies:
        copy.wait()


def prepare(factors, lefts, weights, parts):
    exp_dev, piece, hid = factors[0].shape
    _, rank, block = lefts[0].shape
    vmem = pl.BlockSpec(memory_space=pltpu.VMEM)
    return pl.pallas_call(
        functools.partial(prepare_kernel, parts),
        in_specs=[vmem] * 5 + [pl.BlockSpec(memory_space=pltpu.HBM)],
        out_specs=[vmem] * (2 + parts),
        out_shape=[pltpu.VMEM(weights.shape, weights.dtype)]
        + [jax.ShapeDtypeStruct((2 * exp_dev * rank, block), BF)]
        + [jax.ShapeDtypeStruct((3, exp_dev * piece, hid // parts), BF)] * parts,
        scratch_shapes=[pltpu.SemaphoreType.DMA((PIECES,))],
        compiler_params=pltpu.CompilerParams(vmem_limit_bytes=SMALL_LIMIT),
        cost_estimate=BRIEF,
        name="prepare",
    )(*in_hbm(*factors, *lefts, weights))


def spread_kernel(parts, exp_dev, *refs):
    pieces, out_ref = refs[:-1], refs[-1]
    _, ranks, hid = out_ref.shape
    rank = ranks // exp_dev
    piece = rank // parts
    me = lax.axis_index("mp")
    row = lax.broadcasted_iota(jnp.int32, (ranks, ranks), 0)
    col = lax.broadcasted_iota(jnp.int32, (ranks, ranks), 1)
    step = lax.rem(me - row % rank // piece + parts, parts)
    source = (step * exp_dev + row // rank) * piece + row % piece
    order = (col == source).astype(F32).astype(BF)
    cols = hid // exp_dev
    place = lax.broadcasted_iota(jnp.int32, (ranks, hid), 1)
    place -= lax.broadcasted_iota(jnp.int32, (ranks, hid), 0) // rank * cols
    own = (place >= 0) & (place < cols)
    for n in range(3):
        value = dot_nn(order, jnp.concatenate([p[n].astype(F32) for p in pieces]).astype(BF))
        value = jnp.concatenate([value] * exp_dev, axis=1)
        out_ref[n] = jnp.where(own, value, 0.0).astype(BF)


def spread(pieces, parts, exp_dev):
    _, span, cols = pieces[0].shape
    return pl.pallas_call(
        functools.partial(spread_kernel, parts, exp_dev),
        out_shape=jax.ShapeDtypeStruct((3, span * parts, cols * exp_dev), BF),
        compiler_params=pltpu.CompilerParams(vmem_limit_bytes=SMALL_LIMIT),
        cost_estimate=BRIEF,
        name="spread",
    )(*pieces)


def inner_kernel(parts, rows, count, *refs):
    lines, left_ref, outs = refs[:count], refs[count], refs[count + 1 :]
    block = left_ref.shape[1]
    offset = pl.multiple_of(lax.axis_index("mp") * block, 128)
    x = jnp.concatenate([line[:, pl.ds(offset, block)] for line in lines])
    value = dot_nt(x, left_ref[...])
    for k in range(parts):
        outs[k][...] = rotated(value, rows, parts, k).astype(BF)


def inner_products(lines, left, parts, rows):
    total = sum(line.shape[0] for line in lines)
    ranks = left.shape[0]
    return pl.pallas_call(
        functools.partial(inner_kernel, parts, rows, len(lines)),
        out_shape=[jax.ShapeDtypeStruct((total, ranks), BF)] * parts,
        compiler_params=pltpu.CompilerParams(vmem_limit_bytes=VMEM_LIMIT),
        cost_estimate=BRIEF,
        name="inner",
    )(*lines, left)


def raw_kernel(count, tile, *refs):
    lines, (gate_w, up_w, gate_ref, up_ref) = refs[:count], refs[count:]
    hid, width = gate_w.shape
    x = jnp.concatenate([line[:, :width] for line in lines])
    for i in range(hid // tile):
        span = pl.ds(i * tile, tile)
        gate_ref[:, span] = dot_nt(gate_w[span], x).T
        up_ref[:, span] = dot_nt(up_w[span], x).T


def raw_products(lines, gate_w, up_w):
    hid = gate_w.shape[0]
    total = sum(line.shape[0] for line in lines)
    tile = 384
    return pl.pallas_call(
        functools.partial(raw_kernel, len(lines), tile),
        out_shape=[jax.ShapeDtypeStruct((total, hid), F32)] * 2,
        compiler_params=pltpu.CompilerParams(vmem_limit_bytes=VMEM_LIMIT),
        cost_estimate=BRIEF,
        name="raw",
    )(*lines, gate_w, up_w)


def hidden_kernel(parts, count, exp_dev, pair, *refs):
    lines, inner, rest = refs[:count], refs[count : count + parts], refs[count + parts :]
    gate_ref, up_ref, diag_ref, hidden_ref, near_ref, far_ref = rest
    hid = gate_ref.shape[1]
    ranks = diag_ref.shape[1]
    wide = lines[0].shape[1] - pair
    total = sum(ref[...].astype(F32) for ref in inner).astype(BF)
    gate = gate_ref[...] + dot_nn(total[:, :ranks], diag_ref[0])
    up = up_ref[...] + dot_nn(total[:, ranks:], diag_ref[1])
    lane = lax.broadcasted_iota(jnp.int32, (pair, hid), 0)
    lane = jnp.where(lane < pair // 2, lane, lane - pair // 2)
    cols = hid // exp_dev
    first = (lax.axis_index("y") * 2 + lax.axis_index("core")) * exp_dev
    place = lax.broadcasted_iota(jnp.int32, (pair, hid), 1) - (lane - first) * cols
    pick = ((place >= 0) & (place < cols)).astype(F32).astype(BF)
    scale = dot_nn(jnp.concatenate([line[:, wide:] for line in lines]), pick)
    hidden = (gate / (1.0 + jnp.exp(-gate)) * up * scale).astype(BF)
    hidden_ref[...] = hidden
    value = dot_nt(hidden, diag_ref[2])
    near = near_ref.shape[0]
    near_ref[...] = value[:near].astype(BF)
    far_ref[...] = value[near:].astype(BF)


def hidden_units(lines, inner, raw, diag, parts, exp_dev, pair):
    total, hid = raw[0].shape
    ranks = diag.shape[1]
    return pl.pallas_call(
        functools.partial(hidden_kernel, parts, len(lines), exp_dev, pair),
        out_shape=[jax.ShapeDtypeStruct((total, hid), BF)]
        + [jax.ShapeDtypeStruct((total // 2, ranks), BF)] * 2,
        compiler_params=pltpu.CompilerParams(vmem_limit_bytes=VMEM_LIMIT),
        cost_estimate=BRIEF,
        name="hidden",
    )(*lines, *inner, *raw, diag)


def down_kernel(hidden_ref, down_ref, near_ref, far_ref):
    near, width = near_ref.shape
    hidden = hidden_ref[...]
    tile = min(1024, width)
    for i in range(width // tile):
        span = slice(i * tile, (i + 1) * tile)
        value = dot_nn(hidden, down_ref[:, span])
        near_ref[:, span] = value[:near]
        far_ref[:, span] = value[near:].astype(BF)


def down_products(hidden, down_w):
    total, width = hidden.shape[0], down_w.shape[1]
    return pl.pallas_call(
        down_kernel,
        out_shape=[
            jax.ShapeDtypeStruct((total // 2, width), F32),
            jax.ShapeDtypeStruct((total // 2, width), BF),
        ],
        compiler_params=pltpu.CompilerParams(vmem_limit_bytes=VMEM_LIMIT),
        cost_estimate=BRIEF,
        name="down",
    )(hidden, down_w)


def pair_kernel(near_ref, far_ref, *out_refs):
    value = jnp.concatenate([near_ref[...].astype(F32), far_ref[...].astype(F32)], axis=1)
    span = out_refs[0].shape[0]
    for n, out_ref in enumerate(out_refs):
        out_ref[...] = value[n * span : (n + 1) * span].astype(BF)


def side_by_side(near, far, chips):
    total, ranks = near.shape
    return pl.pallas_call(
        pair_kernel,
        out_shape=[jax.ShapeDtypeStruct((total // chips, 2 * ranks), BF)] * chips,
        compiler_params=pltpu.CompilerParams(vmem_limit_bytes=SMALL_LIMIT),
        cost_estimate=BRIEF,
        name="pair",
    )(near, far)


def turn_kernel(rows, chips, *refs):
    ins, outs = refs[:chips], refs[chips:]
    value = jnp.concatenate([ref[...].astype(F32) for ref in ins], axis=1)
    for k, out_ref in enumerate(outs):
        out_ref[...] = rotated(value, rows, len(outs), k).astype(BF)


def turn(lines, parts, rows):
    span, ranks = lines[0].shape
    return pl.pallas_call(
        functools.partial(turn_kernel, rows, len(lines)),
        out_shape=[jax.ShapeDtypeStruct((span, len(lines) * ranks), BF)] * parts,
        compiler_params=pltpu.CompilerParams(vmem_limit_bytes=SMALL_LIMIT),
        cost_estimate=BRIEF,
        name="turn",
    )(*lines)


def add_up_kernel(*refs):
    refs[-1][...] = sum(ref[...].astype(F32) for ref in refs[:-1]).astype(BF)


def add_up(pieces):
    return pl.pallas_call(
        add_up_kernel,
        out_shape=jax.ShapeDtypeStruct(pieces[0].shape, BF),
        compiler_params=pltpu.CompilerParams(vmem_limit_bytes=SMALL_LIMIT),
        cost_estimate=BRIEF,
        name="add_up",
    )(*pieces)


def fold_kernel(near_ref, far_ref, own_ref, *out_refs):
    span = own_ref.shape[0]
    total = near_ref[...] + far_ref[...].astype(F32)
    own_ref[...] = total[:span]
    for n, out_ref in enumerate(out_refs):
        out_ref[...] = total[(n + 1) * span : (n + 2) * span].astype(BF)


def fold(near, far, chips):
    total, width = near.shape
    span = total // chips
    return pl.pallas_call(
        fold_kernel,
        out_shape=[jax.ShapeDtypeStruct((span, width), F32)]
        + [jax.ShapeDtypeStruct((span, width), BF)] * (chips - 1),
        compiler_params=pltpu.CompilerParams(vmem_limit_bytes=VMEM_LIMIT),
        cost_estimate=BRIEF,
        name="fold",
    )(near, far)


def merge_kernel(chips, parts, *refs):
    own_ref, rights, refs = refs[0], refs[1 : 1 + 2 * chips], refs[1 + 2 * chips :]
    low, backs, outs = refs[0][...], refs[1:-parts], refs[-parts:]
    rows = outs[0].shape[0]
    ranks, block = rights[0].shape
    offset = pl.multiple_of(lax.axis_index("mp") * block, 128)
    value = jnp.zeros((low.shape[0], block), F32)
    for n, ref in enumerate(rights):
        at = (2 * n if n < chips else 2 * (n - chips) + 1) * ranks
        value += dot_nn(low[:, at : at + ranks], ref[...])
    total = own_ref[...]
    value += own_ref[:, pl.ds(offset, block)]
    for ref in backs:
        total += ref[...].astype(F32)
        value += ref[:, pl.ds(offset, block)].astype(F32)
    for k, out_ref in enumerate(outs):
        span = slice(k * rows, (k + 1) * rows)
        out_ref[...] = total[span].astype(out_ref.dtype)
        out_ref[:, pl.ds(offset, block)] = value[span].astype(out_ref.dtype)


def merge(own, rights, low, backs, rows):
    total, width = own.shape
    parts = total // rows
    return pl.pallas_call(
        functools.partial(merge_kernel, len(backs) + 1, parts),
        out_shape=[jax.ShapeDtypeStruct((rows, width), F32)]
        + [jax.ShapeDtypeStruct((rows, width), BF)] * (parts - 1),
        compiler_params=pltpu.CompilerParams(vmem_limit_bytes=VMEM_LIMIT),
        cost_estimate=BRIEF,
        name="merge",
    )(own, *rights, low, *backs)


def local(
    tokens,
    routes,
    probs,
    w_gate,
    w_up,
    w_down,
    gate_left,
    gate_right,
    up_left,
    up_right,
    down_left,
    down_right,
):
    rows, width = tokens.shape
    exp_dev, _, cols = w_gate.shape
    rank = gate_left.shape[1]
    block = gate_left.shape[2]
    parts = lax.axis_size("mp")
    chips = lax.axis_size("y")
    experts = exp_dev * chips * 2
    ranks = exp_dev * rank
    hid = exp_dev * cols

    def along_z(value, step):
        return lax.ppermute(value, "mp", [(i, (i + step) % parts) for i in range(parts)])

    def along_y(value, step):
        return lax.ppermute(value, "y", [(i, (i + step) % chips) for i in range(chips)])

    def other_core(value):
        return lax.ppermute(value, "core", [(0, 1), (1, 0)])

    pair = 2 * (-(-experts // 64) * 64)
    sent = attach(tokens, routes, probs, pair)
    arrived = [along_z(sent, k) for k in range(1, parts)]
    first = [along_y(sent, s) for s in range(1, chips)]
    gate_w, up_w = (jnp.swapaxes(w, 1, 2).reshape(hid, width) for w in (w_gate, w_up))
    gate_w, left, *small = prepare(
        (gate_right, up_right, down_left), (gate_left, up_left), gate_w, parts
    )
    right = down_right.reshape(ranks, block)
    partner_right = other_core(right)
    rest = after(jnp.concatenate(arrived), (left, small, gate_w, partner_right))
    up_w = load(after(up_w, rest))
    lines = [jnp.concatenate([sent, rest])]
    partner = [other_core(lines[0])]
    small = after(tuple(small), rest)
    small = [small[0]] + [along_z(small[k], k) for k in range(1, parts)]
    for s in range(1, chips):
        line = jnp.concatenate([first[s - 1], along_y(rest, s)])
        arrival = line
        line = after(line, (tuple(small), up_w))
        lines.append(line)
        partner.append(other_core(line))
    lines += partner
    diag = spread(small, parts, exp_dev)

    lines = after(tuple(lines), diag)
    inner = inner_products(lines, left, parts, rows)
    inner = [inner[0]] + [along_z(inner[k], k) for k in range(1, parts)]
    raw = raw_products(lines, gate_w, up_w)
    right = after(right, arrival)
    rights = [right] + [along_y(right, -s) for s in range(1, chips)]
    raw = after(tuple(raw), rights[1:])
    hidden, near, far = hidden_units(
        lines, inner, raw, diag, parts, exp_dev, pair
    )
    swapped = other_core(far)
    low, *lows = side_by_side(near, swapped, chips)
    lows = [along_y(lows[s - 1], -s) for s in range(1, chips)]
    bottom = turn([low] + lows, parts, rows)
    bottom = [bottom[0]] + [along_z(bottom[k], k) for k in range(1, parts)]

    near, far = down_products(hidden, w_down.reshape(hid, width))
    far = after(other_core(after(far, swapped)), lows)
    out, *others = fold(near, far, chips)
    backs = [along_y(others[s - 1], -s) for s in range(1, chips)]
    rights += [partner_right] + [other_core(after(right, bottom[0])) for right in rights[1:]]
    own, *pieces = merge(out, rights, add_up(bottom[1:] + bottom[:1]), backs, rows)
    result = own
    for k in range(1, parts):
        result += along_z(pieces[k - 1], -k).astype(F32)
    return result.astype(BF)


def solution(mesh):
    count = mesh.shape
    fine = jax.sharding.Mesh(
        mesh.devices.reshape(count["groups"], count["expert"] // 2, 2, count["mp"]),
        ("groups", "y", "core", "mp"),
    )
    expert = ("y", "core")
    return jax.shard_map(
        local,
        mesh=fine,
        in_specs=(
            P(("groups", "y", "core", "mp"), None),
            P(("groups", "y", "core", "mp"), None),
            P(("groups", "y", "core", "mp"), None),
            P(expert, None, "mp"),
            P(expert, None, "mp"),
            P(expert, "mp", None),
            P(expert, None, "mp"),
            P(expert, "mp", None),
            P(expert, None, "mp"),
            P(expert, "mp", None),
            P(expert, "mp", None),
            P(expert, None, "mp"),
        ),
        out_specs=P(("groups", "y", "core", "mp"), None),
        check_vma=False,
    )
```

```python
import functools

import jax
import jax.numpy as jnp
from jax import lax
from jax.experimental import pallas as pl
from jax.experimental.pallas import tpu as pltpu
from jax.sharding import PartitionSpec as P

BF = jnp.bfloat16
F32 = jnp.float32
SMALL_LIMIT = 4 * 1024 * 1024
VMEM_LIMIT = 12 * 1024 * 1024
PIECES = 8
LONG = pl.CostEstimate(flops=1_000_000_000, bytes_accessed=1, transcendentals=0)
LONGER = pl.CostEstimate(flops=10_000_000_000, bytes_accessed=1, transcendentals=0)
BRIEF = pl.CostEstimate(flops=1, bytes_accessed=1, transcendentals=0)


def dot_nt(a, b):
    return lax.dot_general(a, b, (((1,), (1,)), ((), ())), preferred_element_type=F32)


def dot_nn(a, b):
    return lax.dot_general(a, b, (((1,), (0,)), ((), ())), preferred_element_type=F32)


def in_hbm(*values):
    return [pltpu.with_memory_space_constraint(v, pltpu.HBM) for v in values]


def after(value, earlier):
    return lax.optimization_barrier((value, earlier))[0]


def rotated(value, rows, parts, step):
    if step == 0:
        return value
    span = rows * parts
    lines = []
    for start in range(0, value.shape[0], span):
        cut = start + span - step * rows
        lines += [value[cut : start + span], value[start:cut]]
    return jnp.concatenate(lines)


def attach_kernel(tokens_ref, routes_ref, probs_ref, out_ref):
    rows, width = tokens_ref.shape
    pair = out_ref.shape[1] - width
    out_ref[:, :width] = tokens_ref[...]
    routes = routes_ref[...]
    probs = probs_ref[...]
    lane = lax.broadcasted_iota(jnp.int32, (rows, pair), 1)
    ids = jnp.where(lane < pair // 2, lane, lane - pair // 2)
    weight = jnp.zeros((rows, pair), F32)
    for k in range(routes.shape[1]):
        weight += jnp.where(ids == routes[:, k : k + 1], probs[:, k : k + 1], 0.0)
    high = weight.astype(BF).astype(F32)
    out_ref[:, width:] = jnp.where(lane < pair // 2, high, weight - high).astype(BF)


def attach(tokens, routes, probs, pair):
    rows, width = tokens.shape
    return pl.pallas_call(
        attach_kernel,
        out_shape=jax.ShapeDtypeStruct((rows, width + pair), BF),
        compiler_params=pltpu.CompilerParams(vmem_limit_bytes=SMALL_LIMIT),
        cost_estimate=BRIEF,
        name="attach",
    )(*in_hbm(tokens, routes, probs))


def piece_copies(source, target, sems):
    step = source.shape[0] // PIECES
    spans = [pl.ds(i * step, step) for i in range(PIECES)]
    return [
        pltpu.make_async_copy(source.at[span], target.at[span], sems.at[i])
        for i, span in enumerate(spans)
    ]


def load_kernel(source, target, sems):
    copies = piece_copies(source, target, sems)
    for copy in copies:
        copy.start()
    for copy in copies:
        copy.wait()


def load(weights):
    return pl.pallas_call(
        load_kernel,
        in_specs=[pl.BlockSpec(memory_space=pltpu.HBM)],
        out_specs=pl.BlockSpec(memory_space=pltpu.VMEM),
        out_shape=pltpu.VMEM(weights.shape, weights.dtype),
        scratch_shapes=[pltpu.SemaphoreType.DMA((PIECES,))],
        compiler_params=pltpu.CompilerParams(vmem_limit_bytes=SMALL_LIMIT),
        cost_estimate=BRIEF,
        name="load",
    )(*in_hbm(weights))


def prepare_kernel(parts, *refs):
    ins, lefts, source = refs[:3], refs[3:5], refs[5]
    target, left_ref, outs, sems = refs[6], refs[7], refs[8:-1], refs[-1]
    copies = piece_copies(source, target, sems)
    for copy in copies:
        copy.start()
    half = left_ref.shape[0] // 2
    for n, ref in enumerate(lefts):
        left_ref[n * half : (n + 1) * half] = ref[...].reshape(half, left_ref.shape[1])
    exp_dev, piece, hid = ins[0].shape
    cols = hid // parts
    me = lax.axis_index("mp")
    for n, ref in enumerate(ins):
        value = ref[...].reshape(exp_dev * piece, hid).astype(F32)
        blocks = [value[:, j * cols : (j + 1) * cols] for j in range(parts)]
        for k in range(parts):
            device = lax.rem(me + k, parts)
            block = blocks[0]
            for j in range(1, parts):
                block = jnp.where(device == j, blocks[j], block)
            outs[k][n] = block.astype(BF)
    for copy in copies:
        copy.wait()


def prepare(factors, lefts, weights, parts):
    exp_dev, piece, hid = factors[0].shape
    _, rank, block = lefts[0].shape
    vmem = pl.BlockSpec(memory_space=pltpu.VMEM)
    return pl.pallas_call(
        functools.partial(prepare_kernel, parts),
        in_specs=[vmem] * 5 + [pl.BlockSpec(memory_space=pltpu.HBM)],
        out_specs=[vmem] * (2 + parts),
        out_shape=[pltpu.VMEM(weights.shape, weights.dtype)]
        + [jax.ShapeDtypeStruct((2 * exp_dev * rank, block), BF)]
        + [jax.ShapeDtypeStruct((3, exp_dev * piece, hid // parts), BF)] * parts,
        scratch_shapes=[pltpu.SemaphoreType.DMA((PIECES,))],
        compiler_params=pltpu.CompilerParams(vmem_limit_bytes=SMALL_LIMIT),
        cost_estimate=BRIEF,
        name="prepare",
    )(*in_hbm(*factors, *lefts, weights))


def spread_kernel(parts, exp_dev, *refs):
    pieces, out_ref = refs[:-1], refs[-1]
    _, ranks, hid = out_ref.shape
    rank = ranks // exp_dev
    piece = rank // parts
    me = lax.axis_index("mp")
    row = lax.broadcasted_iota(jnp.int32, (ranks, ranks), 0)
    col = lax.broadcasted_iota(jnp.int32, (ranks, ranks), 1)
    step = lax.rem(me - row % rank // piece + parts, parts)
    source = (step * exp_dev + row // rank) * piece + row % piece
    order = (col == source).astype(F32).astype(BF)
    cols = hid // exp_dev
    place = lax.broadcasted_iota(jnp.int32, (ranks, hid), 1)
    place -= lax.broadcasted_iota(jnp.int32, (ranks, hid), 0) // rank * cols
    own = (place >= 0) & (place < cols)
    for n in range(3):
        value = dot_nn(order, jnp.concatenate([p[n].astype(F32) for p in pieces]).astype(BF))
        value = jnp.concatenate([value] * exp_dev, axis=1)
        out_ref[n] = jnp.where(own, value, 0.0).astype(BF)


def spread(pieces, parts, exp_dev):
    _, span, cols = pieces[0].shape
    return pl.pallas_call(
        functools.partial(spread_kernel, parts, exp_dev),
        out_shape=jax.ShapeDtypeStruct((3, span * parts, cols * exp_dev), BF),
        compiler_params=pltpu.CompilerParams(vmem_limit_bytes=SMALL_LIMIT),
        cost_estimate=BRIEF,
        name="spread",
    )(*pieces)


def inner_kernel(parts, rows, count, *refs):
    lines, left_ref, outs = refs[:count], refs[count], refs[count + 1 :]
    block = left_ref.shape[1]
    offset = pl.multiple_of(lax.axis_index("mp") * block, 128)
    x = jnp.concatenate([line[:, pl.ds(offset, block)] for line in lines])
    value = dot_nt(x, left_ref[...])
    for k in range(parts):
        outs[k][...] = rotated(value, rows, parts, k).astype(BF)


def inner_products(lines, left, parts, rows):
    total = sum(line.shape[0] for line in lines)
    ranks = left.shape[0]
    return pl.pallas_call(
        functools.partial(inner_kernel, parts, rows, len(lines)),
        out_shape=[jax.ShapeDtypeStruct((total, ranks), BF)] * parts,
        compiler_params=pltpu.CompilerParams(vmem_limit_bytes=VMEM_LIMIT),
        cost_estimate=BRIEF,
        name="inner",
    )(*lines, left)


def raw_kernel(count, tile, *refs):
    lines, (gate_w, up_w, gate_ref, up_ref) = refs[:count], refs[count:]
    hid, width = gate_w.shape
    x = jnp.concatenate([line[:, :width] for line in lines])
    for i in range(hid // tile):
        span = pl.ds(i * tile, tile)
        gate_ref[:, span] = dot_nt(gate_w[span], x).T
        up_ref[:, span] = dot_nt(up_w[span], x).T


def raw_products(lines, gate_w, up_w):
    hid = gate_w.shape[0]
    total = sum(line.shape[0] for line in lines)
    tile = 384
    return pl.pallas_call(
        functools.partial(raw_kernel, len(lines), tile),
        out_shape=[jax.ShapeDtypeStruct((total, hid), F32)] * 2,
        compiler_params=pltpu.CompilerParams(vmem_limit_bytes=VMEM_LIMIT),
        cost_estimate=BRIEF,
        name="raw",
    )(*lines, gate_w, up_w)


def hidden_kernel(parts, count, exp_dev, pair, *refs):
    lines, inner, rest = refs[:count], refs[count : count + parts], refs[count + parts :]
    gate_ref, up_ref, diag_ref, hidden_ref = rest[:4]
    outs = rest[4:]
    hid = gate_ref.shape[1]
    ranks = diag_ref.shape[1]
    wide = lines[0].shape[1] - pair
    total = sum(ref[...].astype(F32) for ref in inner).astype(BF)
    gate = gate_ref[...] + dot_nn(total[:, :ranks], diag_ref[0])
    up = up_ref[...] + dot_nn(total[:, ranks:], diag_ref[1])
    lane = lax.broadcasted_iota(jnp.int32, (pair, hid), 0)
    lane = jnp.where(lane < pair // 2, lane, lane - pair // 2)
    cols = hid // exp_dev
    first = (lax.axis_index("y") * 2 + lax.axis_index("core")) * exp_dev
    place = lax.broadcasted_iota(jnp.int32, (pair, hid), 1) - (lane - first) * cols
    pick = ((place >= 0) & (place < cols)).astype(F32).astype(BF)
    scale = dot_nn(jnp.concatenate([line[:, wide:] for line in lines]), pick)
    hidden = (gate / (1.0 + jnp.exp(-gate)) * up * scale).astype(BF)
    hidden_ref[...] = hidden
    value = dot_nt(hidden, diag_ref[2])
    chips = len(outs)
    span = value.shape[0] // (2 * chips)
    for n, out_ref in enumerate(outs):
        rows = [value[i * span : (i + 1) * span] for i in (n, n + chips)]
        out_ref[...] = jnp.concatenate(rows).astype(BF)


def hidden_units(lines, inner, raw, diag, parts, exp_dev, pair, chips):
    total, hid = raw[0].shape
    ranks = diag.shape[1]
    return pl.pallas_call(
        functools.partial(hidden_kernel, parts, len(lines), exp_dev, pair),
        out_shape=[jax.ShapeDtypeStruct((total, hid), BF)]
        + [jax.ShapeDtypeStruct((total // chips, ranks), BF)] * chips,
        compiler_params=pltpu.CompilerParams(vmem_limit_bytes=VMEM_LIMIT),
        cost_estimate=BRIEF,
        name="hidden",
    )(*lines, *inner, *raw, diag)


def down_kernel(hidden_ref, down_ref, near_ref, far_ref):
    near, width = near_ref.shape
    hidden = hidden_ref[...]
    tile = min(1024, width)
    for i in range(width // tile):
        span = slice(i * tile, (i + 1) * tile)
        value = dot_nn(hidden, down_ref[:, span])
        near_ref[:, span] = value[:near]
        far_ref[:, span] = value[near:].astype(BF)


def down_products(hidden, down_w):
    total, width = hidden.shape[0], down_w.shape[1]
    return pl.pallas_call(
        down_kernel,
        out_shape=[
            jax.ShapeDtypeStruct((total // 2, width), F32),
            jax.ShapeDtypeStruct((total // 2, width), BF),
        ],
        compiler_params=pltpu.CompilerParams(vmem_limit_bytes=VMEM_LIMIT),
        cost_estimate=BRIEF,
        name="down",
    )(hidden, down_w)


def pair_kernel(*refs):
    ins, (near_ref, far_ref) = refs[:-2], refs[-2:]
    value = jnp.concatenate([ref[...].astype(F32) for ref in ins], axis=1)
    span = near_ref.shape[0]
    near_ref[...] = value[:span].astype(BF)
    far_ref[...] = value[span:].astype(BF)


def side_by_side(lines):
    total, ranks = lines[0].shape
    return pl.pallas_call(
        pair_kernel,
        out_shape=[jax.ShapeDtypeStruct((total // 2, len(lines) * ranks), BF)] * 2,
        compiler_params=pltpu.CompilerParams(vmem_limit_bytes=SMALL_LIMIT),
        cost_estimate=LONGER,
        name="pair",
    )(*lines)


def turn_kernel(rows, near_ref, far_ref, *outs):
    value = jnp.concatenate([near_ref[...].astype(F32), far_ref[...].astype(F32)], axis=1)
    for k, out_ref in enumerate(outs):
        out_ref[...] = rotated(value, rows, len(outs), k).astype(BF)


def turn(near, far, parts, rows):
    span, ranks = near.shape
    return pl.pallas_call(
        functools.partial(turn_kernel, rows),
        out_shape=[jax.ShapeDtypeStruct((span, 2 * ranks), BF)] * parts,
        compiler_params=pltpu.CompilerParams(vmem_limit_bytes=SMALL_LIMIT),
        cost_estimate=BRIEF,
        name="turn",
    )(near, far)


def add_up_kernel(*refs):
    refs[-1][...] = sum(ref[...].astype(F32) for ref in refs[:-1]).astype(BF)


def add_up(pieces):
    return pl.pallas_call(
        add_up_kernel,
        out_shape=jax.ShapeDtypeStruct(pieces[0].shape, BF),
        compiler_params=pltpu.CompilerParams(vmem_limit_bytes=SMALL_LIMIT),
        cost_estimate=LONG,
        name="add_up",
    )(*pieces)


def fold_kernel(head, near_ref, far_ref, own_ref, *out_refs):
    span = own_ref.shape[0]
    total = near_ref[...] + far_ref[...].astype(F32)
    own_ref[...] = total[:span]
    for n in range(len(out_refs) // 2):
        line = total[(n + 1) * span : (n + 2) * span]
        out_refs[2 * n][...] = line[:head].astype(BF)
        out_refs[2 * n + 1][...] = line[head:].astype(BF)


def fold(near, far, chips, head):
    total, width = near.shape
    span = total // chips
    return pl.pallas_call(
        functools.partial(fold_kernel, head),
        out_shape=[jax.ShapeDtypeStruct((span, width), F32)]
        + [jax.ShapeDtypeStruct((rows, width), BF) for rows in (head, span - head)]
        * (chips - 1),
        compiler_params=pltpu.CompilerParams(vmem_limit_bytes=VMEM_LIMIT),
        cost_estimate=BRIEF,
        name="fold",
    )(near, far)


def merge_kernel(chips, parts, *refs):
    own_ref, rights, refs = refs[0], refs[1 : 1 + 2 * chips], refs[1 + 2 * chips :]
    low, backs, outs = refs[0][...], refs[1:-parts], refs[-parts:]
    rows = outs[0].shape[0]
    ranks, block = rights[0].shape
    offset = pl.multiple_of(lax.axis_index("mp") * block, 128)
    value = jnp.zeros((low.shape[0], block), F32)
    for n, ref in enumerate(rights):
        value += dot_nn(low[:, n * ranks : (n + 1) * ranks], ref[...])
    total = own_ref[...]
    value += own_ref[:, pl.ds(offset, block)]
    for n in range(0, len(backs), 2):
        total += jnp.concatenate([ref[...].astype(F32) for ref in backs[n : n + 2]])
        value += jnp.concatenate(
            [ref[:, pl.ds(offset, block)].astype(F32) for ref in backs[n : n + 2]]
        )
    for k, out_ref in enumerate(outs):
        span = slice(k * rows, (k + 1) * rows)
        out_ref[...] = total[span].astype(out_ref.dtype)
        out_ref[:, pl.ds(offset, block)] = value[span].astype(out_ref.dtype)


def merge(own, rights, low, backs, rows):
    total, width = own.shape
    parts = total // rows
    return pl.pallas_call(
        functools.partial(merge_kernel, len(rights) // 2, parts),
        out_shape=[jax.ShapeDtypeStruct((rows, width), F32)]
        + [jax.ShapeDtypeStruct((rows, width), BF)] * (parts - 1),
        compiler_params=pltpu.CompilerParams(vmem_limit_bytes=VMEM_LIMIT),
        cost_estimate=BRIEF,
        name="merge",
    )(own, *rights, low, *backs)


def local(
    tokens,
    routes,
    probs,
    w_gate,
    w_up,
    w_down,
    gate_left,
    gate_right,
    up_left,
    up_right,
    down_left,
    down_right,
):
    rows, width = tokens.shape
    exp_dev, _, cols = w_gate.shape
    rank = gate_left.shape[1]
    block = gate_left.shape[2]
    parts = lax.axis_size("mp")
    chips = lax.axis_size("y")
    experts = exp_dev * chips * 2
    ranks = exp_dev * rank
    hid = exp_dev * cols

    def along_z(value, step):
        return lax.ppermute(value, "mp", [(i, (i + step) % parts) for i in range(parts)])

    def along_y(value, step):
        return lax.ppermute(value, "y", [(i, (i + step) % chips) for i in range(chips)])

    def other_core(value):
        return lax.ppermute(value, "core", [(0, 1), (1, 0)])

    pair = 2 * (-(-experts // 64) * 64)
    sent = attach(tokens, routes, probs, pair)
    arrived = [along_z(sent, k) for k in range(1, parts)]
    first = [along_y(sent, s) for s in range(1, chips)]
    gate_w, up_w = (jnp.swapaxes(w, 1, 2).reshape(hid, width) for w in (w_gate, w_up))
    gate_w, left, *small = prepare(
        (gate_right, up_right, down_left), (gate_left, up_left), gate_w, parts
    )
    right = down_right.reshape(ranks, block)
    partner_right = other_core(right)
    rest = after(jnp.concatenate(arrived), (left, small, gate_w, partner_right))
    up_w = load(after(up_w, rest))
    lines = [jnp.concatenate([sent, rest])]
    partner = [other_core(lines[0])]
    small = after(tuple(small), rest)
    small = [small[0]] + [along_z(small[k], k) for k in range(1, parts)]
    for s in range(1, chips):
        line = jnp.concatenate([first[s - 1], along_y(rest, s)])
        arrival = line
        line = after(line, (tuple(small), up_w))
        lines.append(line)
        partner.append(other_core(line))
    lines += partner
    diag = spread(small, parts, exp_dev)

    lines = after(tuple(lines), diag)
    inner = inner_products(lines, left, parts, rows)
    inner = [inner[0]] + [along_z(inner[k], k) for k in range(1, parts)]
    raw = raw_products(lines, gate_w, up_w)
    right = after(right, arrival)
    rights = [right] + [along_y(right, -s) for s in range(1, chips)]
    raw = after(tuple(raw), rights[1:])
    hidden, low, *lows = hidden_units(
        lines, inner, raw, diag, parts, exp_dev, pair, chips
    )
    lows = [along_y(lows[s - 1], -s) for s in range(1, chips)]
    near, far = side_by_side([low] + lows)
    bottom = turn(near, other_core(far), parts, rows)
    bottom = [bottom[0]] + [along_z(bottom[k], k) for k in range(1, parts)]

    near, far = down_products(hidden, w_down.reshape(hid, width))
    out, *others = fold(near, other_core(far), chips, rows)
    backs = [along_y(others[n], -(n // 2 + 1)) for n in range(2 * chips - 2)]
    rights += [partner_right] + [other_core(after(right, bottom[0])) for right in rights[1:]]
    own, *pieces = merge(out, rights, add_up(bottom[1:] + bottom[:1]), backs, rows)
    result = own
    for k in range(1, parts):
        result += along_z(pieces[k - 1], -k).astype(F32)
    return result.astype(BF)


def solution(mesh):
    count = mesh.shape
    fine = jax.sharding.Mesh(
        mesh.devices.reshape(count["groups"], count["expert"] // 2, 2, count["mp"]),
        ("groups", "y", "core", "mp"),
    )
    expert = ("y", "core")
    return jax.shard_map(
        local,
        mesh=fine,
        in_specs=(
            P(("groups", "y", "core", "mp"), None),
            P(("groups", "y", "core", "mp"), None),
            P(("groups", "y", "core", "mp"), None),
            P(expert, None, "mp"),
            P(expert, None, "mp"),
            P(expert, "mp", None),
            P(expert, None, "mp"),
            P(expert, "mp", None),
            P(expert, None, "mp"),
            P(expert, "mp", None),
            P(expert, "mp", None),
            P(expert, None, "mp"),
        ),
        out_specs=P(("groups", "y", "core", "mp"), None),
        check_vma=False,
    )
```

```python
import functools

import jax
import jax.numpy as jnp
from jax import lax
from jax.experimental import pallas as pl
from jax.experimental.pallas import tpu as pltpu
from jax.sharding import PartitionSpec as P

BF = jnp.bfloat16
F32 = jnp.float32
SMALL_LIMIT = 4 * 1024 * 1024
VMEM_LIMIT = 12 * 1024 * 1024
PIECES = 8
LONG = pl.CostEstimate(flops=1_000_000_000, bytes_accessed=1, transcendentals=0)
LONGER = pl.CostEstimate(flops=10_000_000_000, bytes_accessed=1, transcendentals=0)
LAST = pl.CostEstimate(flops=1_000_000_000, bytes_accessed=1, transcendentals=0)
BRIEF = pl.CostEstimate(flops=1, bytes_accessed=1, transcendentals=0)


def dot_nt(a, b):
    return lax.dot_general(a, b, (((1,), (1,)), ((), ())), preferred_element_type=F32)


def dot_nn(a, b):
    return lax.dot_general(a, b, (((1,), (0,)), ((), ())), preferred_element_type=F32)


def in_hbm(*values):
    return [pltpu.with_memory_space_constraint(v, pltpu.HBM) for v in values]


def after(value, earlier):
    return lax.optimization_barrier((value, earlier))[0]


def rotated(value, rows, parts, step):
    if step == 0:
        return value
    span = rows * parts
    lines = []
    for start in range(0, value.shape[0], span):
        cut = start + span - step * rows
        lines += [value[cut : start + span], value[start:cut]]
    return jnp.concatenate(lines)


def attach_kernel(tokens_ref, routes_ref, probs_ref, out_ref):
    rows, width = tokens_ref.shape
    pair = out_ref.shape[1] - width
    out_ref[:, :width] = tokens_ref[...]
    routes = routes_ref[...]
    probs = probs_ref[...]
    lane = lax.broadcasted_iota(jnp.int32, (rows, pair), 1)
    ids = jnp.where(lane < pair // 2, lane, lane - pair // 2)
    weight = jnp.zeros((rows, pair), F32)
    for k in range(routes.shape[1]):
        weight += jnp.where(ids == routes[:, k : k + 1], probs[:, k : k + 1], 0.0)
    high = weight.astype(BF).astype(F32)
    out_ref[:, width:] = jnp.where(lane < pair // 2, high, weight - high).astype(BF)


def attach(tokens, routes, probs, pair):
    rows, width = tokens.shape
    return pl.pallas_call(
        attach_kernel,
        out_shape=jax.ShapeDtypeStruct((rows, width + pair), BF),
        compiler_params=pltpu.CompilerParams(vmem_limit_bytes=SMALL_LIMIT),
        cost_estimate=BRIEF,
        name="attach",
    )(*in_hbm(tokens, routes, probs))


def piece_copies(source, target, sems):
    step = source.shape[0] // PIECES
    spans = [pl.ds(i * step, step) for i in range(PIECES)]
    return [
        pltpu.make_async_copy(source.at[span], target.at[span], sems.at[i])
        for i, span in enumerate(spans)
    ]


def load_kernel(source, target, sems):
    copies = piece_copies(source, target, sems)
    for copy in copies:
        copy.start()
    for copy in copies:
        copy.wait()


def load(weights):
    return pl.pallas_call(
        load_kernel,
        in_specs=[pl.BlockSpec(memory_space=pltpu.HBM)],
        out_specs=pl.BlockSpec(memory_space=pltpu.VMEM),
        out_shape=pltpu.VMEM(weights.shape, weights.dtype),
        scratch_shapes=[pltpu.SemaphoreType.DMA((PIECES,))],
        compiler_params=pltpu.CompilerParams(vmem_limit_bytes=SMALL_LIMIT),
        cost_estimate=BRIEF,
        name="load",
    )(*in_hbm(weights))


def prepare_kernel(parts, *refs):
    ins, lefts, source = refs[:3], refs[3:5], refs[5]
    target, left_ref, outs, sems = refs[6], refs[7], refs[8:-1], refs[-1]
    copies = piece_copies(source, target, sems)
    for copy in copies:
        copy.start()
    half = left_ref.shape[0] // 2
    for n, ref in enumerate(lefts):
        left_ref[n * half : (n + 1) * half] = ref[...].reshape(half, left_ref.shape[1])
    exp_dev, piece, hid = ins[0].shape
    cols = hid // parts
    me = lax.axis_index("mp")
    for n, ref in enumerate(ins):
        value = ref[...].reshape(exp_dev * piece, hid).astype(F32)
        blocks = [value[:, j * cols : (j + 1) * cols] for j in range(parts)]
        for k in range(parts):
            device = lax.rem(me + k, parts)
            block = blocks[0]
            for j in range(1, parts):
                block = jnp.where(device == j, blocks[j], block)
            outs[k][n] = block.astype(BF)
    for copy in copies:
        copy.wait()


def prepare(factors, lefts, weights, parts):
    exp_dev, piece, hid = factors[0].shape
    _, rank, block = lefts[0].shape
    vmem = pl.BlockSpec(memory_space=pltpu.VMEM)
    return pl.pallas_call(
        functools.partial(prepare_kernel, parts),
        in_specs=[vmem] * 5 + [pl.BlockSpec(memory_space=pltpu.HBM)],
        out_specs=[vmem] * (2 + parts),
        out_shape=[pltpu.VMEM(weights.shape, weights.dtype)]
        + [jax.ShapeDtypeStruct((2 * exp_dev * rank, block), BF)]
        + [jax.ShapeDtypeStruct((3, exp_dev * piece, hid // parts), BF)] * parts,
        scratch_shapes=[pltpu.SemaphoreType.DMA((PIECES,))],
        compiler_params=pltpu.CompilerParams(vmem_limit_bytes=SMALL_LIMIT),
        cost_estimate=BRIEF,
        name="prepare",
    )(*in_hbm(*factors, *lefts, weights))


def spread_kernel(parts, exp_dev, *refs):
    pieces, out_ref = refs[:-1], refs[-1]
    _, ranks, hid = out_ref.shape
    rank = ranks // exp_dev
    piece = rank // parts
    me = lax.axis_index("mp")
    row = lax.broadcasted_iota(jnp.int32, (ranks, ranks), 0)
    col = lax.broadcasted_iota(jnp.int32, (ranks, ranks), 1)
    step = lax.rem(me - row % rank // piece + parts, parts)
    source = (step * exp_dev + row // rank) * piece + row % piece
    order = (col == source).astype(F32).astype(BF)
    cols = hid // exp_dev
    place = lax.broadcasted_iota(jnp.int32, (ranks, hid), 1)
    place -= lax.broadcasted_iota(jnp.int32, (ranks, hid), 0) // rank * cols
    own = (place >= 0) & (place < cols)
    for n in range(3):
        value = dot_nn(order, jnp.concatenate([p[n].astype(F32) for p in pieces]).astype(BF))
        value = jnp.concatenate([value] * exp_dev, axis=1)
        out_ref[n] = jnp.where(own, value, 0.0).astype(BF)


def spread(pieces, parts, exp_dev):
    _, span, cols = pieces[0].shape
    return pl.pallas_call(
        functools.partial(spread_kernel, parts, exp_dev),
        out_shape=jax.ShapeDtypeStruct((3, span * parts, cols * exp_dev), BF),
        compiler_params=pltpu.CompilerParams(vmem_limit_bytes=SMALL_LIMIT),
        cost_estimate=BRIEF,
        name="spread",
    )(*pieces)


def inner_kernel(parts, rows, count, *refs):
    lines, left_ref, outs = refs[:count], refs[count], refs[count + 1 :]
    block = left_ref.shape[1]
    offset = pl.multiple_of(lax.axis_index("mp") * block, 128)
    x = jnp.concatenate([line[:, pl.ds(offset, block)] for line in lines])
    value = dot_nt(x, left_ref[...])
    for k in range(parts):
        outs[k][...] = rotated(value, rows, parts, k).astype(BF)


def inner_products(lines, left, parts, rows):
    total = sum(line.shape[0] for line in lines)
    ranks = left.shape[0]
    return pl.pallas_call(
        functools.partial(inner_kernel, parts, rows, len(lines)),
        out_shape=[jax.ShapeDtypeStruct((total, ranks), BF)] * parts,
        compiler_params=pltpu.CompilerParams(vmem_limit_bytes=VMEM_LIMIT),
        cost_estimate=BRIEF,
        name="inner",
    )(*lines, left)


def raw_kernel(count, tile, *refs):
    lines, (gate_w, up_w, gate_ref, up_ref) = refs[:count], refs[count:]
    hid, width = gate_w.shape
    x = jnp.concatenate([line[:, :width] for line in lines])
    for i in range(hid // tile):
        span = pl.ds(i * tile, tile)
        gate_ref[:, span] = dot_nt(gate_w[span], x).T
        up_ref[:, span] = dot_nt(up_w[span], x).T


def raw_products(lines, gate_w, up_w):
    hid = gate_w.shape[0]
    total = sum(line.shape[0] for line in lines)
    tile = 384
    return pl.pallas_call(
        functools.partial(raw_kernel, len(lines), tile),
        out_shape=[jax.ShapeDtypeStruct((total, hid), F32)] * 2,
        compiler_params=pltpu.CompilerParams(vmem_limit_bytes=VMEM_LIMIT),
        cost_estimate=BRIEF,
        name="raw",
    )(*lines, gate_w, up_w)


def hidden_kernel(parts, count, exp_dev, pair, *refs):
    lines, inner, rest = refs[:count], refs[count : count + parts], refs[count + parts :]
    gate_ref, up_ref, diag_ref, hidden_ref = rest[:4]
    outs = rest[4:]
    hid = gate_ref.shape[1]
    ranks = diag_ref.shape[1]
    wide = lines[0].shape[1] - pair
    total = sum(ref[...].astype(F32) for ref in inner).astype(BF)
    gate = gate_ref[...] + dot_nn(total[:, :ranks], diag_ref[0])
    up = up_ref[...] + dot_nn(total[:, ranks:], diag_ref[1])
    lane = lax.broadcasted_iota(jnp.int32, (pair, hid), 0)
    lane = jnp.where(lane < pair // 2, lane, lane - pair // 2)
    cols = hid // exp_dev
    first = (lax.axis_index("y") * 2 + lax.axis_index("core")) * exp_dev
    place = lax.broadcasted_iota(jnp.int32, (pair, hid), 1) - (lane - first) * cols
    pick = ((place >= 0) & (place < cols)).astype(F32).astype(BF)
    scale = dot_nn(jnp.concatenate([line[:, wide:] for line in lines]), pick)
    hidden = (gate / (1.0 + jnp.exp(-gate)) * up * scale).astype(BF)
    hidden_ref[...] = hidden
    value = dot_nt(hidden, diag_ref[2])
    chips = len(outs)
    span = value.shape[0] // (2 * chips)
    for n, out_ref in enumerate(outs):
        rows = [value[i * span : (i + 1) * span] for i in (n, n + chips)]
        out_ref[...] = jnp.concatenate(rows).astype(BF)


def hidden_units(lines, inner, raw, diag, parts, exp_dev, pair, chips):
    total, hid = raw[0].shape
    ranks = diag.shape[1]
    return pl.pallas_call(
        functools.partial(hidden_kernel, parts, len(lines), exp_dev, pair),
        out_shape=[jax.ShapeDtypeStruct((total, hid), BF)]
        + [jax.ShapeDtypeStruct((total // chips, ranks), BF)] * chips,
        compiler_params=pltpu.CompilerParams(vmem_limit_bytes=VMEM_LIMIT),
        cost_estimate=BRIEF,
        name="hidden",
    )(*lines, *inner, *raw, diag)


def down_kernel(hidden_ref, down_ref, near_ref, far_ref):
    near, width = near_ref.shape
    hidden = hidden_ref[...]
    tile = min(1024, width)
    for i in range(width // tile):
        span = slice(i * tile, (i + 1) * tile)
        value = dot_nn(hidden, down_ref[:, span])
        near_ref[:, span] = value[:near]
        far_ref[:, span] = value[near:].astype(BF)


def down_products(hidden, down_w):
    total, width = hidden.shape[0], down_w.shape[1]
    return pl.pallas_call(
        down_kernel,
        out_shape=[
            jax.ShapeDtypeStruct((total // 2, width), F32),
            jax.ShapeDtypeStruct((total // 2, width), BF),
        ],
        compiler_params=pltpu.CompilerParams(vmem_limit_bytes=VMEM_LIMIT),
        cost_estimate=BRIEF,
        name="down",
    )(hidden, down_w)


def pair_kernel(*refs):
    ins, (near_ref, far_ref) = refs[:-2], refs[-2:]
    value = jnp.concatenate([ref[...].astype(F32) for ref in ins], axis=1)
    span = near_ref.shape[0]
    near_ref[...] = value[:span].astype(BF)
    far_ref[...] = value[span:].astype(BF)


def side_by_side(lines):
    total, ranks = lines[0].shape
    return pl.pallas_call(
        pair_kernel,
        out_shape=[jax.ShapeDtypeStruct((total // 2, len(lines) * ranks), BF)] * 2,
        compiler_params=pltpu.CompilerParams(vmem_limit_bytes=SMALL_LIMIT),
        cost_estimate=LONGER,
        name="pair",
    )(*lines)


def turn_kernel(rows, near_ref, far_ref, *outs):
    value = jnp.concatenate([near_ref[...].astype(F32), far_ref[...].astype(F32)], axis=1)
    for k, out_ref in enumerate(outs):
        out_ref[...] = rotated(value, rows, len(outs), k).astype(BF)


def turn(near, far, parts, rows):
    span, ranks = near.shape
    return pl.pallas_call(
        functools.partial(turn_kernel, rows),
        out_shape=[jax.ShapeDtypeStruct((span, 2 * ranks), BF)] * parts,
        compiler_params=pltpu.CompilerParams(vmem_limit_bytes=SMALL_LIMIT),
        cost_estimate=BRIEF,
        name="turn",
    )(near, far)


def add_up_kernel(*refs):
    refs[-1][...] = sum(ref[...].astype(F32) for ref in refs[:-1]).astype(BF)


def add_up(pieces):
    return pl.pallas_call(
        add_up_kernel,
        out_shape=jax.ShapeDtypeStruct(pieces[0].shape, BF),
        compiler_params=pltpu.CompilerParams(vmem_limit_bytes=SMALL_LIMIT),
        cost_estimate=LONG,
        name="add_up",
    )(*pieces)


def fold_kernel(head, near_ref, far_ref, own_ref, *out_refs):
    span = own_ref.shape[0]
    total = near_ref[...] + far_ref[...].astype(F32)
    own_ref[...] = total[:span]
    for n in range(len(out_refs) // 2):
        line = total[(n + 1) * span : (n + 2) * span]
        out_refs[2 * n][...] = line[:head].astype(BF)
        out_refs[2 * n + 1][...] = line[head:].astype(BF)


def fold(near, far, chips, head):
    total, width = near.shape
    span = total // chips
    return pl.pallas_call(
        functools.partial(fold_kernel, head),
        out_shape=[jax.ShapeDtypeStruct((span, width), F32)]
        + [jax.ShapeDtypeStruct((rows, width), BF) for rows in (head, span - head)]
        * (chips - 1),
        compiler_params=pltpu.CompilerParams(vmem_limit_bytes=VMEM_LIMIT),
        cost_estimate=BRIEF,
        name="fold",
    )(near, far)


def merge_kernel(chips, parts, *refs):
    own_ref, rights, refs = refs[0], refs[1 : 1 + 2 * chips], refs[1 + 2 * chips :]
    low, backs, outs = refs[0][...], refs[1:-parts], refs[-parts:]
    rows = outs[0].shape[0]
    ranks, block = rights[0].shape
    offset = pl.multiple_of(lax.axis_index("mp") * block, 128)
    value = jnp.zeros((low.shape[0], block), F32)
    for n, ref in enumerate(rights):
        value += dot_nn(low[:, n * ranks : (n + 1) * ranks], ref[...])
    total = own_ref[...]
    value += own_ref[:, pl.ds(offset, block)]
    rest, rest_value = total[rows:], value[rows:]
    for ref in backs:
        rest += ref[...].astype(F32)
        rest_value += ref[:, pl.ds(offset, block)].astype(F32)
    outs[0][...] = total[:rows]
    outs[0][:, pl.ds(offset, block)] = value[:rows]
    for k in range(1, parts):
        span = slice((k - 1) * rows, k * rows)
        outs[k][...] = rest[span].astype(BF)
        outs[k][:, pl.ds(offset, block)] = rest_value[span].astype(BF)


def plus_kernel(own_ref, *refs):
    total = own_ref[...]
    for ref in refs[:-1]:
        total += ref[...].astype(F32)
    refs[-1][...] = total


def plus(own, pieces):
    return pl.pallas_call(
        plus_kernel,
        out_shape=jax.ShapeDtypeStruct(own.shape, F32),
        compiler_params=pltpu.CompilerParams(vmem_limit_bytes=SMALL_LIMIT),
        cost_estimate=LAST,
        name="plus",
    )(own, *pieces)


def merge(own, rights, low, backs, rows):
    total, width = own.shape
    parts = total // rows
    return pl.pallas_call(
        functools.partial(merge_kernel, len(rights) // 2, parts),
        out_shape=[jax.ShapeDtypeStruct((rows, width), F32)]
        + [jax.ShapeDtypeStruct((rows, width), BF)] * (parts - 1),
        compiler_params=pltpu.CompilerParams(vmem_limit_bytes=VMEM_LIMIT),
        cost_estimate=BRIEF,
        name="merge",
    )(own, *rights, low, *backs)


def local(
    tokens,
    routes,
    probs,
    w_gate,
    w_up,
    w_down,
    gate_left,
    gate_right,
    up_left,
    up_right,
    down_left,
    down_right,
):
    rows, width = tokens.shape
    exp_dev, _, cols = w_gate.shape
    rank = gate_left.shape[1]
    block = gate_left.shape[2]
    parts = lax.axis_size("mp")
    chips = lax.axis_size("y")
    experts = exp_dev * chips * 2
    ranks = exp_dev * rank
    hid = exp_dev * cols

    def along_z(value, step):
        return lax.ppermute(value, "mp", [(i, (i + step) % parts) for i in range(parts)])

    def along_y(value, step):
        return lax.ppermute(value, "y", [(i, (i + step) % chips) for i in range(chips)])

    def other_core(value):
        return lax.ppermute(value, "core", [(0, 1), (1, 0)])

    pair = 2 * (-(-experts // 64) * 64)
    sent = attach(tokens, routes, probs, pair)
    arrived = [along_z(sent, k) for k in range(1, parts)]
    first = [along_y(sent, s) for s in range(1, chips)]
    gate_w, up_w = (jnp.swapaxes(w, 1, 2).reshape(hid, width) for w in (w_gate, w_up))
    gate_w, left, *small = prepare(
        (gate_right, up_right, down_left), (gate_left, up_left), gate_w, parts
    )
    right = down_right.reshape(ranks, block)
    partner_right = other_core(right)
    rest = after(jnp.concatenate(arrived), (left, small, gate_w, partner_right))
    up_w = load(after(up_w, rest))
    lines = [jnp.concatenate([sent, rest])]
    partner = [other_core(lines[0])]
    small = after(tuple(small), rest)
    small = [small[0]] + [along_z(small[k], k) for k in range(1, parts)]
    for s in range(1, chips):
        line = jnp.concatenate([first[s - 1], along_y(rest, s)])
        arrival = line
        line = after(line, (tuple(small), up_w))
        lines.append(line)
        partner.append(other_core(line))
    lines += partner
    diag = spread(small, parts, exp_dev)

    lines = after(tuple(lines), diag)
    inner = inner_products(lines, left, parts, rows)
    inner = [inner[0]] + [along_z(inner[k], k) for k in range(1, parts)]
    raw = raw_products(lines, gate_w, up_w)
    right = after(right, arrival)
    rights = [right] + [along_y(right, -s) for s in range(1, chips)]
    raw = after(tuple(raw), rights[1:])
    hidden, low, *lows = hidden_units(
        lines, inner, raw, diag, parts, exp_dev, pair, chips
    )
    lows = [along_y(lows[s - 1], -s) for s in range(1, chips)]
    near, far = side_by_side([low] + lows)
    bottom = turn(near, other_core(far), parts, rows)
    bottom = [bottom[0]] + [along_z(bottom[k], k) for k in range(1, parts)]

    near, far = down_products(hidden, w_down.reshape(hid, width))
    out, *others = fold(near, other_core(far), chips, rows)
    backs = [along_y(others[n], -(n // 2 + 1)) for n in range(2 * chips - 2)]
    rights += [partner_right] + [other_core(after(right, bottom[0])) for right in rights[1:]]
    own, *pieces = merge(out, rights, add_up(bottom[1:] + bottom[:1]), backs[1::2], rows)
    result = plus(own, backs[::2])
    for k in range(1, parts):
        result += along_z(pieces[k - 1], -k).astype(F32)
    return result.astype(BF)


def solution(mesh):
    count = mesh.shape
    fine = jax.sharding.Mesh(
        mesh.devices.reshape(count["groups"], count["expert"] // 2, 2, count["mp"]),
        ("groups", "y", "core", "mp"),
    )
    expert = ("y", "core")
    return jax.shard_map(
        local,
        mesh=fine,
        in_specs=(
            P(("groups", "y", "core", "mp"), None),
            P(("groups", "y", "core", "mp"), None),
            P(("groups", "y", "core", "mp"), None),
            P(expert, None, "mp"),
            P(expert, None, "mp"),
            P(expert, "mp", None),
            P(expert, None, "mp"),
            P(expert, "mp", None),
            P(expert, None, "mp"),
            P(expert, "mp", None),
            P(expert, "mp", None),
            P(expert, None, "mp"),
        ),
        out_specs=P(("groups", "y", "core", "mp"), None),
        check_vma=False,
    )
```

```python
import functools

import jax
import jax.numpy as jnp
from jax import lax
from jax.experimental import pallas as pl
from jax.experimental.pallas import tpu as pltpu
from jax.sharding import PartitionSpec as P

BF = jnp.bfloat16
F32 = jnp.float32
SMALL_LIMIT = 4 * 1024 * 1024
VMEM_LIMIT = 12 * 1024 * 1024
STREAM_LIMIT = 14 * 1024 * 1024
PIECES = 8
LONG = pl.CostEstimate(flops=1_000_000_000, bytes_accessed=1, transcendentals=0)
LONGER = pl.CostEstimate(flops=10_000_000_000, bytes_accessed=1, transcendentals=0)
LAST = pl.CostEstimate(flops=1_000_000_000, bytes_accessed=1, transcendentals=0)
SOME = pl.CostEstimate(flops=3_000_000_000, bytes_accessed=1, transcendentals=0)
BRIEF = pl.CostEstimate(flops=1, bytes_accessed=1, transcendentals=0)


def dot_nt(a, b):
    return lax.dot_general(a, b, (((1,), (1,)), ((), ())), preferred_element_type=F32)


def dot_nn(a, b):
    return lax.dot_general(a, b, (((1,), (0,)), ((), ())), preferred_element_type=F32)


def in_hbm(*values):
    return [pltpu.with_memory_space_constraint(v, pltpu.HBM) for v in values]


def after(value, earlier):
    return lax.optimization_barrier((value, earlier))[0]


def rotated(value, rows, parts, step):
    if step == 0:
        return value
    span = rows * parts
    lines = []
    for start in range(0, value.shape[0], span):
        cut = start + span - step * rows
        lines += [value[cut : start + span], value[start:cut]]
    return jnp.concatenate(lines)


def attach_kernel(tokens_ref, routes_ref, probs_ref, out_ref):
    rows, width = tokens_ref.shape
    pair = out_ref.shape[1] - width
    out_ref[:, :width] = tokens_ref[...]
    routes = routes_ref[...]
    probs = probs_ref[...]
    lane = lax.broadcasted_iota(jnp.int32, (rows, pair), 1)
    ids = jnp.where(lane < pair // 2, lane, lane - pair // 2)
    weight = jnp.zeros((rows, pair), F32)
    for k in range(routes.shape[1]):
        weight += jnp.where(ids == routes[:, k : k + 1], probs[:, k : k + 1], 0.0)
    high = weight.astype(BF).astype(F32)
    out_ref[:, width:] = jnp.where(lane < pair // 2, high, weight - high).astype(BF)


def attach(tokens, routes, probs, pair):
    rows, width = tokens.shape
    return pl.pallas_call(
        attach_kernel,
        out_shape=jax.ShapeDtypeStruct((rows, width + pair), BF),
        compiler_params=pltpu.CompilerParams(vmem_limit_bytes=SMALL_LIMIT),
        cost_estimate=BRIEF,
        name="attach",
    )(*in_hbm(tokens, routes, probs))


def piece_copies(source, target, sems):
    step = source.shape[0] // PIECES
    spans = [pl.ds(i * step, step) for i in range(PIECES)]
    return [
        pltpu.make_async_copy(source.at[span], target.at[span], sems.at[i])
        for i, span in enumerate(spans)
    ]


def prepare_kernel(parts, *refs):
    ins, lefts, source = refs[:3], refs[3:5], refs[5]
    target, left_ref, outs, sems = refs[6], refs[7], refs[8:-1], refs[-1]
    copies = piece_copies(source, target, sems)
    for copy in copies:
        copy.start()
    half = left_ref.shape[0] // 2
    for n, ref in enumerate(lefts):
        left_ref[n * half : (n + 1) * half] = ref[...].reshape(half, left_ref.shape[1])
    exp_dev, piece, hid = ins[0].shape
    cols = hid // parts
    me = lax.axis_index("mp")
    for n, ref in enumerate(ins):
        value = ref[...].reshape(exp_dev * piece, hid).astype(F32)
        blocks = [value[:, j * cols : (j + 1) * cols] for j in range(parts)]
        for k in range(parts):
            device = lax.rem(me + k, parts)
            block = blocks[0]
            for j in range(1, parts):
                block = jnp.where(device == j, blocks[j], block)
            outs[k][n] = block.astype(BF)
    for copy in copies:
        copy.wait()


def prepare(factors, lefts, weights, parts):
    exp_dev, piece, hid = factors[0].shape
    _, rank, block = lefts[0].shape
    vmem = pl.BlockSpec(memory_space=pltpu.VMEM)
    return pl.pallas_call(
        functools.partial(prepare_kernel, parts),
        in_specs=[vmem] * 5 + [pl.BlockSpec(memory_space=pltpu.HBM)],
        out_specs=[vmem] * (2 + parts),
        out_shape=[pltpu.VMEM(weights.shape, weights.dtype)]
        + [jax.ShapeDtypeStruct((2 * exp_dev * rank, block), BF)]
        + [jax.ShapeDtypeStruct((3, exp_dev * piece, hid // parts), BF)] * parts,
        scratch_shapes=[pltpu.SemaphoreType.DMA((PIECES,))],
        compiler_params=pltpu.CompilerParams(vmem_limit_bytes=SMALL_LIMIT),
        cost_estimate=BRIEF,
        name="prepare",
    )(*in_hbm(*factors, *lefts, weights))


def spread_kernel(parts, exp_dev, *refs):
    pieces, out_ref = refs[:-1], refs[-1]
    _, ranks, hid = out_ref.shape
    rank = ranks // exp_dev
    piece = rank // parts
    me = lax.axis_index("mp")
    row = lax.broadcasted_iota(jnp.int32, (ranks, ranks), 0)
    col = lax.broadcasted_iota(jnp.int32, (ranks, ranks), 1)
    step = lax.rem(me - row % rank // piece + parts, parts)
    source = (step * exp_dev + row // rank) * piece + row % piece
    order = (col == source).astype(F32).astype(BF)
    cols = hid // exp_dev
    place = lax.broadcasted_iota(jnp.int32, (ranks, hid), 1)
    place -= lax.broadcasted_iota(jnp.int32, (ranks, hid), 0) // rank * cols
    own = (place >= 0) & (place < cols)
    for n in range(3):
        value = dot_nn(order, jnp.concatenate([p[n].astype(F32) for p in pieces]).astype(BF))
        value = jnp.concatenate([value] * exp_dev, axis=1)
        out_ref[n] = jnp.where(own, value, 0.0).astype(BF)


def spread(pieces, parts, exp_dev):
    _, span, cols = pieces[0].shape
    return pl.pallas_call(
        functools.partial(spread_kernel, parts, exp_dev),
        out_shape=jax.ShapeDtypeStruct((3, span * parts, cols * exp_dev), BF),
        compiler_params=pltpu.CompilerParams(vmem_limit_bytes=SMALL_LIMIT),
        cost_estimate=SOME,
        name="spread",
    )(*pieces)


def inner_kernel(parts, rows, count, *refs):
    lines, left_ref, outs = refs[:count], refs[count], refs[count + 1 :]
    block = left_ref.shape[1]
    offset = pl.multiple_of(lax.axis_index("mp") * block, 128)
    x = jnp.concatenate([line[:, pl.ds(offset, block)] for line in lines])
    value = dot_nt(x, left_ref[...])
    for k in range(parts):
        outs[k][...] = rotated(value, rows, parts, k).astype(BF)


def inner_products(lines, left, parts, rows):
    total = sum(line.shape[0] for line in lines)
    ranks = left.shape[0]
    return pl.pallas_call(
        functools.partial(inner_kernel, parts, rows, len(lines)),
        out_shape=[jax.ShapeDtypeStruct((total, ranks), BF)] * parts,
        compiler_params=pltpu.CompilerParams(vmem_limit_bytes=VMEM_LIMIT),
        cost_estimate=BRIEF,
        name="inner",
    )(*lines, left)


def raw_kernel(count, tile, *refs):
    lines, (gate_w, up_w, gate_ref, up_ref, scratch, sems) = refs[:count], refs[count:]
    hid, width = gate_w.shape
    copies = piece_copies(up_w, scratch, sems)
    for copy in copies:
        copy.start()
    x = jnp.concatenate([line[:, :width] for line in lines])
    spans = [pl.ds(i * tile, tile) for i in range(hid // tile)]
    for span in spans:
        gate_ref[:, span] = dot_nt(gate_w[span], x).T
    per = PIECES // len(spans)
    for i, span in enumerate(spans):
        for copy in copies[i * per : (i + 1) * per]:
            copy.wait()
        up_ref[:, span] = dot_nt(scratch[span], x).T


def raw_products(lines, gate_w, up_w):
    hid = gate_w.shape[0]
    total = sum(line.shape[0] for line in lines)
    vmem = pl.BlockSpec(memory_space=pltpu.VMEM)
    return pl.pallas_call(
        functools.partial(raw_kernel, len(lines), 384),
        in_specs=[vmem] * (len(lines) + 1) + [pl.BlockSpec(memory_space=pltpu.HBM)],
        out_specs=[vmem] * 2,
        out_shape=[jax.ShapeDtypeStruct((total, hid), F32)] * 2,
        scratch_shapes=[pltpu.VMEM(up_w.shape, BF), pltpu.SemaphoreType.DMA((PIECES,))],
        compiler_params=pltpu.CompilerParams(vmem_limit_bytes=STREAM_LIMIT),
        cost_estimate=BRIEF,
        name="raw",
    )(*lines, gate_w, *in_hbm(up_w))


def hidden_kernel(parts, count, exp_dev, pair, *refs):
    lines, inner, rest = refs[:count], refs[count : count + parts], refs[count + parts :]
    gate_ref, up_ref, diag_ref, hidden_ref = rest[:4]
    outs = rest[4:]
    hid = gate_ref.shape[1]
    ranks = diag_ref.shape[1]
    wide = lines[0].shape[1] - pair
    total = sum(ref[...].astype(F32) for ref in inner).astype(BF)
    gate = gate_ref[...] + dot_nn(total[:, :ranks], diag_ref[0])
    up = up_ref[...] + dot_nn(total[:, ranks:], diag_ref[1])
    lane = lax.broadcasted_iota(jnp.int32, (pair, hid), 0)
    lane = jnp.where(lane < pair // 2, lane, lane - pair // 2)
    cols = hid // exp_dev
    first = (lax.axis_index("y") * 2 + lax.axis_index("core")) * exp_dev
    place = lax.broadcasted_iota(jnp.int32, (pair, hid), 1) - (lane - first) * cols
    pick = ((place >= 0) & (place < cols)).astype(F32).astype(BF)
    scale = dot_nn(jnp.concatenate([line[:, wide:] for line in lines]), pick)
    hidden = (gate / (1.0 + jnp.exp(-gate)) * up * scale).astype(BF)
    hidden_ref[...] = hidden
    value = dot_nt(hidden, diag_ref[2])
    chips = len(outs)
    span = value.shape[0] // (2 * chips)
    for n, out_ref in enumerate(outs):
        rows = [value[i * span : (i + 1) * span] for i in (n, n + chips)]
        out_ref[...] = jnp.concatenate(rows).astype(BF)


def hidden_units(lines, inner, raw, diag, parts, exp_dev, pair, chips):
    total, hid = raw[0].shape
    ranks = diag.shape[1]
    return pl.pallas_call(
        functools.partial(hidden_kernel, parts, len(lines), exp_dev, pair),
        out_shape=[jax.ShapeDtypeStruct((total, hid), BF)]
        + [jax.ShapeDtypeStruct((total // chips, ranks), BF)] * chips,
        compiler_params=pltpu.CompilerParams(vmem_limit_bytes=VMEM_LIMIT),
        cost_estimate=BRIEF,
        name="hidden",
    )(*lines, *inner, *raw, diag)


def down_kernel(hidden_ref, down_ref, near_ref, far_ref):
    near, width = near_ref.shape
    hidden = hidden_ref[...]
    tile = min(1024, width)
    for i in range(width // tile):
        span = slice(i * tile, (i + 1) * tile)
        value = dot_nn(hidden, down_ref[:, span])
        near_ref[:, span] = value[:near]
        far_ref[:, span] = value[near:].astype(BF)


def down_products(hidden, down_w):
    total, width = hidden.shape[0], down_w.shape[1]
    return pl.pallas_call(
        down_kernel,
        out_shape=[
            jax.ShapeDtypeStruct((total // 2, width), F32),
            jax.ShapeDtypeStruct((total // 2, width), BF),
        ],
        compiler_params=pltpu.CompilerParams(vmem_limit_bytes=VMEM_LIMIT),
        cost_estimate=BRIEF,
        name="down",
    )(hidden, down_w)


def pair_kernel(*refs):
    ins, (near_ref, far_ref) = refs[:-2], refs[-2:]
    value = jnp.concatenate([ref[...].astype(F32) for ref in ins], axis=1)
    span = near_ref.shape[0]
    near_ref[...] = value[:span].astype(BF)
    far_ref[...] = value[span:].astype(BF)


def side_by_side(lines):
    total, ranks = lines[0].shape
    return pl.pallas_call(
        pair_kernel,
        out_shape=[jax.ShapeDtypeStruct((total // 2, len(lines) * ranks), BF)] * 2,
        compiler_params=pltpu.CompilerParams(vmem_limit_bytes=SMALL_LIMIT),
        cost_estimate=LONGER,
        name="pair",
    )(*lines)


def turn_kernel(rows, near_ref, far_ref, *outs):
    value = jnp.concatenate([near_ref[...].astype(F32), far_ref[...].astype(F32)], axis=1)
    for k, out_ref in enumerate(outs):
        out_ref[...] = rotated(value, rows, len(outs), k).astype(BF)


def turn(near, far, parts, rows):
    span, ranks = near.shape
    return pl.pallas_call(
        functools.partial(turn_kernel, rows),
        out_shape=[jax.ShapeDtypeStruct((span, 2 * ranks), BF)] * parts,
        compiler_params=pltpu.CompilerParams(vmem_limit_bytes=SMALL_LIMIT),
        cost_estimate=BRIEF,
        name="turn",
    )(near, far)


def add_up_kernel(*refs):
    refs[-1][...] = sum(ref[...].astype(F32) for ref in refs[:-1]).astype(BF)


def add_up(pieces):
    return pl.pallas_call(
        add_up_kernel,
        out_shape=jax.ShapeDtypeStruct(pieces[0].shape, BF),
        compiler_params=pltpu.CompilerParams(vmem_limit_bytes=SMALL_LIMIT),
        cost_estimate=LONG,
        name="add_up",
    )(*pieces)


def fold_kernel(head, near_ref, far_ref, own_ref, *out_refs):
    span = own_ref.shape[0]
    total = near_ref[...] + far_ref[...].astype(F32)
    own_ref[...] = total[:span]
    for n in range(len(out_refs) // 2):
        line = total[(n + 1) * span : (n + 2) * span]
        out_refs[2 * n][...] = line[:head].astype(BF)
        out_refs[2 * n + 1][...] = line[head:].astype(BF)


def fold(near, far, chips, head):
    total, width = near.shape
    span = total // chips
    return pl.pallas_call(
        functools.partial(fold_kernel, head),
        out_shape=[jax.ShapeDtypeStruct((span, width), F32)]
        + [jax.ShapeDtypeStruct((rows, width), BF) for rows in (head, span - head)]
        * (chips - 1),
        compiler_params=pltpu.CompilerParams(vmem_limit_bytes=VMEM_LIMIT),
        cost_estimate=BRIEF,
        name="fold",
    )(near, far)


def merge_kernel(chips, parts, *refs):
    own_ref, rights, refs = refs[0], refs[1 : 1 + 2 * chips], refs[1 + 2 * chips :]
    low, backs, outs = refs[0][...], refs[1:-parts], refs[-parts:]
    rows = outs[0].shape[0]
    ranks, block = rights[0].shape
    offset = pl.multiple_of(lax.axis_index("mp") * block, 128)
    value = jnp.zeros((low.shape[0], block), F32)
    for n, ref in enumerate(rights):
        value += dot_nn(low[:, n * ranks : (n + 1) * ranks], ref[...])
    total = own_ref[...]
    value += own_ref[:, pl.ds(offset, block)]
    rest, rest_value = total[rows:], value[rows:]
    for ref in backs:
        rest += ref[...].astype(F32)
        rest_value += ref[:, pl.ds(offset, block)].astype(F32)
    outs[0][...] = total[:rows]
    outs[0][:, pl.ds(offset, block)] = value[:rows]
    for k in range(1, parts):
        span = slice((k - 1) * rows, k * rows)
        outs[k][...] = rest[span].astype(BF)
        outs[k][:, pl.ds(offset, block)] = rest_value[span].astype(BF)


def plus_kernel(own_ref, *refs):
    total = own_ref[...]
    for ref in refs[:-1]:
        total += ref[...].astype(F32)
    refs[-1][...] = total


def plus(own, pieces):
    return pl.pallas_call(
        plus_kernel,
        out_shape=jax.ShapeDtypeStruct(own.shape, F32),
        compiler_params=pltpu.CompilerParams(vmem_limit_bytes=SMALL_LIMIT),
        cost_estimate=LAST,
        name="plus",
    )(own, *pieces)


def merge(own, rights, low, backs, rows):
    total, width = own.shape
    parts = total // rows
    return pl.pallas_call(
        functools.partial(merge_kernel, len(rights) // 2, parts),
        out_shape=[jax.ShapeDtypeStruct((rows, width), F32)]
        + [jax.ShapeDtypeStruct((rows, width), BF)] * (parts - 1),
        compiler_params=pltpu.CompilerParams(vmem_limit_bytes=VMEM_LIMIT),
        cost_estimate=BRIEF,
        name="merge",
    )(own, *rights, low, *backs)


def local(
    tokens,
    routes,
    probs,
    w_gate,
    w_up,
    w_down,
    gate_left,
    gate_right,
    up_left,
    up_right,
    down_left,
    down_right,
):
    rows, width = tokens.shape
    exp_dev, _, cols = w_gate.shape
    rank = gate_left.shape[1]
    block = gate_left.shape[2]
    parts = lax.axis_size("mp")
    chips = lax.axis_size("y")
    experts = exp_dev * chips * 2
    ranks = exp_dev * rank
    hid = exp_dev * cols

    def along_z(value, step):
        return lax.ppermute(value, "mp", [(i, (i + step) % parts) for i in range(parts)])

    def along_y(value, step):
        return lax.ppermute(value, "y", [(i, (i + step) % chips) for i in range(chips)])

    def other_core(value):
        return lax.ppermute(value, "core", [(0, 1), (1, 0)])

    pair = 2 * (-(-experts // 64) * 64)
    sent = attach(tokens, routes, probs, pair)
    arrived = [along_z(sent, k) for k in range(1, parts)]
    first = [along_y(sent, s) for s in range(1, chips)]
    gate_w, up_w = (jnp.swapaxes(w, 1, 2).reshape(hid, width) for w in (w_gate, w_up))
    gate_w, left, *small = prepare(
        (gate_right, up_right, down_left), (gate_left, up_left), gate_w, parts
    )
    right = down_right.reshape(ranks, block)
    partner_right = other_core(right)
    rest = after(jnp.concatenate(arrived), (left, small, gate_w, partner_right))
    lines = [jnp.concatenate([sent, rest])]
    partner = [other_core(lines[0])]
    small = after(tuple(small), rest)
    small = [small[0]] + [along_z(small[k], k) for k in range(1, parts)]
    for s in range(1, chips):
        line = jnp.concatenate([first[s - 1], along_y(rest, s)])
        arrival = line
        lines.append(line)
        partner.append(other_core(line))
    lines += partner
    diag = spread(small, parts, exp_dev)

    lines = after(tuple(lines), diag)
    inner = inner_products(lines, left, parts, rows)
    inner = [inner[0]] + [along_z(inner[k], k) for k in range(1, parts)]
    raw = raw_products(lines, gate_w, up_w)
    right = after(right, arrival)
    rights = [right] + [along_y(right, -s) for s in range(1, chips)]
    raw = after(tuple(raw), rights[1:])
    hidden, low, *lows = hidden_units(
        lines, inner, raw, diag, parts, exp_dev, pair, chips
    )
    lows = [along_y(lows[s - 1], -s) for s in range(1, chips)]
    near, far = side_by_side([low] + lows)
    bottom = turn(near, other_core(far), parts, rows)
    bottom = [bottom[0]] + [along_z(bottom[k], k) for k in range(1, parts)]

    near, far = down_products(hidden, w_down.reshape(hid, width))
    out, *others = fold(near, other_core(far), chips, rows)
    backs = [along_y(others[n], -(n // 2 + 1)) for n in range(2 * chips - 2)]
    rights += [partner_right] + [other_core(after(right, bottom[0])) for right in rights[1:]]
    own, *pieces = merge(out, rights, add_up(bottom[1:] + bottom[:1]), backs[1::2], rows)
    result = plus(own, backs[::2])
    for k in range(1, parts):
        result += along_z(pieces[k - 1], -k).astype(F32)
    return result.astype(BF)


def solution(mesh):
    count = mesh.shape
    fine = jax.sharding.Mesh(
        mesh.devices.reshape(count["groups"], count["expert"] // 2, 2, count["mp"]),
        ("groups", "y", "core", "mp"),
    )
    expert = ("y", "core")
    return jax.shard_map(
        local,
        mesh=fine,
        in_specs=(
            P(("groups", "y", "core", "mp"), None),
            P(("groups", "y", "core", "mp"), None),
            P(("groups", "y", "core", "mp"), None),
            P(expert, None, "mp"),
            P(expert, None, "mp"),
            P(expert, "mp", None),
            P(expert, None, "mp"),
            P(expert, "mp", None),
            P(expert, None, "mp"),
            P(expert, "mp", None),
            P(expert, "mp", None),
            P(expert, None, "mp"),
        ),
        out_specs=P(("groups", "y", "core", "mp"), None),
        check_vma=False,
    )
```

```python
import functools

import jax
import jax.numpy as jnp
from jax import lax
from jax.experimental import pallas as pl
from jax.experimental.pallas import tpu as pltpu
from jax.sharding import PartitionSpec as P

BF = jnp.bfloat16
F32 = jnp.float32
SMALL_LIMIT = 4 * 1024 * 1024
VMEM_LIMIT = 12 * 1024 * 1024
PIECES = 8
LONG = pl.CostEstimate(flops=1_000_000_000, bytes_accessed=1, transcendentals=0)
LONGER = pl.CostEstimate(flops=10_000_000_000, bytes_accessed=1, transcendentals=0)
LAST = pl.CostEstimate(flops=1_000_000_000, bytes_accessed=1, transcendentals=0)
SOME = pl.CostEstimate(flops=3_000_000_000, bytes_accessed=1, transcendentals=0)
BRIEF = pl.CostEstimate(flops=1, bytes_accessed=1, transcendentals=0)


def dot_nt(a, b):
    return lax.dot_general(a, b, (((1,), (1,)), ((), ())), preferred_element_type=F32)


def dot_nn(a, b):
    return lax.dot_general(a, b, (((1,), (0,)), ((), ())), preferred_element_type=F32)


def in_hbm(*values):
    return [pltpu.with_memory_space_constraint(v, pltpu.HBM) for v in values]


def after(value, earlier):
    return lax.optimization_barrier((value, earlier))[0]


def rotated(value, rows, parts, step):
    if step == 0:
        return value
    span = rows * parts
    lines = []
    for start in range(0, value.shape[0], span):
        cut = start + span - step * rows
        lines += [value[cut : start + span], value[start:cut]]
    return jnp.concatenate(lines)


def attach_kernel(tokens_ref, routes_ref, probs_ref, out_ref):
    rows, width = tokens_ref.shape
    pair = out_ref.shape[1] - width
    out_ref[:, :width] = tokens_ref[...]
    routes = routes_ref[...]
    probs = probs_ref[...]
    lane = lax.broadcasted_iota(jnp.int32, (rows, pair), 1)
    ids = jnp.where(lane < pair // 2, lane, lane - pair // 2)
    weight = jnp.zeros((rows, pair), F32)
    for k in range(routes.shape[1]):
        weight += jnp.where(ids == routes[:, k : k + 1], probs[:, k : k + 1], 0.0)
    high = weight.astype(BF).astype(F32)
    out_ref[:, width:] = jnp.where(lane < pair // 2, high, weight - high).astype(BF)


def attach(tokens, routes, probs, pair):
    rows, width = tokens.shape
    return pl.pallas_call(
        attach_kernel,
        out_shape=jax.ShapeDtypeStruct((rows, width + pair), BF),
        compiler_params=pltpu.CompilerParams(vmem_limit_bytes=SMALL_LIMIT),
        cost_estimate=BRIEF,
        name="attach",
    )(*in_hbm(tokens, routes, probs))


def piece_copies(source, target, sems):
    step = source.shape[0] // PIECES
    spans = [pl.ds(i * step, step) for i in range(PIECES)]
    return [
        pltpu.make_async_copy(source.at[span], target.at[span], sems.at[i])
        for i, span in enumerate(spans)
    ]


def load_kernel(source, target, sems):
    copies = piece_copies(source, target, sems)
    for copy in copies:
        copy.start()
    for copy in copies:
        copy.wait()


def load(weights):
    return pl.pallas_call(
        load_kernel,
        in_specs=[pl.BlockSpec(memory_space=pltpu.HBM)],
        out_specs=pl.BlockSpec(memory_space=pltpu.VMEM),
        out_shape=pltpu.VMEM(weights.shape, weights.dtype),
        scratch_shapes=[pltpu.SemaphoreType.DMA((PIECES,))],
        compiler_params=pltpu.CompilerParams(vmem_limit_bytes=SMALL_LIMIT),
        cost_estimate=SOME,
        name="load",
    )(*in_hbm(weights))


def prepare_kernel(parts, *refs):
    ins, lefts, source = refs[:3], refs[3:5], refs[5]
    target, left_ref, outs, sems = refs[6], refs[7], refs[8:-1], refs[-1]
    copies = piece_copies(source, target, sems)
    for copy in copies:
        copy.start()
    half = left_ref.shape[0] // 2
    for n, ref in enumerate(lefts):
        left_ref[n * half : (n + 1) * half] = ref[...].reshape(half, left_ref.shape[1])
    exp_dev, piece, hid = ins[0].shape
    cols = hid // parts
    me = lax.axis_index("mp")
    for n, ref in enumerate(ins):
        value = ref[...].reshape(exp_dev * piece, hid).astype(F32)
        blocks = [value[:, j * cols : (j + 1) * cols] for j in range(parts)]
        for k in range(parts):
            device = lax.rem(me + k, parts)
            block = blocks[0]
            for j in range(1, parts):
                block = jnp.where(device == j, blocks[j], block)
            outs[k][n] = block.astype(BF)
    for copy in copies:
        copy.wait()


def prepare(factors, lefts, weights, parts):
    exp_dev, piece, hid = factors[0].shape
    _, rank, block = lefts[0].shape
    vmem = pl.BlockSpec(memory_space=pltpu.VMEM)
    return pl.pallas_call(
        functools.partial(prepare_kernel, parts),
        in_specs=[vmem] * 5 + [pl.BlockSpec(memory_space=pltpu.HBM)],
        out_specs=[vmem] * (2 + parts),
        out_shape=[pltpu.VMEM(weights.shape, weights.dtype)]
        + [jax.ShapeDtypeStruct((2 * exp_dev * rank, block), BF)]
        + [jax.ShapeDtypeStruct((3, exp_dev * piece, hid // parts), BF)] * parts,
        scratch_shapes=[pltpu.SemaphoreType.DMA((PIECES,))],
        compiler_params=pltpu.CompilerParams(vmem_limit_bytes=SMALL_LIMIT),
        cost_estimate=BRIEF,
        name="prepare",
    )(*in_hbm(*factors, *lefts, weights))


def spread_kernel(parts, exp_dev, *refs):
    pieces, out_ref = refs[:-1], refs[-1]
    _, ranks, hid = out_ref.shape
    rank = ranks // exp_dev
    piece = rank // parts
    me = lax.axis_index("mp")
    row = lax.broadcasted_iota(jnp.int32, (ranks, ranks), 0)
    col = lax.broadcasted_iota(jnp.int32, (ranks, ranks), 1)
    step = lax.rem(me - row % rank // piece + parts, parts)
    source = (step * exp_dev + row // rank) * piece + row % piece
    order = (col == source).astype(F32).astype(BF)
    cols = hid // exp_dev
    place = lax.broadcasted_iota(jnp.int32, (ranks, hid), 1)
    place -= lax.broadcasted_iota(jnp.int32, (ranks, hid), 0) // rank * cols
    own = (place >= 0) & (place < cols)
    for n in range(3):
        value = dot_nn(order, jnp.concatenate([p[n].astype(F32) for p in pieces]).astype(BF))
        value = jnp.concatenate([value] * exp_dev, axis=1)
        out_ref[n] = jnp.where(own, value, 0.0).astype(BF)


def spread(pieces, parts, exp_dev):
    _, span, cols = pieces[0].shape
    return pl.pallas_call(
        functools.partial(spread_kernel, parts, exp_dev),
        out_shape=jax.ShapeDtypeStruct((3, span * parts, cols * exp_dev), BF),
        compiler_params=pltpu.CompilerParams(vmem_limit_bytes=SMALL_LIMIT),
        cost_estimate=SOME,
        name="spread",
    )(*pieces)


def inner_kernel(parts, rows, count, *refs):
    lines, left_ref, outs = refs[:count], refs[count], refs[count + 1 :]
    block = left_ref.shape[1]
    offset = pl.multiple_of(lax.axis_index("mp") * block, 128)
    x = jnp.concatenate([line[:, pl.ds(offset, block)] for line in lines])
    value = dot_nt(x, left_ref[...])
    for k in range(parts):
        outs[k][...] = rotated(value, rows, parts, k).astype(BF)


def inner_products(lines, left, parts, rows):
    total = sum(line.shape[0] for line in lines)
    ranks = left.shape[0]
    return pl.pallas_call(
        functools.partial(inner_kernel, parts, rows, len(lines)),
        out_shape=[jax.ShapeDtypeStruct((total, ranks), BF)] * parts,
        compiler_params=pltpu.CompilerParams(vmem_limit_bytes=VMEM_LIMIT),
        cost_estimate=BRIEF,
        name="inner",
    )(*lines, left)


def raw_kernel(count, tile, *refs):
    lines, (gate_w, up_w, gate_ref, up_ref) = refs[:count], refs[count:]
    hid, width = gate_w.shape
    x = jnp.concatenate([line[:, :width] for line in lines])
    for i in range(hid // tile):
        span = pl.ds(i * tile, tile)
        gate_ref[:, span] = dot_nt(gate_w[span], x).T
        up_ref[:, span] = dot_nt(up_w[span], x).T


def raw_products(lines, gate_w, up_w):
    hid = gate_w.shape[0]
    total = sum(line.shape[0] for line in lines)
    tile = 384
    return pl.pallas_call(
        functools.partial(raw_kernel, len(lines), tile),
        out_shape=[jax.ShapeDtypeStruct((total, hid), F32)] * 2,
        compiler_params=pltpu.CompilerParams(vmem_limit_bytes=VMEM_LIMIT),
        cost_estimate=BRIEF,
        name="raw",
    )(*lines, gate_w, up_w)


def hidden_kernel(parts, count, exp_dev, pair, *refs):
    lines, inner, rest = refs[:count], refs[count : count + parts], refs[count + parts :]
    gate_ref, up_ref, diag_ref, hidden_ref = rest[:4]
    outs = rest[4:]
    hid = gate_ref.shape[1]
    ranks = diag_ref.shape[1]
    wide = lines[0].shape[1] - pair
    total = sum(ref[...].astype(F32) for ref in inner).astype(BF)
    gate = gate_ref[...] + dot_nn(total[:, :ranks], diag_ref[0])
    up = up_ref[...] + dot_nn(total[:, ranks:], diag_ref[1])
    lane = lax.broadcasted_iota(jnp.int32, (pair, hid), 0)
    lane = jnp.where(lane < pair // 2, lane, lane - pair // 2)
    cols = hid // exp_dev
    first = (lax.axis_index("y") * 2 + lax.axis_index("core")) * exp_dev
    place = lax.broadcasted_iota(jnp.int32, (pair, hid), 1) - (lane - first) * cols
    pick = ((place >= 0) & (place < cols)).astype(F32).astype(BF)
    scale = dot_nn(jnp.concatenate([line[:, wide:] for line in lines]), pick)
    hidden = (gate / (1.0 + jnp.exp(-gate)) * up * scale).astype(BF)
    hidden_ref[...] = hidden
    value = dot_nt(hidden, diag_ref[2])
    chips = len(outs)
    span = value.shape[0] // (2 * chips)
    for n, out_ref in enumerate(outs):
        rows = [value[i * span : (i + 1) * span] for i in (n, n + chips)]
        out_ref[...] = jnp.concatenate(rows).astype(BF)


def hidden_units(lines, inner, raw, diag, parts, exp_dev, pair, chips):
    total, hid = raw[0].shape
    ranks = diag.shape[1]
    return pl.pallas_call(
        functools.partial(hidden_kernel, parts, len(lines), exp_dev, pair),
        out_shape=[jax.ShapeDtypeStruct((total, hid), BF)]
        + [jax.ShapeDtypeStruct((total // chips, ranks), BF)] * chips,
        compiler_params=pltpu.CompilerParams(vmem_limit_bytes=VMEM_LIMIT),
        cost_estimate=BRIEF,
        name="hidden",
    )(*lines, *inner, *raw, diag)


def down_kernel(hidden_ref, down_ref, near_ref, far_ref):
    near, width = near_ref.shape
    hidden = hidden_ref[...]
    tile = min(1024, width)
    for i in range(width // tile):
        span = slice(i * tile, (i + 1) * tile)
        value = dot_nn(hidden, down_ref[:, span])
        near_ref[:, span] = value[:near]
        far_ref[:, span] = value[near:].astype(BF)


def down_products(hidden, down_w):
    total, width = hidden.shape[0], down_w.shape[1]
    return pl.pallas_call(
        down_kernel,
        out_shape=[
            jax.ShapeDtypeStruct((total // 2, width), F32),
            jax.ShapeDtypeStruct((total // 2, width), BF),
        ],
        compiler_params=pltpu.CompilerParams(vmem_limit_bytes=VMEM_LIMIT),
        cost_estimate=BRIEF,
        name="down",
    )(hidden, down_w)


def pair_kernel(*refs):
    ins, (near_ref, far_ref) = refs[:-2], refs[-2:]
    value = jnp.concatenate([ref[...].astype(F32) for ref in ins], axis=1)
    span = near_ref.shape[0]
    near_ref[...] = value[:span].astype(BF)
    far_ref[...] = value[span:].astype(BF)


def side_by_side(lines):
    total, ranks = lines[0].shape
    return pl.pallas_call(
        pair_kernel,
        out_shape=[jax.ShapeDtypeStruct((total // 2, len(lines) * ranks), BF)] * 2,
        compiler_params=pltpu.CompilerParams(vmem_limit_bytes=SMALL_LIMIT),
        cost_estimate=LONGER,
        name="pair",
    )(*lines)


def turn_kernel(rows, near_ref, far_ref, *outs):
    value = jnp.concatenate([near_ref[...].astype(F32), far_ref[...].astype(F32)], axis=1)
    for k, out_ref in enumerate(outs):
        out_ref[...] = rotated(value, rows, len(outs), k).astype(BF)


def turn(near, far, parts, rows):
    span, ranks = near.shape
    return pl.pallas_call(
        functools.partial(turn_kernel, rows),
        out_shape=[jax.ShapeDtypeStruct((span, 2 * ranks), BF)] * parts,
        compiler_params=pltpu.CompilerParams(vmem_limit_bytes=SMALL_LIMIT),
        cost_estimate=BRIEF,
        name="turn",
    )(near, far)


def add_up_kernel(*refs):
    refs[-1][...] = sum(ref[...].astype(F32) for ref in refs[:-1]).astype(BF)


def add_up(pieces):
    return pl.pallas_call(
        add_up_kernel,
        out_shape=jax.ShapeDtypeStruct(pieces[0].shape, BF),
        compiler_params=pltpu.CompilerParams(vmem_limit_bytes=SMALL_LIMIT),
        cost_estimate=LONG,
        name="add_up",
    )(*pieces)


def fold_kernel(head, near_ref, far_ref, own_ref, *out_refs):
    span = own_ref.shape[0]
    total = near_ref[...] + far_ref[...].astype(F32)
    own_ref[...] = total[:span]
    for n in range(len(out_refs) // 2):
        line = total[(n + 1) * span : (n + 2) * span]
        out_refs[2 * n][...] = line[:head].astype(BF)
        out_refs[2 * n + 1][...] = line[head:].astype(BF)


def fold(near, far, chips, head):
    total, width = near.shape
    span = total // chips
    return pl.pallas_call(
        functools.partial(fold_kernel, head),
        out_shape=[jax.ShapeDtypeStruct((span, width), F32)]
        + [jax.ShapeDtypeStruct((rows, width), BF) for rows in (head, span - head)]
        * (chips - 1),
        compiler_params=pltpu.CompilerParams(vmem_limit_bytes=VMEM_LIMIT),
        cost_estimate=BRIEF,
        name="fold",
    )(near, far)


def merge_kernel(chips, parts, *refs):
    own_ref, rights, refs = refs[0], refs[1 : 1 + 2 * chips], refs[1 + 2 * chips :]
    low, backs, outs = refs[0][...], refs[1:-parts], refs[-parts:]
    rows = outs[0].shape[0]
    ranks, block = rights[0].shape
    offset = pl.multiple_of(lax.axis_index("mp") * block, 128)
    value = jnp.zeros((low.shape[0], block), F32)
    for n, ref in enumerate(rights):
        value += dot_nn(low[:, n * ranks : (n + 1) * ranks], ref[...])
    total = own_ref[...]
    value += own_ref[:, pl.ds(offset, block)]
    rest, rest_value = total[rows:], value[rows:]
    for ref in backs:
        rest += ref[...].astype(F32)
        rest_value += ref[:, pl.ds(offset, block)].astype(F32)
    outs[0][...] = total[:rows]
    outs[0][:, pl.ds(offset, block)] = value[:rows]
    for k in range(1, parts):
        span = slice((k - 1) * rows, k * rows)
        outs[k][...] = rest[span].astype(BF)
        outs[k][:, pl.ds(offset, block)] = rest_value[span].astype(BF)


def plus_kernel(own_ref, *refs):
    total = own_ref[...]
    for ref in refs[:-1]:
        total += ref[...].astype(F32)
    refs[-1][...] = total


def plus(own, pieces):
    return pl.pallas_call(
        plus_kernel,
        out_shape=jax.ShapeDtypeStruct(own.shape, F32),
        compiler_params=pltpu.CompilerParams(vmem_limit_bytes=SMALL_LIMIT),
        cost_estimate=LAST,
        name="plus",
    )(own, *pieces)


def merge(own, rights, low, backs, rows):
    total, width = own.shape
    parts = total // rows
    return pl.pallas_call(
        functools.partial(merge_kernel, len(rights) // 2, parts),
        out_shape=[jax.ShapeDtypeStruct((rows, width), F32)]
        + [jax.ShapeDtypeStruct((rows, width), BF)] * (parts - 1),
        compiler_params=pltpu.CompilerParams(vmem_limit_bytes=VMEM_LIMIT),
        cost_estimate=BRIEF,
        name="merge",
    )(own, *rights, low, *backs)


def local(
    tokens,
    routes,
    probs,
    w_gate,
    w_up,
    w_down,
    gate_left,
    gate_right,
    up_left,
    up_right,
    down_left,
    down_right,
):
    rows, width = tokens.shape
    exp_dev, _, cols = w_gate.shape
    rank = gate_left.shape[1]
    block = gate_left.shape[2]
    parts = lax.axis_size("mp")
    chips = lax.axis_size("y")
    experts = exp_dev * chips * 2
    ranks = exp_dev * rank
    hid = exp_dev * cols

    def along_z(value, step):
        return lax.ppermute(value, "mp", [(i, (i + step) % parts) for i in range(parts)])

    def along_y(value, step):
        return lax.ppermute(value, "y", [(i, (i + step) % chips) for i in range(chips)])

    def other_core(value):
        return lax.ppermute(value, "core", [(0, 1), (1, 0)])

    pair = 2 * (-(-experts // 64) * 64)
    sent = attach(tokens, routes, probs, pair)
    arrived = [along_z(sent, k) for k in range(1, parts)]
    first = [along_y(sent, s) for s in range(1, chips)]
    gate_w, up_w = (jnp.swapaxes(w, 1, 2).reshape(hid, width) for w in (w_gate, w_up))
    gate_w, left, *small = prepare(
        (gate_right, up_right, down_left), (gate_left, up_left), gate_w, parts
    )
    right = down_right.reshape(ranks, block)
    partner_right = other_core(right)
    rest = after(jnp.concatenate(arrived), (left, small, gate_w, partner_right))
    up_w = load(after(up_w, rest))
    lines = [jnp.concatenate([sent, rest])]
    partner = [other_core(lines[0])]
    small = after(tuple(small), rest)
    small = [small[0]] + [along_z(small[k], k) for k in range(1, parts)]
    for s in range(1, chips):
        line = jnp.concatenate([first[s - 1], along_y(rest, s)])
        arrival = line
        line = after(line, up_w)
        lines.append(line)
        partner.append(other_core(line))
    lines += partner
    diag = spread(small, parts, exp_dev)

    lines = after(tuple(lines), diag)
    inner = inner_products(lines, left, parts, rows)
    inner = [inner[0]] + [along_z(inner[k], k) for k in range(1, parts)]
    raw = raw_products(lines, gate_w, up_w)
    right = after(right, arrival)
    rights = [right] + [along_y(right, -s) for s in range(1, chips)]
    raw = after(tuple(raw), rights[1:])
    hidden, low, *lows = hidden_units(
        lines, inner, raw, diag, parts, exp_dev, pair, chips
    )
    lows = [along_y(lows[s - 1], -s) for s in range(1, chips)]
    near, far = side_by_side([low] + lows)
    bottom = turn(near, other_core(far), parts, rows)
    bottom = [bottom[0]] + [along_z(bottom[k], k) for k in range(1, parts)]

    near, far = down_products(hidden, w_down.reshape(hid, width))
    out, *others = fold(near, other_core(far), chips, rows)
    backs = [along_y(others[n], -(n // 2 + 1)) for n in range(2 * chips - 2)]
    rights += [partner_right] + [other_core(after(right, bottom[0])) for right in rights[1:]]
    own, *pieces = merge(out, rights, add_up(bottom[1:] + bottom[:1]), backs[1::2], rows)
    result = plus(own, backs[::2])
    for k in range(1, parts):
        result += along_z(pieces[k - 1], -k).astype(F32)
    return result.astype(BF)


def solution(mesh):
    count = mesh.shape
    fine = jax.sharding.Mesh(
        mesh.devices.reshape(count["groups"], count["expert"] // 2, 2, count["mp"]),
        ("groups", "y", "core", "mp"),
    )
    expert = ("y", "core")
    return jax.shard_map(
        local,
        mesh=fine,
        in_specs=(
            P(("groups", "y", "core", "mp"), None),
            P(("groups", "y", "core", "mp"), None),
            P(("groups", "y", "core", "mp"), None),
            P(expert, None, "mp"),
            P(expert, None, "mp"),
            P(expert, "mp", None),
            P(expert, None, "mp"),
            P(expert, "mp", None),
            P(expert, None, "mp"),
            P(expert, "mp", None),
            P(expert, "mp", None),
            P(expert, None, "mp"),
        ),
        out_specs=P(("groups", "y", "core", "mp"), None),
        check_vma=False,
    )
```

```python
import functools

import jax
import jax.numpy as jnp
from jax import lax
from jax.experimental import pallas as pl
from jax.experimental.pallas import tpu as pltpu
from jax.sharding import PartitionSpec as P

BF = jnp.bfloat16
F32 = jnp.float32
SMALL_LIMIT = 4 * 1024 * 1024
VMEM_LIMIT = 12 * 1024 * 1024
PIECES = 8
LONG = pl.CostEstimate(flops=1_000_000_000, bytes_accessed=1, transcendentals=0)
LONGER = pl.CostEstimate(flops=10_000_000_000, bytes_accessed=1, transcendentals=0)
LAST = pl.CostEstimate(flops=1_000_000_000, bytes_accessed=1, transcendentals=0)
SOME = pl.CostEstimate(flops=3_000_000_000, bytes_accessed=1, transcendentals=0)
TURN = pl.CostEstimate(flops=3_000_000_000, bytes_accessed=1, transcendentals=0)
BRIEF = pl.CostEstimate(flops=1, bytes_accessed=1, transcendentals=0)


def dot_nt(a, b):
    return lax.dot_general(a, b, (((1,), (1,)), ((), ())), preferred_element_type=F32)


def dot_nn(a, b):
    return lax.dot_general(a, b, (((1,), (0,)), ((), ())), preferred_element_type=F32)


def in_hbm(*values):
    return [pltpu.with_memory_space_constraint(v, pltpu.HBM) for v in values]


def after(value, earlier):
    return lax.optimization_barrier((value, earlier))[0]


def rotated(value, rows, parts, step):
    if step == 0:
        return value
    span = rows * parts
    lines = []
    for start in range(0, value.shape[0], span):
        cut = start + span - step * rows
        lines += [value[cut : start + span], value[start:cut]]
    return jnp.concatenate(lines)


def attach_kernel(tokens_ref, routes_ref, probs_ref, out_ref):
    rows, width = tokens_ref.shape
    pair = out_ref.shape[1] - width
    out_ref[:, :width] = tokens_ref[...]
    routes = routes_ref[...]
    probs = probs_ref[...]
    lane = lax.broadcasted_iota(jnp.int32, (rows, pair), 1)
    ids = jnp.where(lane < pair // 2, lane, lane - pair // 2)
    weight = jnp.zeros((rows, pair), F32)
    for k in range(routes.shape[1]):
        weight += jnp.where(ids == routes[:, k : k + 1], probs[:, k : k + 1], 0.0)
    high = weight.astype(BF).astype(F32)
    out_ref[:, width:] = jnp.where(lane < pair // 2, high, weight - high).astype(BF)


def attach(tokens, routes, probs, pair):
    rows, width = tokens.shape
    return pl.pallas_call(
        attach_kernel,
        out_shape=jax.ShapeDtypeStruct((rows, width + pair), BF),
        compiler_params=pltpu.CompilerParams(vmem_limit_bytes=SMALL_LIMIT),
        cost_estimate=BRIEF,
        name="attach",
    )(*in_hbm(tokens, routes, probs))


def piece_copies(source, target, sems):
    step = source.shape[0] // PIECES
    spans = [pl.ds(i * step, step) for i in range(PIECES)]
    return [
        pltpu.make_async_copy(source.at[span], target.at[span], sems.at[i])
        for i, span in enumerate(spans)
    ]


def load_kernel(source, target, sems):
    copies = piece_copies(source, target, sems)
    for copy in copies:
        copy.start()
    for copy in copies:
        copy.wait()


def load(weights):
    return pl.pallas_call(
        load_kernel,
        in_specs=[pl.BlockSpec(memory_space=pltpu.HBM)],
        out_specs=pl.BlockSpec(memory_space=pltpu.VMEM),
        out_shape=pltpu.VMEM(weights.shape, weights.dtype),
        scratch_shapes=[pltpu.SemaphoreType.DMA((PIECES,))],
        compiler_params=pltpu.CompilerParams(vmem_limit_bytes=SMALL_LIMIT),
        cost_estimate=SOME,
        name="load",
    )(*in_hbm(weights))


def prepare_kernel(parts, *refs):
    ins, lefts, source = refs[:3], refs[3:5], refs[5]
    target, left_ref, outs, sems = refs[6], refs[7], refs[8:-1], refs[-1]
    copies = piece_copies(source, target, sems)
    for copy in copies:
        copy.start()
    half = left_ref.shape[0] // 2
    for n, ref in enumerate(lefts):
        left_ref[n * half : (n + 1) * half] = ref[...].reshape(half, left_ref.shape[1])
    exp_dev, piece, hid = ins[0].shape
    cols = hid // parts
    me = lax.axis_index("mp")
    for n, ref in enumerate(ins):
        value = ref[...].reshape(exp_dev * piece, hid).astype(F32)
        blocks = [value[:, j * cols : (j + 1) * cols] for j in range(parts)]
        for k in range(parts):
            device = lax.rem(me + k, parts)
            block = blocks[0]
            for j in range(1, parts):
                block = jnp.where(device == j, blocks[j], block)
            outs[k][n] = block.astype(BF)
    for copy in copies:
        copy.wait()


def prepare(factors, lefts, weights, parts):
    exp_dev, piece, hid = factors[0].shape
    _, rank, block = lefts[0].shape
    vmem = pl.BlockSpec(memory_space=pltpu.VMEM)
    return pl.pallas_call(
        functools.partial(prepare_kernel, parts),
        in_specs=[vmem] * 5 + [pl.BlockSpec(memory_space=pltpu.HBM)],
        out_specs=[vmem] * (2 + parts),
        out_shape=[pltpu.VMEM(weights.shape, weights.dtype)]
        + [jax.ShapeDtypeStruct((2 * exp_dev * rank, block), BF)]
        + [jax.ShapeDtypeStruct((3, exp_dev * piece, hid // parts), BF)] * parts,
        scratch_shapes=[pltpu.SemaphoreType.DMA((PIECES,))],
        compiler_params=pltpu.CompilerParams(vmem_limit_bytes=SMALL_LIMIT),
        cost_estimate=BRIEF,
        name="prepare",
    )(*in_hbm(*factors, *lefts, weights))


def spread_kernel(parts, exp_dev, *refs):
    pieces, out_ref = refs[:-1], refs[-1]
    _, ranks, hid = out_ref.shape
    rank = ranks // exp_dev
    piece = rank // parts
    me = lax.axis_index("mp")
    row = lax.broadcasted_iota(jnp.int32, (ranks, ranks), 0)
    col = lax.broadcasted_iota(jnp.int32, (ranks, ranks), 1)
    step = lax.rem(me - row % rank // piece + parts, parts)
    source = (step * exp_dev + row // rank) * piece + row % piece
    order = (col == source).astype(F32).astype(BF)
    cols = hid // exp_dev
    place = lax.broadcasted_iota(jnp.int32, (ranks, hid), 1)
    place -= lax.broadcasted_iota(jnp.int32, (ranks, hid), 0) // rank * cols
    own = (place >= 0) & (place < cols)
    for n in range(3):
        value = dot_nn(order, jnp.concatenate([p[n].astype(F32) for p in pieces]).astype(BF))
        value = jnp.concatenate([value] * exp_dev, axis=1)
        out_ref[n] = jnp.where(own, value, 0.0).astype(BF)


def spread(pieces, parts, exp_dev):
    _, span, cols = pieces[0].shape
    return pl.pallas_call(
        functools.partial(spread_kernel, parts, exp_dev),
        out_shape=jax.ShapeDtypeStruct((3, span * parts, cols * exp_dev), BF),
        compiler_params=pltpu.CompilerParams(vmem_limit_bytes=SMALL_LIMIT),
        cost_estimate=SOME,
        name="spread",
    )(*pieces)


def inner_kernel(parts, rows, count, *refs):
    lines, left_ref, outs = refs[:count], refs[count], refs[count + 1 :]
    block = left_ref.shape[1]
    offset = pl.multiple_of(lax.axis_index("mp") * block, 128)
    x = jnp.concatenate([line[:, pl.ds(offset, block)] for line in lines])
    value = dot_nt(x, left_ref[...])
    for k in range(parts):
        outs[k][...] = rotated(value, rows, parts, k).astype(BF)


def inner_products(lines, left, parts, rows):
    total = sum(line.shape[0] for line in lines)
    ranks = left.shape[0]
    return pl.pallas_call(
        functools.partial(inner_kernel, parts, rows, len(lines)),
        out_shape=[jax.ShapeDtypeStruct((total, ranks), BF)] * parts,
        compiler_params=pltpu.CompilerParams(vmem_limit_bytes=VMEM_LIMIT),
        cost_estimate=BRIEF,
        name="inner",
    )(*lines, left)


def raw_kernel(count, tile, *refs):
    lines, (gate_w, up_w, gate_ref, up_ref) = refs[:count], refs[count:]
    hid, width = gate_w.shape
    x = jnp.concatenate([line[:, :width] for line in lines])
    for i in range(hid // tile):
        span = pl.ds(i * tile, tile)
        gate_ref[:, span] = dot_nt(gate_w[span], x).T
        up_ref[:, span] = dot_nt(up_w[span], x).T


def raw_products(lines, gate_w, up_w):
    hid = gate_w.shape[0]
    total = sum(line.shape[0] for line in lines)
    tile = 384
    return pl.pallas_call(
        functools.partial(raw_kernel, len(lines), tile),
        out_shape=[jax.ShapeDtypeStruct((total, hid), F32)] * 2,
        compiler_params=pltpu.CompilerParams(vmem_limit_bytes=VMEM_LIMIT),
        cost_estimate=BRIEF,
        name="raw",
    )(*lines, gate_w, up_w)


def hidden_kernel(parts, count, exp_dev, pair, *refs):
    lines, inner, rest = refs[:count], refs[count : count + parts], refs[count + parts :]
    gate_ref, up_ref, diag_ref, hidden_ref = rest[:4]
    outs = rest[4:]
    hid = gate_ref.shape[1]
    ranks = diag_ref.shape[1]
    wide = lines[0].shape[1] - pair
    total = sum(ref[...].astype(F32) for ref in inner).astype(BF)
    gate = gate_ref[...] + dot_nn(total[:, :ranks], diag_ref[0])
    up = up_ref[...] + dot_nn(total[:, ranks:], diag_ref[1])
    lane = lax.broadcasted_iota(jnp.int32, (pair, hid), 0)
    lane = jnp.where(lane < pair // 2, lane, lane - pair // 2)
    cols = hid // exp_dev
    first = (lax.axis_index("y") * 2 + lax.axis_index("core")) * exp_dev
    place = lax.broadcasted_iota(jnp.int32, (pair, hid), 1) - (lane - first) * cols
    pick = ((place >= 0) & (place < cols)).astype(F32).astype(BF)
    scale = dot_nn(jnp.concatenate([line[:, wide:] for line in lines]), pick)
    hidden = (gate / (1.0 + jnp.exp(-gate)) * up * scale).astype(BF)
    hidden_ref[...] = hidden
    value = dot_nt(hidden, diag_ref[2])
    chips = len(outs)
    span = value.shape[0] // (2 * chips)
    for n, out_ref in enumerate(outs):
        rows = [value[i * span : (i + 1) * span] for i in (n, n + chips)]
        out_ref[...] = jnp.concatenate(rows).astype(BF)


def hidden_units(lines, inner, raw, diag, parts, exp_dev, pair, chips):
    total, hid = raw[0].shape
    ranks = diag.shape[1]
    return pl.pallas_call(
        functools.partial(hidden_kernel, parts, len(lines), exp_dev, pair),
        out_shape=[jax.ShapeDtypeStruct((total, hid), BF)]
        + [jax.ShapeDtypeStruct((total // chips, ranks), BF)] * chips,
        compiler_params=pltpu.CompilerParams(vmem_limit_bytes=VMEM_LIMIT),
        cost_estimate=BRIEF,
        name="hidden",
    )(*lines, *inner, *raw, diag)


def down_kernel(hidden_ref, down_ref, near_ref, far_ref):
    near, width = near_ref.shape
    hidden = hidden_ref[...]
    tile = min(1024, width)
    for i in range(width // tile):
        span = slice(i * tile, (i + 1) * tile)
        value = dot_nn(hidden, down_ref[:, span])
        near_ref[:, span] = value[:near]
        far_ref[:, span] = value[near:].astype(BF)


def down_products(hidden, down_w):
    total, width = hidden.shape[0], down_w.shape[1]
    return pl.pallas_call(
        down_kernel,
        out_shape=[
            jax.ShapeDtypeStruct((total // 2, width), F32),
            jax.ShapeDtypeStruct((total // 2, width), BF),
        ],
        compiler_params=pltpu.CompilerParams(vmem_limit_bytes=VMEM_LIMIT),
        cost_estimate=BRIEF,
        name="down",
    )(hidden, down_w)


def pair_kernel(*refs):
    ins, (near_ref, far_ref) = refs[:-2], refs[-2:]
    value = jnp.concatenate([ref[...].astype(F32) for ref in ins], axis=1)
    span = near_ref.shape[0]
    near_ref[...] = value[:span].astype(BF)
    far_ref[...] = value[span:].astype(BF)


def side_by_side(lines):
    total, ranks = lines[0].shape
    return pl.pallas_call(
        pair_kernel,
        out_shape=[jax.ShapeDtypeStruct((total // 2, len(lines) * ranks), BF)] * 2,
        compiler_params=pltpu.CompilerParams(vmem_limit_bytes=SMALL_LIMIT),
        cost_estimate=LONGER,
        name="pair",
    )(*lines)


def turn_kernel(rows, near_ref, far_ref, *outs):
    value = jnp.concatenate([near_ref[...].astype(F32), far_ref[...].astype(F32)], axis=1)
    for k, out_ref in enumerate(outs):
        out_ref[...] = rotated(value, rows, len(outs), k).astype(BF)


def turn(near, far, parts, rows):
    span, ranks = near.shape
    return pl.pallas_call(
        functools.partial(turn_kernel, rows),
        out_shape=[jax.ShapeDtypeStruct((span, 2 * ranks), BF)] * parts,
        compiler_params=pltpu.CompilerParams(vmem_limit_bytes=SMALL_LIMIT),
        cost_estimate=TURN,
        name="turn",
    )(near, far)


def add_up_kernel(*refs):
    refs[-1][...] = sum(ref[...].astype(F32) for ref in refs[:-1]).astype(BF)


def add_up(pieces):
    return pl.pallas_call(
        add_up_kernel,
        out_shape=jax.ShapeDtypeStruct(pieces[0].shape, BF),
        compiler_params=pltpu.CompilerParams(vmem_limit_bytes=SMALL_LIMIT),
        cost_estimate=LONG,
        name="add_up",
    )(*pieces)


def fold_kernel(head, near_ref, far_ref, own_ref, *out_refs):
    span = own_ref.shape[0]
    total = near_ref[...] + far_ref[...].astype(F32)
    own_ref[...] = total[:span]
    for n in range(len(out_refs) // 2):
        line = total[(n + 1) * span : (n + 2) * span]
        out_refs[2 * n][...] = line[:head].astype(BF)
        out_refs[2 * n + 1][...] = line[head:].astype(BF)


def fold(near, far, chips, head):
    total, width = near.shape
    span = total // chips
    return pl.pallas_call(
        functools.partial(fold_kernel, head),
        out_shape=[jax.ShapeDtypeStruct((span, width), F32)]
        + [jax.ShapeDtypeStruct((rows, width), BF) for rows in (head, span - head)]
        * (chips - 1),
        compiler_params=pltpu.CompilerParams(vmem_limit_bytes=VMEM_LIMIT),
        cost_estimate=BRIEF,
        name="fold",
    )(near, far)


def merge_kernel(chips, parts, *refs):
    own_ref, rights, refs = refs[0], refs[1 : 1 + 2 * chips], refs[1 + 2 * chips :]
    low, backs, outs = refs[0][...], refs[1:-parts], refs[-parts:]
    rows = outs[0].shape[0]
    ranks, block = rights[0].shape
    offset = pl.multiple_of(lax.axis_index("mp") * block, 128)
    value = jnp.zeros((low.shape[0], block), F32)
    for n, ref in enumerate(rights):
        value += dot_nn(low[:, n * ranks : (n + 1) * ranks], ref[...])
    total = own_ref[...]
    value += own_ref[:, pl.ds(offset, block)]
    rest, rest_value = total[rows:], value[rows:]
    for ref in backs:
        rest += ref[...].astype(F32)
        rest_value += ref[:, pl.ds(offset, block)].astype(F32)
    outs[0][...] = total[:rows]
    outs[0][:, pl.ds(offset, block)] = value[:rows]
    for k in range(1, parts):
        span = slice((k - 1) * rows, k * rows)
        outs[k][...] = rest[span].astype(BF)
        outs[k][:, pl.ds(offset, block)] = rest_value[span].astype(BF)


def plus_kernel(own_ref, *refs):
    total = own_ref[...]
    for ref in refs[:-1]:
        total += ref[...].astype(F32)
    refs[-1][...] = total


def plus(own, pieces):
    return pl.pallas_call(
        plus_kernel,
        out_shape=jax.ShapeDtypeStruct(own.shape, F32),
        compiler_params=pltpu.CompilerParams(vmem_limit_bytes=SMALL_LIMIT),
        cost_estimate=LAST,
        name="plus",
    )(own, *pieces)


def merge(own, rights, low, backs, rows):
    total, width = own.shape
    parts = total // rows
    return pl.pallas_call(
        functools.partial(merge_kernel, len(rights) // 2, parts),
        out_shape=[jax.ShapeDtypeStruct((rows, width), F32)]
        + [jax.ShapeDtypeStruct((rows, width), BF)] * (parts - 1),
        compiler_params=pltpu.CompilerParams(vmem_limit_bytes=VMEM_LIMIT),
        cost_estimate=BRIEF,
        name="merge",
    )(own, *rights, low, *backs)


def local(
    tokens,
    routes,
    probs,
    w_gate,
    w_up,
    w_down,
    gate_left,
    gate_right,
    up_left,
    up_right,
    down_left,
    down_right,
):
    rows, width = tokens.shape
    exp_dev, _, cols = w_gate.shape
    rank = gate_left.shape[1]
    block = gate_left.shape[2]
    parts = lax.axis_size("mp")
    chips = lax.axis_size("y")
    experts = exp_dev * chips * 2
    ranks = exp_dev * rank
    hid = exp_dev * cols

    def along_z(value, step):
        return lax.ppermute(value, "mp", [(i, (i + step) % parts) for i in range(parts)])

    def along_y(value, step):
        return lax.ppermute(value, "y", [(i, (i + step) % chips) for i in range(chips)])

    def other_core(value):
        return lax.ppermute(value, "core", [(0, 1), (1, 0)])

    pair = 2 * (-(-experts // 64) * 64)
    sent = attach(tokens, routes, probs, pair)
    arrived = [along_z(sent, k) for k in range(1, parts)]
    first = [along_y(sent, s) for s in range(1, chips)]
    gate_w, up_w = (jnp.swapaxes(w, 1, 2).reshape(hid, width) for w in (w_gate, w_up))
    gate_w, left, *small = prepare(
        (gate_right, up_right, down_left), (gate_left, up_left), gate_w, parts
    )
    right = down_right.reshape(ranks, block)
    partner_right = other_core(right)
    rest = after(jnp.concatenate(arrived), (left, small, gate_w, partner_right))
    up_w = load(after(up_w, rest))
    lines = [jnp.concatenate([sent, rest])]
    partner = [other_core(lines[0])]
    small = after(tuple(small), rest)
    small = [small[0]] + [along_z(small[k], k) for k in range(1, parts)]
    for s in range(1, chips):
        line = jnp.concatenate([first[s - 1], along_y(rest, s)])
        arrival = line
        line = after(line, up_w)
        lines.append(line)
        partner.append(other_core(line))
    lines += partner
    diag = spread(small, parts, exp_dev)

    lines = after(tuple(lines), diag)
    inner = inner_products(lines, left, parts, rows)
    inner = [inner[0]] + [along_z(inner[k], k) for k in range(1, parts)]
    raw = raw_products(lines, gate_w, up_w)
    right = after(right, arrival)
    rights = [right] + [along_y(right, -s) for s in range(1, chips)]
    raw = after(tuple(raw), rights[1:])
    hidden, low, *lows = hidden_units(
        lines, inner, raw, diag, parts, exp_dev, pair, chips
    )
    lows = [along_y(lows[s - 1], -s) for s in range(1, chips)]
    near, far = side_by_side([low] + lows)
    bottom = turn(near, other_core(far), parts, rows)
    bottom = [bottom[0]] + [along_z(bottom[k], k) for k in range(1, parts)]

    near, far = down_products(hidden, w_down.reshape(hid, width))
    out, *others = fold(near, other_core(far), chips, rows)
    backs = [along_y(others[n], -(n // 2 + 1)) for n in range(2 * chips - 2)]
    rights += [partner_right] + [other_core(after(right, out)) for right in rights[1:]]
    own, *pieces = merge(out, rights, add_up(bottom[1:] + bottom[:1]), backs[1::2], rows)
    result = plus(own, backs[::2])
    for k in range(1, parts):
        result += along_z(pieces[k - 1], -k).astype(F32)
    return result.astype(BF)


def solution(mesh):
    count = mesh.shape
    fine = jax.sharding.Mesh(
        mesh.devices.reshape(count["groups"], count["expert"] // 2, 2, count["mp"]),
        ("groups", "y", "core", "mp"),
    )
    expert = ("y", "core")
    return jax.shard_map(
        local,
        mesh=fine,
        in_specs=(
            P(("groups", "y", "core", "mp"), None),
            P(("groups", "y", "core", "mp"), None),
            P(("groups", "y", "core", "mp"), None),
            P(expert, None, "mp"),
            P(expert, None, "mp"),
            P(expert, "mp", None),
            P(expert, None, "mp"),
            P(expert, "mp", None),
            P(expert, None, "mp"),
            P(expert, "mp", None),
            P(expert, "mp", None),
            P(expert, None, "mp"),
        ),
        out_specs=P(("groups", "y", "core", "mp"), None),
        check_vma=False,
    )
```

```python
import functools

import jax
import jax.numpy as jnp
from jax import lax
from jax.experimental import pallas as pl
from jax.experimental.pallas import tpu as pltpu
from jax.sharding import PartitionSpec as P

BF = jnp.bfloat16
F32 = jnp.float32
SMALL_LIMIT = 4 * 1024 * 1024
VMEM_LIMIT = 12 * 1024 * 1024
PIECES = 8
FIRST = 128
LONG = pl.CostEstimate(flops=1_000_000_000, bytes_accessed=1, transcendentals=0)
LONGER = pl.CostEstimate(flops=10_000_000_000, bytes_accessed=1, transcendentals=0)
LAST = pl.CostEstimate(flops=1_000_000_000, bytes_accessed=1, transcendentals=0)
SOME = pl.CostEstimate(flops=3_000_000_000, bytes_accessed=1, transcendentals=0)
TURN = pl.CostEstimate(flops=3_000_000_000, bytes_accessed=1, transcendentals=0)
BRIEF = pl.CostEstimate(flops=1, bytes_accessed=1, transcendentals=0)


def dot_nt(a, b):
    return lax.dot_general(a, b, (((1,), (1,)), ((), ())), preferred_element_type=F32)


def dot_nn(a, b):
    return lax.dot_general(a, b, (((1,), (0,)), ((), ())), preferred_element_type=F32)


def in_hbm(*values):
    return [pltpu.with_memory_space_constraint(v, pltpu.HBM) for v in values]


def after(value, earlier):
    return lax.optimization_barrier((value, earlier))[0]


def rotated(value, rows, parts, step):
    if step == 0:
        return value
    span = rows * parts
    lines = []
    for start in range(0, value.shape[0], span):
        cut = start + span - step * rows
        lines += [value[cut : start + span], value[start:cut]]
    return jnp.concatenate(lines)


def attach_kernel(tokens_ref, routes_ref, probs_ref, out_ref):
    rows, width = tokens_ref.shape
    pair = out_ref.shape[1] - width
    out_ref[:, :width] = tokens_ref[...]
    routes = routes_ref[...]
    probs = probs_ref[...]
    lane = lax.broadcasted_iota(jnp.int32, (rows, pair), 1)
    ids = jnp.where(lane < pair // 2, lane, lane - pair // 2)
    weight = jnp.zeros((rows, pair), F32)
    for k in range(routes.shape[1]):
        weight += jnp.where(ids == routes[:, k : k + 1], probs[:, k : k + 1], 0.0)
    high = weight.astype(BF).astype(F32)
    out_ref[:, width:] = jnp.where(lane < pair // 2, high, weight - high).astype(BF)


def attach(tokens, routes, probs, pair):
    rows, width = tokens.shape
    return pl.pallas_call(
        attach_kernel,
        out_shape=jax.ShapeDtypeStruct((rows, width + pair), BF),
        compiler_params=pltpu.CompilerParams(vmem_limit_bytes=SMALL_LIMIT),
        cost_estimate=BRIEF,
        name="attach",
    )(*in_hbm(tokens, routes, probs))


def piece_copies(source, target, sems, skip=0):
    step = target.shape[0] // PIECES
    return [
        pltpu.make_async_copy(
            source.at[pl.ds(skip + i * step, step)],
            target.at[pl.ds(i * step, step)],
            sems.at[i],
        )
        for i in range(PIECES)
    ]


def load_kernel(source, target, sems):
    copies = piece_copies(source, target, sems, source.shape[0] - target.shape[0])
    for copy in copies:
        copy.start()
    for copy in copies:
        copy.wait()


def load(weights):
    return pl.pallas_call(
        load_kernel,
        in_specs=[pl.BlockSpec(memory_space=pltpu.HBM)],
        out_specs=pl.BlockSpec(memory_space=pltpu.VMEM),
        out_shape=pltpu.VMEM((weights.shape[0] - FIRST, weights.shape[1]), weights.dtype),
        scratch_shapes=[pltpu.SemaphoreType.DMA((PIECES,))],
        compiler_params=pltpu.CompilerParams(vmem_limit_bytes=SMALL_LIMIT),
        cost_estimate=SOME,
        name="load",
    )(*in_hbm(weights))


def prepare_kernel(parts, *refs):
    ins, lefts, sources = refs[:3], refs[3:5], refs[5:7]
    targets, left_ref, outs, sems = refs[7:9], refs[9], refs[10:-1], refs[-1]
    copies = piece_copies(sources[0], targets[0], sems)
    copies.append(
        pltpu.make_async_copy(sources[1].at[pl.ds(0, FIRST)], targets[1], sems.at[PIECES])
    )
    for copy in copies:
        copy.start()
    half = left_ref.shape[0] // 2
    for n, ref in enumerate(lefts):
        left_ref[n * half : (n + 1) * half] = ref[...].reshape(half, left_ref.shape[1])
    exp_dev, piece, hid = ins[0].shape
    cols = hid // parts
    me = lax.axis_index("mp")
    for n, ref in enumerate(ins):
        value = ref[...].reshape(exp_dev * piece, hid).astype(F32)
        blocks = [value[:, j * cols : (j + 1) * cols] for j in range(parts)]
        for k in range(parts):
            device = lax.rem(me + k, parts)
            block = blocks[0]
            for j in range(1, parts):
                block = jnp.where(device == j, blocks[j], block)
            outs[k][n] = block.astype(BF)
    for copy in copies:
        copy.wait()


def prepare(factors, lefts, weights, parts):
    exp_dev, piece, hid = factors[0].shape
    _, rank, block = lefts[0].shape
    vmem = pl.BlockSpec(memory_space=pltpu.VMEM)
    return pl.pallas_call(
        functools.partial(prepare_kernel, parts),
        in_specs=[vmem] * 5 + [pl.BlockSpec(memory_space=pltpu.HBM)] * 2,
        out_specs=[vmem] * (3 + parts),
        out_shape=[
            pltpu.VMEM(weights[0].shape, BF),
            pltpu.VMEM((FIRST, weights[1].shape[1]), BF),
        ]
        + [jax.ShapeDtypeStruct((2 * exp_dev * rank, block), BF)]
        + [jax.ShapeDtypeStruct((3, exp_dev * piece, hid // parts), BF)] * parts,
        scratch_shapes=[pltpu.SemaphoreType.DMA((PIECES + 1,))],
        compiler_params=pltpu.CompilerParams(vmem_limit_bytes=SMALL_LIMIT),
        cost_estimate=BRIEF,
        name="prepare",
    )(*in_hbm(*factors, *lefts, *weights))


def spread_kernel(parts, exp_dev, *refs):
    pieces, out_ref = refs[:-1], refs[-1]
    _, ranks, hid = out_ref.shape
    rank = ranks // exp_dev
    piece = rank // parts
    me = lax.axis_index("mp")
    row = lax.broadcasted_iota(jnp.int32, (ranks, ranks), 0)
    col = lax.broadcasted_iota(jnp.int32, (ranks, ranks), 1)
    step = lax.rem(me - row % rank // piece + parts, parts)
    source = (step * exp_dev + row // rank) * piece + row % piece
    order = (col == source).astype(F32).astype(BF)
    cols = hid // exp_dev
    place = lax.broadcasted_iota(jnp.int32, (ranks, hid), 1)
    place -= lax.broadcasted_iota(jnp.int32, (ranks, hid), 0) // rank * cols
    own = (place >= 0) & (place < cols)
    for n in range(3):
        value = dot_nn(order, jnp.concatenate([p[n].astype(F32) for p in pieces]).astype(BF))
        value = jnp.concatenate([value] * exp_dev, axis=1)
        out_ref[n] = jnp.where(own, value, 0.0).astype(BF)


def spread(pieces, parts, exp_dev):
    _, span, cols = pieces[0].shape
    return pl.pallas_call(
        functools.partial(spread_kernel, parts, exp_dev),
        out_shape=jax.ShapeDtypeStruct((3, span * parts, cols * exp_dev), BF),
        compiler_params=pltpu.CompilerParams(vmem_limit_bytes=SMALL_LIMIT),
        cost_estimate=SOME,
        name="spread",
    )(*pieces)


def inner_kernel(parts, rows, count, *refs):
    lines, left_ref, outs = refs[:count], refs[count], refs[count + 1 :]
    block = left_ref.shape[1]
    offset = pl.multiple_of(lax.axis_index("mp") * block, 128)
    x = jnp.concatenate([line[:, pl.ds(offset, block)] for line in lines])
    value = dot_nt(x, left_ref[...])
    for k in range(parts):
        outs[k][...] = rotated(value, rows, parts, k).astype(BF)


def inner_products(lines, left, parts, rows):
    total = sum(line.shape[0] for line in lines)
    ranks = left.shape[0]
    return pl.pallas_call(
        functools.partial(inner_kernel, parts, rows, len(lines)),
        out_shape=[jax.ShapeDtypeStruct((total, ranks), BF)] * parts,
        compiler_params=pltpu.CompilerParams(vmem_limit_bytes=VMEM_LIMIT),
        cost_estimate=BRIEF,
        name="inner",
    )(*lines, left)


def raw_kernel(count, tile, *refs):
    lines, (gate_w, up_first, up_w, gate_ref, up_ref) = refs[:count], refs[count:]
    hid, width = gate_w.shape
    x = jnp.concatenate([line[:, :width] for line in lines])
    for i in range(hid // tile):
        span = pl.ds(i * tile, tile)
        gate_ref[:, span] = dot_nt(gate_w[span], x).T
    up_ref[:, :FIRST] = dot_nt(up_first[...], x).T
    up_ref[:, FIRST:] = dot_nt(up_w[...], x).T


def raw_products(lines, gate_w, up_first, up_w):
    hid = gate_w.shape[0]
    total = sum(line.shape[0] for line in lines)
    tile = 384
    return pl.pallas_call(
        functools.partial(raw_kernel, len(lines), tile),
        out_shape=[jax.ShapeDtypeStruct((total, hid), F32)] * 2,
        compiler_params=pltpu.CompilerParams(vmem_limit_bytes=VMEM_LIMIT),
        cost_estimate=BRIEF,
        name="raw",
    )(*lines, gate_w, up_first, up_w)


def hidden_kernel(parts, count, exp_dev, pair, *refs):
    lines, inner, rest = refs[:count], refs[count : count + parts], refs[count + parts :]
    gate_ref, up_ref, diag_ref, hidden_ref = rest[:4]
    outs = rest[4:]
    hid = gate_ref.shape[1]
    ranks = diag_ref.shape[1]
    wide = lines[0].shape[1] - pair
    total = sum(ref[...].astype(F32) for ref in inner).astype(BF)
    gate = gate_ref[...] + dot_nn(total[:, :ranks], diag_ref[0])
    up = up_ref[...] + dot_nn(total[:, ranks:], diag_ref[1])
    lane = lax.broadcasted_iota(jnp.int32, (pair, hid), 0)
    lane = jnp.where(lane < pair // 2, lane, lane - pair // 2)
    cols = hid // exp_dev
    first = (lax.axis_index("y") * 2 + lax.axis_index("core")) * exp_dev
    place = lax.broadcasted_iota(jnp.int32, (pair, hid), 1) - (lane - first) * cols
    pick = ((place >= 0) & (place < cols)).astype(F32).astype(BF)
    scale = dot_nn(jnp.concatenate([line[:, wide:] for line in lines]), pick)
    hidden = (gate / (1.0 + jnp.exp(-gate)) * up * scale).astype(BF)
    hidden_ref[...] = hidden
    value = dot_nt(hidden, diag_ref[2])
    chips = len(outs)
    span = value.shape[0] // (2 * chips)
    for n, out_ref in enumerate(outs):
        rows = [value[i * span : (i + 1) * span] for i in (n, n + chips)]
        out_ref[...] = jnp.concatenate(rows).astype(BF)


def hidden_units(lines, inner, raw, diag, parts, exp_dev, pair, chips):
    total, hid = raw[0].shape
    ranks = diag.shape[1]
    return pl.pallas_call(
        functools.partial(hidden_kernel, parts, len(lines), exp_dev, pair),
        out_shape=[jax.ShapeDtypeStruct((total, hid), BF)]
        + [jax.ShapeDtypeStruct((total // chips, ranks), BF)] * chips,
        compiler_params=pltpu.CompilerParams(vmem_limit_bytes=VMEM_LIMIT),
        cost_estimate=BRIEF,
        name="hidden",
    )(*lines, *inner, *raw, diag)


def down_kernel(hidden_ref, down_ref, near_ref, far_ref):
    near, width = near_ref.shape
    hidden = hidden_ref[...]
    tile = min(1024, width)
    for i in range(width // tile):
        span = slice(i * tile, (i + 1) * tile)
        value = dot_nn(hidden, down_ref[:, span])
        near_ref[:, span] = value[:near]
        far_ref[:, span] = value[near:].astype(BF)


def down_products(hidden, down_w):
    total, width = hidden.shape[0], down_w.shape[1]
    return pl.pallas_call(
        down_kernel,
        out_shape=[
            jax.ShapeDtypeStruct((total // 2, width), F32),
            jax.ShapeDtypeStruct((total // 2, width), BF),
        ],
        compiler_params=pltpu.CompilerParams(vmem_limit_bytes=VMEM_LIMIT),
        cost_estimate=BRIEF,
        name="down",
    )(hidden, down_w)


def pair_kernel(*refs):
    ins, (near_ref, far_ref) = refs[:-2], refs[-2:]
    value = jnp.concatenate([ref[...].astype(F32) for ref in ins], axis=1)
    span = near_ref.shape[0]
    near_ref[...] = value[:span].astype(BF)
    far_ref[...] = value[span:].astype(BF)


def side_by_side(lines):
    total, ranks = lines[0].shape
    return pl.pallas_call(
        pair_kernel,
        out_shape=[jax.ShapeDtypeStruct((total // 2, len(lines) * ranks), BF)] * 2,
        compiler_params=pltpu.CompilerParams(vmem_limit_bytes=SMALL_LIMIT),
        cost_estimate=LONGER,
        name="pair",
    )(*lines)


def turn_kernel(rows, near_ref, far_ref, *outs):
    value = jnp.concatenate([near_ref[...].astype(F32), far_ref[...].astype(F32)], axis=1)
    for k, out_ref in enumerate(outs):
        out_ref[...] = rotated(value, rows, len(outs), k).astype(BF)


def turn(near, far, parts, rows):
    span, ranks = near.shape
    return pl.pallas_call(
        functools.partial(turn_kernel, rows),
        out_shape=[jax.ShapeDtypeStruct((span, 2 * ranks), BF)] * parts,
        compiler_params=pltpu.CompilerParams(vmem_limit_bytes=SMALL_LIMIT),
        cost_estimate=TURN,
        name="turn",
    )(near, far)


def add_up_kernel(*refs):
    refs[-1][...] = sum(ref[...].astype(F32) for ref in refs[:-1]).astype(BF)


def add_up(pieces):
    return pl.pallas_call(
        add_up_kernel,
        out_shape=jax.ShapeDtypeStruct(pieces[0].shape, BF),
        compiler_params=pltpu.CompilerParams(vmem_limit_bytes=SMALL_LIMIT),
        cost_estimate=LONG,
        name="add_up",
    )(*pieces)


def fold_kernel(head, near_ref, far_ref, own_ref, *out_refs):
    span = own_ref.shape[0]
    total = near_ref[...] + far_ref[...].astype(F32)
    own_ref[...] = total[:span]
    for n in range(len(out_refs) // 2):
        line = total[(n + 1) * span : (n + 2) * span]
        out_refs[2 * n][...] = line[:head].astype(BF)
        out_refs[2 * n + 1][...] = line[head:].astype(BF)


def fold(near, far, chips, head):
    total, width = near.shape
    span = total // chips
    return pl.pallas_call(
        functools.partial(fold_kernel, head),
        out_shape=[jax.ShapeDtypeStruct((span, width), F32)]
        + [jax.ShapeDtypeStruct((rows, width), BF) for rows in (head, span - head)]
        * (chips - 1),
        compiler_params=pltpu.CompilerParams(vmem_limit_bytes=VMEM_LIMIT),
        cost_estimate=BRIEF,
        name="fold",
    )(near, far)


def merge_kernel(chips, parts, *refs):
    own_ref, rights, refs = refs[0], refs[1 : 1 + 2 * chips], refs[1 + 2 * chips :]
    low, backs, outs = refs[0][...], refs[1:-parts], refs[-parts:]
    rows = outs[0].shape[0]
    ranks, block = rights[0].shape
    offset = pl.multiple_of(lax.axis_index("mp") * block, 128)
    value = jnp.zeros((low.shape[0], block), F32)
    for n, ref in enumerate(rights):
        value += dot_nn(low[:, n * ranks : (n + 1) * ranks], ref[...])
    total = own_ref[...]
    value += own_ref[:, pl.ds(offset, block)]
    rest, rest_value = total[rows:], value[rows:]
    for ref in backs:
        rest += ref[...].astype(F32)
        rest_value += ref[:, pl.ds(offset, block)].astype(F32)
    outs[0][...] = total[:rows]
    outs[0][:, pl.ds(offset, block)] = value[:rows]
    for k in range(1, parts):
        span = slice((k - 1) * rows, k * rows)
        outs[k][...] = rest[span].astype(BF)
        outs[k][:, pl.ds(offset, block)] = rest_value[span].astype(BF)


def plus_kernel(own_ref, *refs):
    total = own_ref[...]
    for ref in refs[:-1]:
        total += ref[...].astype(F32)
    refs[-1][...] = total


def plus(own, pieces):
    return pl.pallas_call(
        plus_kernel,
        out_shape=jax.ShapeDtypeStruct(own.shape, F32),
        compiler_params=pltpu.CompilerParams(vmem_limit_bytes=SMALL_LIMIT),
        cost_estimate=LAST,
        name="plus",
    )(own, *pieces)


def merge(own, rights, low, backs, rows):
    total, width = own.shape
    parts = total // rows
    return pl.pallas_call(
        functools.partial(merge_kernel, len(rights) // 2, parts),
        out_shape=[jax.ShapeDtypeStruct((rows, width), F32)]
        + [jax.ShapeDtypeStruct((rows, width), BF)] * (parts - 1),
        compiler_params=pltpu.CompilerParams(vmem_limit_bytes=VMEM_LIMIT),
        cost_estimate=BRIEF,
        name="merge",
    )(own, *rights, low, *backs)


def local(
    tokens,
    routes,
    probs,
    w_gate,
    w_up,
    w_down,
    gate_left,
    gate_right,
    up_left,
    up_right,
    down_left,
    down_right,
):
    rows, width = tokens.shape
    exp_dev, _, cols = w_gate.shape
    rank = gate_left.shape[1]
    block = gate_left.shape[2]
    parts = lax.axis_size("mp")
    chips = lax.axis_size("y")
    experts = exp_dev * chips * 2
    ranks = exp_dev * rank
    hid = exp_dev * cols

    def along_z(value, step):
        return lax.ppermute(value, "mp", [(i, (i + step) % parts) for i in range(parts)])

    def along_y(value, step):
        return lax.ppermute(value, "y", [(i, (i + step) % chips) for i in range(chips)])

    def other_core(value):
        return lax.ppermute(value, "core", [(0, 1), (1, 0)])

    pair = 2 * (-(-experts // 64) * 64)
    sent = attach(tokens, routes, probs, pair)
    arrived = [along_z(sent, k) for k in range(1, parts)]
    first = [along_y(sent, s) for s in range(1, chips)]
    gate_w, up_w = (jnp.swapaxes(w, 1, 2).reshape(hid, width) for w in (w_gate, w_up))
    gate_w, up_first, left, *small = prepare(
        (gate_right, up_right, down_left), (gate_left, up_left), (gate_w, up_w), parts
    )
    right = down_right.reshape(ranks, block)
    partner_right = other_core(right)
    rest = after(jnp.concatenate(arrived), (left, small, gate_w, up_first, partner_right))
    up_w = load(after(up_w, rest))
    lines = [jnp.concatenate([sent, rest])]
    partner = [other_core(lines[0])]
    small = after(tuple(small), rest)
    small = [small[0]] + [along_z(small[k], k) for k in range(1, parts)]
    for s in range(1, chips):
        line = jnp.concatenate([first[s - 1], along_y(rest, s)])
        arrival = line
        line = after(line, up_w)
        lines.append(line)
        partner.append(other_core(line))
    lines += partner
    diag = spread(small, parts, exp_dev)

    lines = after(tuple(lines), diag)
    inner = inner_products(lines, left, parts, rows)
    inner = [inner[0]] + [along_z(inner[k], k) for k in range(1, parts)]
    raw = raw_products(lines, gate_w, up_first, up_w)
    right = after(right, arrival)
    rights = [right] + [along_y(right, -s) for s in range(1, chips)]
    raw = after(tuple(raw), rights[1:])
    hidden, low, *lows = hidden_units(
        lines, inner, raw, diag, parts, exp_dev, pair, chips
    )
    lows = [along_y(lows[s - 1], -s) for s in range(1, chips)]
    near, far = side_by_side([low] + lows)
    bottom = turn(near, other_core(far), parts, rows)
    bottom = [bottom[0]] + [along_z(bottom[k], k) for k in range(1, parts)]

    near, far = down_products(hidden, w_down.reshape(hid, width))
    out, *others = fold(near, other_core(far), chips, rows)
    backs = [along_y(others[n], -(n // 2 + 1)) for n in range(2 * chips - 2)]
    rights += [partner_right] + [other_core(after(right, out)) for right in rights[1:]]
    own, *pieces = merge(out, rights, add_up(bottom[1:] + bottom[:1]), backs[1::2], rows)
    result = plus(own, backs[::2])
    for k in range(1, parts):
        result += along_z(pieces[k - 1], -k).astype(F32)
    return result.astype(BF)


def solution(mesh):
    count = mesh.shape
    fine = jax.sharding.Mesh(
        mesh.devices.reshape(count["groups"], count["expert"] // 2, 2, count["mp"]),
        ("groups", "y", "core", "mp"),
    )
    expert = ("y", "core")
    return jax.shard_map(
        local,
        mesh=fine,
        in_specs=(
            P(("groups", "y", "core", "mp"), None),
            P(("groups", "y", "core", "mp"), None),
            P(("groups", "y", "core", "mp"), None),
            P(expert, None, "mp"),
            P(expert, None, "mp"),
            P(expert, "mp", None),
            P(expert, None, "mp"),
            P(expert, "mp", None),
            P(expert, None, "mp"),
            P(expert, "mp", None),
            P(expert, "mp", None),
            P(expert, None, "mp"),
        ),
        out_specs=P(("groups", "y", "core", "mp"), None),
        check_vma=False,
    )
```

```python
import functools

import jax
import jax.numpy as jnp
from jax import lax
from jax.experimental import pallas as pl
from jax.experimental.pallas import tpu as pltpu
from jax.sharding import PartitionSpec as P

BF = jnp.bfloat16
F32 = jnp.float32
SMALL_LIMIT = 4 * 1024 * 1024
VMEM_LIMIT = 12 * 1024 * 1024
PIECES = 8
LONG = pl.CostEstimate(flops=1_000_000_000, bytes_accessed=1, transcendentals=0)
LONGER = pl.CostEstimate(flops=10_000_000_000, bytes_accessed=1, transcendentals=0)
LAST = pl.CostEstimate(flops=1_000_000_000, bytes_accessed=1, transcendentals=0)
SOME = pl.CostEstimate(flops=3_000_000_000, bytes_accessed=1, transcendentals=0)
TURN = pl.CostEstimate(flops=3_000_000_000, bytes_accessed=1, transcendentals=0)
BRIEF = pl.CostEstimate(flops=1, bytes_accessed=1, transcendentals=0)


def dot_nt(a, b):
    return lax.dot_general(a, b, (((1,), (1,)), ((), ())), preferred_element_type=F32)


def dot_nn(a, b):
    return lax.dot_general(a, b, (((1,), (0,)), ((), ())), preferred_element_type=F32)


def in_hbm(*values):
    return [pltpu.with_memory_space_constraint(v, pltpu.HBM) for v in values]


def after(value, earlier):
    return lax.optimization_barrier((value, earlier))[0]


def rotated(value, rows, parts, step):
    if step == 0:
        return value
    span = rows * parts
    lines = []
    for start in range(0, value.shape[0], span):
        cut = start + span - step * rows
        lines += [value[cut : start + span], value[start:cut]]
    return jnp.concatenate(lines)


def attach_kernel(tokens_ref, routes_ref, probs_ref, out_ref):
    rows, width = tokens_ref.shape
    pair = out_ref.shape[1] - width
    out_ref[:, :width] = tokens_ref[...]
    routes = routes_ref[...]
    probs = probs_ref[...]
    lane = lax.broadcasted_iota(jnp.int32, (rows, pair), 1)
    ids = jnp.where(lane < pair // 2, lane, lane - pair // 2)
    weight = jnp.zeros((rows, pair), F32)
    for k in range(routes.shape[1]):
        weight += jnp.where(ids == routes[:, k : k + 1], probs[:, k : k + 1], 0.0)
    high = weight.astype(BF).astype(F32)
    out_ref[:, width:] = jnp.where(lane < pair // 2, high, weight - high).astype(BF)


def attach(tokens, routes, probs, pair):
    rows, width = tokens.shape
    return pl.pallas_call(
        attach_kernel,
        out_shape=jax.ShapeDtypeStruct((rows, width + pair), BF),
        compiler_params=pltpu.CompilerParams(vmem_limit_bytes=SMALL_LIMIT),
        cost_estimate=BRIEF,
        name="attach",
    )(*in_hbm(tokens, routes, probs))


def piece_copies(source, target, sems):
    step = source.shape[0] // PIECES
    spans = [pl.ds(i * step, step) for i in range(PIECES)]
    return [
        pltpu.make_async_copy(source.at[span], target.at[span], sems.at[i])
        for i, span in enumerate(spans)
    ]


def load_kernel(source, target, sems):
    copies = piece_copies(source, target, sems)
    for copy in copies:
        copy.start()
    for copy in copies:
        copy.wait()


def load(weights):
    return pl.pallas_call(
        load_kernel,
        in_specs=[pl.BlockSpec(memory_space=pltpu.HBM)],
        out_specs=pl.BlockSpec(memory_space=pltpu.VMEM),
        out_shape=pltpu.VMEM(weights.shape, weights.dtype),
        scratch_shapes=[pltpu.SemaphoreType.DMA((PIECES,))],
        compiler_params=pltpu.CompilerParams(vmem_limit_bytes=SMALL_LIMIT),
        cost_estimate=SOME,
        name="load",
    )(*in_hbm(weights))


def prepare_kernel(parts, *refs):
    ins, lefts, source = refs[:3], refs[3:5], refs[5]
    target, left_ref, outs, sems = refs[6], refs[7], refs[8:-1], refs[-1]
    copies = piece_copies(source, target, sems)
    for copy in copies:
        copy.start()
    half = left_ref.shape[0] // 2
    for n, ref in enumerate(lefts):
        left_ref[n * half : (n + 1) * half] = ref[...].reshape(half, left_ref.shape[1])
    exp_dev, piece, hid = ins[0].shape
    cols = hid // parts
    me = lax.axis_index("mp")
    for n, ref in enumerate(ins):
        value = ref[...].reshape(exp_dev * piece, hid).astype(F32)
        blocks = [value[:, j * cols : (j + 1) * cols] for j in range(parts)]
        for k in range(parts):
            device = lax.rem(me + k, parts)
            block = blocks[0]
            for j in range(1, parts):
                block = jnp.where(device == j, blocks[j], block)
            outs[k][n] = block.astype(BF)
    for copy in copies:
        copy.wait()


def prepare(factors, lefts, weights, parts):
    exp_dev, piece, hid = factors[0].shape
    _, rank, block = lefts[0].shape
    vmem = pl.BlockSpec(memory_space=pltpu.VMEM)
    return pl.pallas_call(
        functools.partial(prepare_kernel, parts),
        in_specs=[vmem] * 5 + [pl.BlockSpec(memory_space=pltpu.HBM)],
        out_specs=[vmem] * (2 + parts),
        out_shape=[pltpu.VMEM(weights.shape, weights.dtype)]
        + [jax.ShapeDtypeStruct((2 * exp_dev * rank, block), BF)]
        + [jax.ShapeDtypeStruct((3, exp_dev * piece, hid // parts), BF)] * parts,
        scratch_shapes=[pltpu.SemaphoreType.DMA((PIECES,))],
        compiler_params=pltpu.CompilerParams(vmem_limit_bytes=SMALL_LIMIT),
        cost_estimate=BRIEF,
        name="prepare",
    )(*in_hbm(*factors, *lefts, weights))


def spread_kernel(parts, exp_dev, *refs):
    pieces, out_ref = refs[:-1], refs[-1]
    _, ranks, hid = out_ref.shape
    rank = ranks // exp_dev
    piece = rank // parts
    me = lax.axis_index("mp")
    row = lax.broadcasted_iota(jnp.int32, (ranks, ranks), 0)
    col = lax.broadcasted_iota(jnp.int32, (ranks, ranks), 1)
    step = lax.rem(me - row % rank // piece + parts, parts)
    source = (step * exp_dev + row // rank) * piece + row % piece
    order = (col == source).astype(F32).astype(BF)
    cols = hid // exp_dev
    place = lax.broadcasted_iota(jnp.int32, (ranks, hid), 1)
    place -= lax.broadcasted_iota(jnp.int32, (ranks, hid), 0) // rank * cols
    own = (place >= 0) & (place < cols)
    for n in range(3):
        value = dot_nn(order, jnp.concatenate([p[n].astype(F32) for p in pieces]).astype(BF))
        value = jnp.concatenate([value] * exp_dev, axis=1)
        out_ref[n] = jnp.where(own, value, 0.0).astype(BF)


def spread(pieces, parts, exp_dev):
    _, span, cols = pieces[0].shape
    return pl.pallas_call(
        functools.partial(spread_kernel, parts, exp_dev),
        out_shape=jax.ShapeDtypeStruct((3, span * parts, cols * exp_dev), BF),
        compiler_params=pltpu.CompilerParams(vmem_limit_bytes=SMALL_LIMIT),
        cost_estimate=SOME,
        name="spread",
    )(*pieces)


def inner_kernel(parts, rows, count, *refs):
    lines, left_ref, outs = refs[:count], refs[count], refs[count + 1 :]
    block = left_ref.shape[1]
    offset = pl.multiple_of(lax.axis_index("mp") * block, 128)
    x = jnp.concatenate([line[:, pl.ds(offset, block)] for line in lines])
    value = dot_nt(x, left_ref[...])
    for k in range(parts):
        outs[k][...] = rotated(value, rows, parts, k).astype(BF)


def inner_products(lines, left, parts, rows):
    total = sum(line.shape[0] for line in lines)
    ranks = left.shape[0]
    return pl.pallas_call(
        functools.partial(inner_kernel, parts, rows, len(lines)),
        out_shape=[jax.ShapeDtypeStruct((total, ranks), BF)] * parts,
        compiler_params=pltpu.CompilerParams(vmem_limit_bytes=VMEM_LIMIT),
        cost_estimate=BRIEF,
        name="inner",
    )(*lines, left)


def raw_kernel(count, tile, *refs):
    lines, (gate_w, up_w, gate_ref, up_ref) = refs[:count], refs[count:]
    hid, width = gate_w.shape
    x = jnp.concatenate([line[:, :width] for line in lines])
    for i in range(hid // tile):
        span = pl.ds(i * tile, tile)
        gate_ref[:, span] = dot_nt(gate_w[span], x).T
        up_ref[:, span] = dot_nt(up_w[span], x).T


def raw_products(lines, gate_w, up_w):
    hid = gate_w.shape[0]
    total = sum(line.shape[0] for line in lines)
    tile = 384
    return pl.pallas_call(
        functools.partial(raw_kernel, len(lines), tile),
        out_shape=[jax.ShapeDtypeStruct((total, hid), F32)] * 2,
        compiler_params=pltpu.CompilerParams(vmem_limit_bytes=VMEM_LIMIT),
        cost_estimate=BRIEF,
        name="raw",
    )(*lines, gate_w, up_w)


def hidden_kernel(parts, count, exp_dev, pair, *refs):
    lines, inner, rest = refs[:count], refs[count : count + parts], refs[count + parts :]
    gate_ref, up_ref, diag_ref, hidden_ref = rest[:4]
    outs = rest[4:]
    hid = gate_ref.shape[1]
    ranks = diag_ref.shape[1]
    wide = lines[0].shape[1] - pair
    total = sum(ref[...].astype(F32) for ref in inner).astype(BF)
    gate = gate_ref[...] + dot_nn(total[:, :ranks], diag_ref[0])
    up = up_ref[...] + dot_nn(total[:, ranks:], diag_ref[1])
    lane = lax.broadcasted_iota(jnp.int32, (pair, hid), 0)
    lane = jnp.where(lane < pair // 2, lane, lane - pair // 2)
    cols = hid // exp_dev
    first = (lax.axis_index("y") * 2 + lax.axis_index("core")) * exp_dev
    place = lax.broadcasted_iota(jnp.int32, (pair, hid), 1) - (lane - first) * cols
    pick = ((place >= 0) & (place < cols)).astype(F32).astype(BF)
    scale = dot_nn(jnp.concatenate([line[:, wide:] for line in lines]), pick)
    hidden = (gate / (1.0 + jnp.exp(-gate)) * up * scale).astype(BF)
    hidden_ref[...] = hidden
    value = dot_nt(hidden, diag_ref[2])
    chips = len(outs)
    span = value.shape[0] // (2 * chips)
    for n, out_ref in enumerate(outs):
        rows = [value[i * span : (i + 1) * span] for i in (n, n + chips)]
        out_ref[...] = jnp.concatenate(rows).astype(BF)


def hidden_units(lines, inner, raw, diag, parts, exp_dev, pair, chips):
    total, hid = raw[0].shape
    ranks = diag.shape[1]
    return pl.pallas_call(
        functools.partial(hidden_kernel, parts, len(lines), exp_dev, pair),
        out_shape=[jax.ShapeDtypeStruct((total, hid), BF)]
        + [jax.ShapeDtypeStruct((total // chips, ranks), BF)] * chips,
        compiler_params=pltpu.CompilerParams(vmem_limit_bytes=VMEM_LIMIT),
        cost_estimate=BRIEF,
        name="hidden",
    )(*lines, *inner, *raw, diag)


def down_kernel(hidden_ref, down_ref, near_ref, far_ref):
    near, width = near_ref.shape
    hidden = hidden_ref[...]
    tile = min(1024, width)
    for i in range(width // tile):
        span = slice(i * tile, (i + 1) * tile)
        value = dot_nn(hidden, down_ref[:, span])
        near_ref[:, span] = value[:near]
        far_ref[:, span] = value[near:].astype(BF)


def down_products(hidden, down_w):
    total, width = hidden.shape[0], down_w.shape[1]
    return pl.pallas_call(
        down_kernel,
        out_shape=[
            jax.ShapeDtypeStruct((total // 2, width), F32),
            jax.ShapeDtypeStruct((total // 2, width), BF),
        ],
        compiler_params=pltpu.CompilerParams(vmem_limit_bytes=VMEM_LIMIT),
        cost_estimate=BRIEF,
        name="down",
    )(hidden, down_w)


def pair_kernel(*refs):
    ins, (near_ref, far_ref) = refs[:-2], refs[-2:]
    value = jnp.concatenate([ref[...].astype(F32) for ref in ins], axis=1)
    span = near_ref.shape[0]
    near_ref[...] = value[:span].astype(BF)
    far_ref[...] = value[span:].astype(BF)


def side_by_side(lines):
    total, ranks = lines[0].shape
    return pl.pallas_call(
        pair_kernel,
        out_shape=[jax.ShapeDtypeStruct((total // 2, len(lines) * ranks), BF)] * 2,
        compiler_params=pltpu.CompilerParams(vmem_limit_bytes=SMALL_LIMIT),
        cost_estimate=LONGER,
        name="pair",
    )(*lines)


def turn_kernel(rows, near_ref, far_ref, *outs):
    value = jnp.concatenate([near_ref[...].astype(F32), far_ref[...].astype(F32)], axis=1)
    for k, out_ref in enumerate(outs):
        out_ref[...] = rotated(value, rows, len(outs), k).astype(BF)


def turn(near, far, parts, rows):
    span, ranks = near.shape
    return pl.pallas_call(
        functools.partial(turn_kernel, rows),
        out_shape=[jax.ShapeDtypeStruct((span, 2 * ranks), BF)] * parts,
        compiler_params=pltpu.CompilerParams(vmem_limit_bytes=SMALL_LIMIT),
        cost_estimate=TURN,
        name="turn",
    )(near, far)


def add_up_kernel(*refs):
    refs[-1][...] = sum(ref[...].astype(F32) for ref in refs[:-1]).astype(BF)


def add_up(pieces):
    return pl.pallas_call(
        add_up_kernel,
        out_shape=jax.ShapeDtypeStruct(pieces[0].shape, BF),
        compiler_params=pltpu.CompilerParams(vmem_limit_bytes=SMALL_LIMIT),
        cost_estimate=LONG,
        name="add_up",
    )(*pieces)


def fold_kernel(head, near_ref, far_ref, own_ref, *out_refs):
    span = own_ref.shape[0]
    total = near_ref[...] + far_ref[...].astype(F32)
    own_ref[...] = total[:span]
    for n in range(len(out_refs) // 2):
        line = total[(n + 1) * span : (n + 2) * span]
        out_refs[2 * n][...] = line[:head].astype(BF)
        out_refs[2 * n + 1][...] = line[head:].astype(BF)


def fold(near, far, chips, head):
    total, width = near.shape
    span = total // chips
    return pl.pallas_call(
        functools.partial(fold_kernel, head),
        out_shape=[jax.ShapeDtypeStruct((span, width), F32)]
        + [jax.ShapeDtypeStruct((rows, width), BF) for rows in (head, span - head)]
        * (chips - 1),
        compiler_params=pltpu.CompilerParams(vmem_limit_bytes=VMEM_LIMIT),
        cost_estimate=BRIEF,
        name="fold",
    )(near, far)


def merge_kernel(chips, parts, *refs):
    own_ref, rights, refs = refs[0], refs[1 : 1 + 2 * chips], refs[1 + 2 * chips :]
    low, backs, outs = refs[0][...], refs[1:-parts], refs[-parts:]
    rows = outs[0].shape[0]
    ranks, block = rights[0].shape
    offset = pl.multiple_of(lax.axis_index("mp") * block, 128)
    value = jnp.zeros((low.shape[0], block), F32)
    for n, ref in enumerate(rights):
        value += dot_nn(low[:, n * ranks : (n + 1) * ranks], ref[...])
    total = own_ref[...]
    value += own_ref[:, pl.ds(offset, block)]
    rest, rest_value = total[rows:], value[rows:]
    for ref in backs:
        rest += ref[...].astype(F32)
        rest_value += ref[:, pl.ds(offset, block)].astype(F32)
    outs[0][...] = total[:rows]
    outs[0][:, pl.ds(offset, block)] = value[:rows]
    for k in range(1, parts):
        span = slice((k - 1) * rows, k * rows)
        outs[k][...] = rest[span].astype(BF)
        outs[k][:, pl.ds(offset, block)] = rest_value[span].astype(BF)


def plus_kernel(own_ref, *refs):
    total = own_ref[...]
    for ref in refs[:-1]:
        total += ref[...].astype(F32)
    refs[-1][...] = total


def plus(own, pieces):
    return pl.pallas_call(
        plus_kernel,
        out_shape=jax.ShapeDtypeStruct(own.shape, F32),
        compiler_params=pltpu.CompilerParams(vmem_limit_bytes=SMALL_LIMIT),
        cost_estimate=LAST,
        name="plus",
    )(own, *pieces)


def merge(own, rights, low, backs, rows):
    total, width = own.shape
    parts = total // rows
    return pl.pallas_call(
        functools.partial(merge_kernel, len(rights) // 2, parts),
        out_shape=[jax.ShapeDtypeStruct((rows, width), F32)]
        + [jax.ShapeDtypeStruct((rows, width), BF)] * (parts - 1),
        compiler_params=pltpu.CompilerParams(vmem_limit_bytes=VMEM_LIMIT),
        cost_estimate=BRIEF,
        name="merge",
    )(own, *rights, low, *backs)


def local(
    tokens,
    routes,
    probs,
    w_gate,
    w_up,
    w_down,
    gate_left,
    gate_right,
    up_left,
    up_right,
    down_left,
    down_right,
):
    rows, width = tokens.shape
    exp_dev, _, cols = w_gate.shape
    rank = gate_left.shape[1]
    block = gate_left.shape[2]
    parts = lax.axis_size("mp")
    chips = lax.axis_size("y")
    experts = exp_dev * chips * 2
    ranks = exp_dev * rank
    hid = exp_dev * cols

    def along_z(value, step):
        return lax.ppermute(value, "mp", [(i, (i + step) % parts) for i in range(parts)])

    def along_y(value, step):
        return lax.ppermute(value, "y", [(i, (i + step) % chips) for i in range(chips)])

    def other_core(value):
        return lax.ppermute(value, "core", [(0, 1), (1, 0)])

    pair = 2 * (-(-experts // 64) * 64)
    sent = attach(tokens, routes, probs, pair)
    arrived = [along_z(sent, k) for k in range(1, parts)]
    first = [along_y(sent, s) for s in range(1, chips)]
    gate_w, up_w = (jnp.swapaxes(w, 1, 2).reshape(hid, width) for w in (w_gate, w_up))
    gate_w, left, *small = prepare(
        (gate_right, up_right, down_left), (gate_left, up_left), gate_w, parts
    )
    right = down_right.reshape(ranks, block)
    partner_right = other_core(right)
    rest = after(jnp.concatenate(arrived), (left, small, gate_w, partner_right))
    up_w = load(after(up_w, rest))
    lines = [jnp.concatenate([sent, rest])]
    partner = [other_core(lines[0])]
    small = after(tuple(small), rest)
    small = [small[0]] + [along_z(small[k], k) for k in range(1, parts)]
    for s in range(1, chips):
        line = jnp.concatenate([first[s - 1], along_y(rest, s)])
        arrival = line
        line = after(line, up_w)
        lines.append(line)
        partner.append(other_core(line))
    lines += partner
    diag = spread(small, parts, exp_dev)

    lines = after(tuple(lines), diag)
    inner = inner_products(lines, left, parts, rows)
    inner = [inner[0]] + [along_z(inner[k], k) for k in range(1, parts)]
    raw = raw_products(lines, gate_w, up_w)
    right = after(right, arrival)
    rights = [right] + [along_y(right, -s) for s in range(1, chips)]
    raw = after(tuple(raw), rights[1:])
    hidden, low, *lows = hidden_units(
        lines, inner, raw, diag, parts, exp_dev, pair, chips
    )
    lows = [along_y(lows[s - 1], -s) for s in range(1, chips)]
    near, far = side_by_side([low] + lows)
    bottom = turn(near, other_core(far), parts, rows)
    bottom = [bottom[0]] + [along_z(bottom[k], k) for k in range(1, parts)]

    near, far = down_products(hidden, w_down.reshape(hid, width))
    out, *others = fold(near, other_core(far), chips, rows)
    backs = [along_y(others[n], -(n // 2 + 1)) for n in range(2 * chips - 2)]
    rights += [partner_right] + [other_core(after(right, out)) for right in rights[1:]]
    own, *pieces = merge(out, rights, add_up(bottom[1:] + bottom[:1]), backs[1::2], rows)
    result = plus(own, backs[::2])
    for k in sorted(range(1, parts), key=lambda k: -min(k, parts - k)):
        result += along_z(pieces[k - 1], -k).astype(F32)
    return result.astype(BF)


def solution(mesh):
    count = mesh.shape
    fine = jax.sharding.Mesh(
        mesh.devices.reshape(count["groups"], count["expert"] // 2, 2, count["mp"]),
        ("groups", "y", "core", "mp"),
    )
    expert = ("y", "core")
    return jax.shard_map(
        local,
        mesh=fine,
        in_specs=(
            P(("groups", "y", "core", "mp"), None),
            P(("groups", "y", "core", "mp"), None),
            P(("groups", "y", "core", "mp"), None),
            P(expert, None, "mp"),
            P(expert, None, "mp"),
            P(expert, "mp", None),
            P(expert, None, "mp"),
            P(expert, "mp", None),
            P(expert, None, "mp"),
            P(expert, "mp", None),
            P(expert, "mp", None),
            P(expert, None, "mp"),
        ),
        out_specs=P(("groups", "y", "core", "mp"), None),
        check_vma=False,
    )
```
